32 devices in a mesh: ty: 8 (over y, x, core), tx: 4 (over z).
Axes of the slice: x: 2, y: 2, z: 4, core: 2. Of those that a mesh axis runs over, the one named last changes fastest.
Arguments:
- spectrum: float32 [2, 4096, 4096], P(None, 'ty', 'tx'), may hold values from -6 to 6
- pupil: float32 [2, 512, 512], replicated, may hold values from -6 to 6
- amplitudes: float32 [96, 512, 512], P(('ty', 'tx')), may hold values from 0 to 3
- offsets: int32 [96, 2], P(('ty', 'tx')), may hold values from 0 to 3584, as said below
- live: int32 [96], P(('ty', 'tx')), may hold values from 0 to 1, as said below
Outputs:
- spectrum_grad: float32 [2, 4096, 4096], P(None, 'ty', 'tx')
- pupil_grad: float32 [2, 512, 512], replicated
The draws below stay inside these ranges and needn't reach their ends.
Inputs may be any that keep to these rules, and one draw needn't show every extreme that they name: `offsets`: the slots of the device at ty index i and tx index j are i * 4 * 3 + j * 3 to that plus 3 - 1; each such slot's corner has row in [i * 512, (i + 1) * 512) and column in [j * 1024, (j + 1) * 1024), and its window lies inside the spectrum. Each device's live slots come first among its 3 slots, and every device has at least one. Two devices with the same tx index whose ty indices differ by 4 hold together at most 4 live slots; some such pair holds exactly that many, and some device has all 3 slots live.
All inputs are finite; a program needn't handle non-finite values.
Results may differ from the reference program's by a relative error of at most 0.0001.
Values sent between devices are 32-bit elements; how exact they have to be, the bound alone decides.
No kernel may reach another device: no remote copies, remote signals or barrier semaphores. Data moves between devices by JAX's collectives and lax.ppermute only.
A program may use at most 192 MiB of HBM per device.

```python
import math
import jax
import jax.numpy as jnp
from jax import lax

M = 512
TR = 512
TC = 1024
CAP = 3
NR = 4096
NC = 4096
SLOTS = 96
N_TY = 8
N_TX = 4


def device_counts(key):
    middle_key = jax.random.fold_in(key, 5)
    row_grid = jnp.broadcast_to(jnp.arange(N_TY)[:, None], (N_TY, N_TX))
    central = (row_grid >= N_TY // 4) & (row_grid < 3 * N_TY // 4)
    edge_count = jnp.ones((N_TY, N_TX), jnp.int32)
    middle = jax.random.randint(middle_key, (N_TY, N_TX), 2, CAP + 1)
    counts = jnp.where(central, middle, edge_count)
    counts = counts.at[N_TY // 2, N_TX // 2].set(CAP)
    return counts.reshape(-1)


def draw_live(key, part):
    counts = device_counts(key)
    slot_ids = jnp.arange(CAP)[None, :]
    return (slot_ids < counts[:, None]).astype(jnp.int32).reshape(-1)


def draw_offsets(key, part):
    key = jax.random.fold_in(key, 7)
    row_key, col_key = jax.random.split(key)
    device_ids = jnp.arange(N_TY * N_TX * CAP) // CAP
    tile_row = device_ids // N_TX
    tile_col = device_ids % N_TX
    row_top = jnp.minimum(TR - 1, TR * N_TY - M - tile_row * TR)
    col_top = jnp.minimum(TC - 1, TC * N_TX - M - tile_col * TC)
    count = N_TY * N_TX * CAP
    row_pick = jax.random.randint(row_key, (count,), 0, row_top + 1)
    col_pick = jax.random.randint(col_key, (count,), 0, col_top + 1)
    last_slot = (N_TY * N_TX - 1) * CAP
    row_pick = row_pick.at[0].set(0).at[last_slot].set(row_top[last_slot])
    col_pick = col_pick.at[0].set(0).at[last_slot].set(col_top[last_slot])
    return jnp.stack([tile_row * TR + row_pick, tile_col * TC + col_pick], axis=1).astype(jnp.int32)


def steps_of(stream_key, dims, cuts, least, largest):
    loudness, own = 1.0, jax.random.fold_in(stream_key, 6)
    for position, blocks in cuts:
        draws = jnp.exp(jax.random.uniform(jax.random.fold_in(own, position), (blocks,), jnp.float32, least / len(cuts), largest / len(cuts)))
        loudness = loudness * jnp.repeat(draws, dims[position] // blocks).reshape([-1 if axis == position else 1 for axis in range(len(dims))])
    return loudness


def noise(key, shape, scale, most, cuts=(), kind=jnp.bfloat16):
    array = jax.random.normal(key, shape, jnp.float32) * scale
    if len(cuts) > 0:
        array = steps_of(key, shape, cuts, -0.22, 0.18) * array
    return jnp.clip(array, min=-most, max=most).astype(kind)


def setup_inputs(seed: int = 0) -> dict:
    streams_of = jax.random.split(jax.random.key(seed), 6)
    return {
        "spectrum": noise(streams_of[0], (2, NR, NC), 1.0, 6.0, ((1, 8), (2, 4)), jnp.float32),
        "pupil": noise(streams_of[1], (2, M, M), 1.0, 6.0, (), jnp.float32),
        "amplitudes": jnp.clip(3.0 * jax.random.uniform(streams_of[2], (SLOTS, M, M), jnp.float32) ** steps_of(streams_of[2], (SLOTS, M, M), ((0, 32),), -0.2, 0.2), 0.0, 3.0),
        "offsets": draw_offsets(jax.random.fold_in(streams_of[5], 71), 0),
        "live": draw_live(jax.random.fold_in(streams_of[5], 71), 0),
    }


def reference(spectrum, pupil, amplitudes, offsets, live):
    pupil_c = lax.complex(pupil[0], pupil[1])
    zero_idx = jnp.zeros((), jnp.int32)

    def one_slot(carried, slot_data):
        spec_grad, pupil_acc = carried
        measured, corner, alive = slot_data
        window = lax.dynamic_slice(spectrum, (zero_idx, corner[0], corner[1]), (2, M, M))
        window_c = lax.complex(window[0], window[1])
        field = jnp.fft.ifft2(window_c * pupil_c, norm='ortho')
        field_re = jnp.real(field)
        field_im = jnp.imag(field)
        modulus = jnp.sqrt(field_re * field_re + field_im * field_im + 1.0)
        residual = (1.0 - measured / modulus) * field
        spectral = jnp.fft.fft2(residual, norm='ortho')
        weight = alive.astype(spectrum.dtype)
        dwin = jnp.conj(pupil_c) * spectral
        dpup = jnp.conj(window_c) * spectral
        dwin_planes = jnp.stack([jnp.real(dwin), jnp.imag(dwin)]) * weight
        dpup_planes = jnp.stack([jnp.real(dpup), jnp.imag(dpup)]) * weight
        current = lax.dynamic_slice(spec_grad, (zero_idx, corner[0], corner[1]), (2, M, M))
        spec_grad = lax.dynamic_update_slice(spec_grad, current + dwin_planes, (zero_idx, corner[0], corner[1]))
        return ((spec_grad, pupil_acc + dpup_planes), None)
    start = (jnp.zeros_like(spectrum), jnp.zeros_like(pupil))
    (spec_grad, pupil_acc), _ = lax.scan(one_slot, start, (amplitudes, offsets, live))
    return (spec_grad, pupil_acc / math.sqrt(N_TY * N_TX))
```

```python
import math

import jax
import jax.numpy as jnp
import ml_dtypes
import numpy as np
from jax import lax
from jax.experimental import pallas as pl
from jax.experimental.pallas import tpu as pltpu
from jax.sharding import PartitionSpec as P

RADIX = 4


def shifted(array, axis, by):
    devices = lax.axis_size(axis)
    pairs = [(i, i + by) for i in range(devices) if 0 <= i + by < devices]
    return lax.ppermute(array, axis, pairs)


def dft_blocks(length):
    short = length // RADIX
    out_idx = np.arange(short)[:, None]
    in_idx = np.arange(short)[None, :]
    blocks = []
    for p in range(RADIX):
        phase = (p * in_idx + RADIX * out_idx * in_idx) % length
        angle = phase * (2.0 * math.pi / length)
        cos = np.cos(angle) / math.sqrt(length)
        sin = np.sin(angle) / math.sqrt(length)
        blocks.append(np.block([[cos, -sin], [sin, cos]]))
    full = np.stack(blocks).astype(np.float32)
    high = full.astype(ml_dtypes.bfloat16)
    low = (full - high.astype(np.float32)).astype(ml_dtypes.bfloat16)
    return high, low


def split(value):
    high = value.astype(jnp.bfloat16)
    low = (value - high.astype(jnp.float32)).astype(jnp.bfloat16)
    return high, low


def dot(lhs, rhs):
    return jnp.dot(lhs, rhs, preferred_element_type=jnp.float32)


def dot3(lhs_hi, lhs_lo, rhs_hi, rhs_lo):
    return dot(lhs_hi, rhs_hi) + (dot(lhs_hi, rhs_lo) + dot(lhs_lo, rhs_hi))


def butterfly(parts, sign):
    (r0, i0), (r1, i1), (r2, i2), (r3, i3) = parts
    sr, si, dr, di = r0 + r2, i0 + i2, r0 - r2, i0 - i2
    tr, ti, er, ei = r1 + r3, i1 + i3, r1 - r3, i1 - i3
    if sign < 0:
        er, ei = -er, -ei
    return [(sr + tr, si + ti), (dr - ei, di + er), (sr - tr, si - ti), (dr + ei, di - er)]


def row_index():
    return lax.broadcasted_iota(jnp.int32, (8, 128), 0)


def lane_index():
    return lax.broadcasted_iota(jnp.int32, (8, 128), 1)


def lane_tiles(tile):
    return [tile[:, i : i + 128] for i in range(0, tile.shape[1], 128)]


def pull_lanes(tile, shift):
    rolled = [pltpu.roll(part, (128 - shift) % 128, 1) for part in lane_tiles(tile)]
    keep = lane_index() < 128 - shift
    return [jnp.where(keep, a, b) for a, b in zip(rolled, rolled[1:])]


def pull_rows(tiles, shift):
    rolled = [[pltpu.roll(part, (8 - shift) % 8, 0) for part in tile] for tile in tiles]
    keep = row_index() < 8 - shift
    return [
        jnp.concatenate([jnp.where(keep, x, y) for x, y in zip(a, b)], axis=1)
        for a, b in zip(rolled, rolled[1:])
    ]


def push_lanes(tile, shift):
    rolled = [pltpu.roll(part, shift, 1) for part in lane_tiles(tile)]
    zero = jnp.zeros((8, 128), jnp.float32)
    keep = lane_index() >= shift
    return [jnp.where(keep, b, a) for a, b in zip([zero] + rolled, rolled + [zero])]


def push_rows(tiles, shift):
    rolled = [[pltpu.roll(part, shift, 0) for part in tile] for tile in tiles]
    keep = row_index() >= shift
    return [
        jnp.concatenate([jnp.where(keep, y, x) for x, y in zip(a, b)], axis=1)
        for a, b in zip(rolled, rolled[1:])
    ]


def slots_kernel(
    meta,
    tile_hbm,
    right_hbm,
    lower_hbm,
    corner_hbm,
    amps_hbm,
    pupil,
    mat_hi,
    mat_lo,
    mat_t_hi,
    mat_t_lo,
    own_out,
    right_out,
    lower_out,
    corner_out,
    dpup,
    region,
    grads,
    win,
    left_hi,
    left_lo,
    right_hi,
    right_lo,
    cols_f32,
    rows_f32,
    dwin,
    amps,
    sems,
):
    side = pupil.shape[-1]
    short = side // RADIX
    tile_rows, tile_cols = tile_hbm.shape[1:]
    slots = amps_hbm.shape[0]
    lanes = 128
    wide = side + lanes

    def pieces(buffer):
        return (
            buffer.at[:, pl.ds(0, tile_rows), pl.ds(0, tile_cols)],
            buffer.at[:, pl.ds(0, tile_rows), pl.ds(tile_cols, side)],
            buffer.at[:, pl.ds(tile_rows, side), pl.ds(0, tile_cols)],
            buffer.at[:, pl.ds(tile_rows, side), pl.ds(tile_cols, side)],
        )

    sources = (tile_hbm, right_hbm, lower_hbm, corner_hbm)
    loads = [
        pltpu.make_async_copy(src, dst, sems.at[n])
        for n, (src, dst) in enumerate(zip(sources, pieces(region)))
    ]
    loads.append(pltpu.make_async_copy(amps_hbm, amps, sems.at[4]))
    for load in loads:
        load.start()

    zero_rows = 16

    @pl.loop(0, grads.shape[1] // zero_rows)
    def _(step):
        rows = pl.ds(pl.multiple_of(step * zero_rows, zero_rows), zero_rows)
        grads[:, rows, :] = jnp.zeros((2, zero_rows, grads.shape[2]), jnp.float32)

    @pl.loop(0, side // zero_rows)
    def _(step):
        rows = pl.ds(pl.multiple_of(step * zero_rows, zero_rows), zero_rows)
        dpup[:, rows, :] = jnp.zeros((2, zero_rows, side), jnp.float32)

    for start in (0, side + 8):
        dwin[:, pl.ds(start, 8), :] = jnp.zeros((2, 8, side), jnp.float32)

    for load in loads:
        load.wait()

    def one_slot(slot):
        row = meta[slot, 0]
        col = meta[slot, 1]
        col_base = pl.multiple_of((col // lanes) * lanes, lanes)
        col_shift = col - col_base
        row_base = pl.multiple_of((row // 8) * 8, 8)
        row_shift = row - row_base

        @pl.loop(0, side // 32)
        def _(step):
            base = pl.multiple_of(step * 32, 32)
            for plane in range(2):
                tiles = []
                for i in range(5):
                    start = pl.multiple_of(row_base + base + 8 * i, 8)
                    tiles.append(region[plane, pl.ds(start, 8), pl.ds(col_base, wide)])
                tiles = [pull_lanes(tile, col_shift) for tile in tiles]
                for i, tile in enumerate(pull_rows(tiles, row_shift)):
                    win[plane, pl.ds(base + 8 * i, 8), :] = tile

        @pl.loop(0, short // 16)
        def _(step):
            base = pl.multiple_of(step * 16, 16)
            for part in range(RADIX):
                cols = pl.ds(part * short, short)
                values = []
                for q in range(RADIX):
                    rows = pl.ds(base + q * short, 16)
                    wr, wi = win[0, rows, cols], win[1, rows, cols]
                    pr, pi = pupil[0, rows, cols], pupil[1, rows, cols]
                    values.append((wr * pr - wi * pi, wr * pi + wi * pr))
                for p, (re, im) in enumerate(butterfly(values, 1)):
                    for offset, value in ((0, re), (short, im)):
                        hi, lo = split(value)
                        rows = pl.ds(base + offset, 16)
                        left_hi[p, rows, cols] = hi
                        left_lo[p, rows, cols] = lo

        for p in range(RADIX):
            for half in range(2):
                cols = pl.ds(half * (side // 2), side // 2)
                rows_f32[p, :, cols] = dot3(
                    mat_hi[p], mat_lo[p], left_hi[p, :, cols], left_lo[p, :, cols]
                )

        for p in range(RADIX):

            @pl.loop(0, short // 16)
            def _(step):
                base = pl.multiple_of(step * 16, 16)
                values = []
                for q in range(RADIX):
                    cols = pl.ds(q * short, short)
                    values.append(
                        (
                            rows_f32[p, pl.ds(base, 16), cols],
                            rows_f32[p, pl.ds(base + short, 16), cols],
                        )
                    )
                for t, (re, im) in enumerate(butterfly(values, 1)):
                    for offset, value in ((0, re), (short, im)):
                        hi, lo = split(value)
                        rows = pl.ds(base + p * short, 16)
                        right_hi[t, rows, pl.ds(offset, short)] = hi
                        right_lo[t, rows, pl.ds(offset, short)] = lo

        for t in range(RADIX):
            for half in range(2):
                rows = pl.ds(half * (side // 2), side // 2)
                field = dot3(right_hi[t, rows, :], right_lo[t, rows, :], mat_t_hi[t], mat_t_lo[t])
                fre, fim = field[:, :short], field[:, short:]
                measured = amps[slot, rows, pl.ds(t * short, short)]
                factor = 1.0 - measured * lax.rsqrt(fre * fre + fim * fim + 1.0)
                residual = jnp.concatenate([factor * fre, factor * fim], axis=1)
                hi, lo = split(residual)
                cols_f32[t, rows, :] = dot3(hi, lo, mat_hi[t], mat_lo[t])

        for p in range(RADIX):

            @pl.loop(0, short // 16)
            def _(step):
                base = pl.multiple_of(step * 16, 16)
                rows = pl.ds(base + p * short, 16)
                values = [
                    (cols_f32[t, rows, pl.ds(0, short)], cols_f32[t, rows, pl.ds(short, short)])
                    for t in range(RADIX)
                ]
                for q, (re, im) in enumerate(butterfly(values, -1)):
                    cols = pl.ds(q * short, short)
                    for offset, value in ((0, re), (short, im)):
                        hi, lo = split(value)
                        left_hi[p, pl.ds(base + offset, 16), cols] = hi
                        left_lo[p, pl.ds(base + offset, 16), cols] = lo

        for p in range(RADIX):
            for half in range(2):
                cols = pl.ds(half * (side // 2), side // 2)
                rows_f32[p, :, cols] = dot3(
                    mat_t_hi[p], mat_t_lo[p], left_hi[p, :, cols], left_lo[p, :, cols]
                )

        @pl.loop(0, short // 8)
        def _(step):
            base = pl.multiple_of(step * 8, 8)
            for part in range(RADIX):
                cols = pl.ds(part * short, short)
                values = [
                    (rows_f32[p, pl.ds(base, 8), cols], rows_f32[p, pl.ds(base + short, 8), cols])
                    for p in range(RADIX)
                ]
                for q, (re, im) in enumerate(butterfly(values, -1)):
                    rows = pl.ds(base + q * short, 8)
                    pr, pi = pupil[0, rows, cols], pupil[1, rows, cols]
                    padded = pl.ds(base + q * short + 8, 8)
                    dwin[0, padded, cols] = pr * re + pi * im
                    dwin[1, padded, cols] = pr * im - pi * re
                    wr, wi = win[0, rows, cols], win[1, rows, cols]
                    dpup[0, rows, cols] += wr * re + wi * im
                    dpup[1, rows, cols] += wr * im - wi * re

        @pl.loop(0, (side + 8) // 40)
        def _(step):
            base = pl.multiple_of(step * 40, 8)
            for plane in range(2):
                tiles = [dwin[plane, pl.ds(base + 8 * i, 8), :] for i in range(6)]
                tiles = [push_lanes(tile, col_shift) for tile in tiles]
                for i, tile in enumerate(push_rows(tiles, row_shift)):
                    start = pl.multiple_of(row_base + base + 8 * i, 8)
                    target = (plane, pl.ds(start, 8), pl.ds(col_base, wide))
                    grads[target] = grads[target] + tile

    @pl.loop(0, slots)
    def _(slot):
        pl.when(meta[slot, 2] != 0)(lambda: one_slot(slot))

    targets = (own_out, right_out, lower_out, corner_out)
    stores = [
        pltpu.make_async_copy(src, dst, sems.at[n])
        for n, (src, dst) in enumerate(zip(pieces(grads), targets))
    ]
    for store in stores:
        store.start()
    for store in stores:
        store.wait()


def slots_call(meta, tile, right, lower, corner, amps, pupil):
    side = pupil.shape[-1]
    short = side // RADIX
    slots = amps.shape[0]
    tile_rows, tile_cols = tile.shape[1:]
    high, low = dft_blocks(side)
    tables = [jnp.asarray(x) for x in (high, low, high.transpose(0, 2, 1), low.transpose(0, 2, 1))]
    whole = pl.BlockSpec(memory_space=pltpu.VMEM)
    anywhere = pl.BlockSpec(memory_space=pl.ANY)
    f32, bf16 = jnp.float32, jnp.bfloat16
    region = (2, tile_rows + side, tile_cols + side)
    return pl.pallas_call(
        slots_kernel,
        out_shape=[
            jax.ShapeDtypeStruct(x.shape, f32) for x in (tile, right, lower, corner, pupil)
        ],
        in_specs=[pl.BlockSpec(memory_space=pltpu.SMEM)] + [anywhere] * 5 + [whole] * 5,
        out_specs=[anywhere] * 4 + [whole],
        scratch_shapes=[
            pltpu.VMEM(region, f32),
            pltpu.VMEM(region, f32),
            pltpu.VMEM((2, side, side), f32),
            pltpu.VMEM((RADIX, 2 * short, side), bf16),
            pltpu.VMEM((RADIX, 2 * short, side), bf16),
            pltpu.VMEM((RADIX, side, 2 * short), bf16),
            pltpu.VMEM((RADIX, side, 2 * short), bf16),
            pltpu.VMEM((RADIX, side, 2 * short), f32),
            pltpu.VMEM((RADIX, 2 * short, side), f32),
            pltpu.VMEM((2, side + 16, side), f32),
            pltpu.VMEM(amps.shape, f32),
            pltpu.SemaphoreType.DMA((5,)),
        ],
        compiler_params=pltpu.CompilerParams(vmem_limit_bytes=56 * 1024 * 1024),
        cost_estimate=pl.CostEstimate(
            flops=slots * 48 * 2 * 4 * short * short * side,
            bytes_accessed=40 * 1024 * 1024,
            transcendentals=slots * side * side,
        ),
        name="slots",
    )(meta, tile, right, lower, corner, amps, pupil, *tables)


def sum_scatter(value, axis, members, inner):
    rows = value.shape[0] // members
    own = lax.axis_index(axis) // inner % members
    size = lax.axis_size(axis)

    def piece(index):
        return lax.dynamic_slice_in_dim(value, index * rows, rows, 0)

    total = piece(own)
    for step in range(1, members):
        total = total + lax.ppermute(
            piece((own + step) % members), axis, cyclic(size, members, inner, step)
        )
    return total


def cyclic(size, members, inner, step):
    pairs = []
    for i in range(size):
        group = i // inner % members
        pairs.append((i, i + ((group + step) % members - group) * inner))
    return pairs


def gather(value, axis, members, inner):
    rows = value.shape[0]
    own = lax.axis_index(axis) // inner % members
    size = lax.axis_size(axis)
    parts = [value]
    for step in range(1, members):
        parts.append(lax.ppermute(value, axis, cyclic(size, members, inner, step)))
    out = jnp.zeros((members * rows,) + value.shape[1:], value.dtype)
    for step, part in enumerate(parts):
        out = lax.dynamic_update_slice_in_dim(out, part, (own - step) % members * rows, 0)
    return out


def pupil_sum(dpup):
    n_ty, n_tx = lax.axis_size("ty"), lax.axis_size("tx")
    flat = dpup.reshape(-1, dpup.shape[-1])
    part = sum_scatter(flat, "ty", 2, 1)
    part = sum_scatter(part, "ty", n_ty // 2, 2)
    part = sum_scatter(part, "tx", n_tx, 1)
    part = part * (1.0 / math.sqrt(n_ty * n_tx))
    part = gather(part, "tx", n_tx, 1)
    part = gather(part, "ty", n_ty // 2, 2)
    part = gather(part, "ty", 2, 1)
    return part.reshape(dpup.shape)


def body(spectrum, pupil, amplitudes, offsets, live):
    side = pupil.shape[-1]
    short = side // RADIX
    slots = amplitudes.shape[0]
    tile_rows, tile_cols = spectrum.shape[1:]
    rows_local = offsets[:, 0] - lax.axis_index("ty") * tile_rows
    cols_local = offsets[:, 1] - lax.axis_index("tx") * tile_cols
    meta = jnp.stack([rows_local, cols_local, live], axis=1)

    right = shifted(spectrum[:, :, :side], "tx", -1)
    lower = shifted(spectrum[:, :side, :], "ty", -1)
    corner = shifted(right[:, :side, :], "ty", -1)
    amps = amplitudes.reshape(slots, short, RADIX, short, RADIX)
    amps = amps.transpose(0, 2, 1, 4, 3).reshape(slots, side, side)

    own_g, right_g, lower_g, corner_g, dpup = slots_call(
        meta, spectrum, right, lower, corner, amps, pupil
    )

    corner_back = shifted(corner_g, "ty", 1)
    lower_back = shifted(lower_g, "ty", 1)
    right_back = shifted(right_g + corner_back, "tx", 1)
    spec_grad = (own_g + lower_back).at[:, :, :side].add(right_back)
    return spec_grad, pupil_sum(dpup)


def solution(mesh):
    return jax.shard_map(
        body,
        mesh=mesh,
        in_specs=(
            P(None, "ty", "tx"),
            P(),
            P(("ty", "tx"), None, None),
            P(("ty", "tx"), None),
            P(("ty", "tx")),
        ),
        out_specs=(P(None, "ty", "tx"), P()),
        check_vma=False,
    )
```

```python
import math

import jax
import jax.numpy as jnp
import ml_dtypes
import numpy as np
from jax import lax
from jax.experimental import pallas as pl
from jax.experimental.pallas import tpu as pltpu
from jax.sharding import PartitionSpec as P

RADIX = 4


def dft_blocks(length):
    short = length // RADIX
    out_idx = np.arange(short)[:, None]
    in_idx = np.arange(short)[None, :]
    blocks = []
    for p in range(RADIX):
        phase = (p * in_idx + RADIX * out_idx * in_idx) % length
        angle = phase * (2.0 * math.pi / length)
        cos = np.cos(angle) / math.sqrt(length)
        sin = np.sin(angle) / math.sqrt(length)
        blocks.append(np.block([[cos, -sin], [sin, cos]]))
    full = np.stack(blocks).astype(np.float32)
    high = full.astype(ml_dtypes.bfloat16)
    low = (full - high.astype(np.float32)).astype(ml_dtypes.bfloat16)
    return high, low


def split(value):
    high = value.astype(jnp.bfloat16)
    low = (value - high.astype(jnp.float32)).astype(jnp.bfloat16)
    return high, low


def dot(lhs, rhs):
    return jnp.dot(lhs, rhs, preferred_element_type=jnp.float32)


def dot3(lhs_hi, lhs_lo, rhs_hi, rhs_lo):
    return dot(lhs_hi, rhs_hi) + (dot(lhs_hi, rhs_lo) + dot(lhs_lo, rhs_hi))


def butterfly(parts, sign):
    (r0, i0), (r1, i1), (r2, i2), (r3, i3) = parts
    sr, si, dr, di = r0 + r2, i0 + i2, r0 - r2, i0 - i2
    tr, ti, er, ei = r1 + r3, i1 + i3, r1 - r3, i1 - i3
    if sign < 0:
        er, ei = -er, -ei
    return [(sr + tr, si + ti), (dr - ei, di + er), (sr - tr, si - ti), (dr + ei, di - er)]


def row_index():
    return lax.broadcasted_iota(jnp.int32, (8, 128), 0)


def lane_index():
    return lax.broadcasted_iota(jnp.int32, (8, 128), 1)


def lane_tiles(tile):
    return [tile[:, i : i + 128] for i in range(0, tile.shape[1], 128)]


def pull_lanes(tile, shift):
    rolled = [pltpu.roll(part, (128 - shift) % 128, 1) for part in lane_tiles(tile)]
    keep = lane_index() < 128 - shift
    return [jnp.where(keep, a, b) for a, b in zip(rolled, rolled[1:])]


def pull_rows(tiles, shift):
    rolled = [[pltpu.roll(part, (8 - shift) % 8, 0) for part in tile] for tile in tiles]
    keep = row_index() < 8 - shift
    return [
        jnp.concatenate([jnp.where(keep, x, y) for x, y in zip(a, b)], axis=1)
        for a, b in zip(rolled, rolled[1:])
    ]


def push_lanes(tile, shift):
    rolled = [pltpu.roll(part, shift, 1) for part in lane_tiles(tile)]
    zero = jnp.zeros((8, 128), jnp.float32)
    keep = lane_index() >= shift
    return [jnp.where(keep, b, a) for a, b in zip([zero] + rolled, rolled + [zero])]


def push_rows(tiles, shift):
    rolled = [[pltpu.roll(part, shift, 0) for part in tile] for tile in tiles]
    keep = row_index() >= shift
    return [
        jnp.concatenate([jnp.where(keep, y, x) for x, y in zip(a, b)], axis=1)
        for a, b in zip(rolled, rolled[1:])
    ]


def slots_kernel(
    meta,
    tile_hbm,
    right_hbm,
    lower_hbm,
    corner_a_hbm,
    corner_up_hbm,
    corner_side_hbm,
    amps_hbm,
    pupil,
    mat_hi,
    mat_lo,
    mat_t_hi,
    mat_t_lo,
    own_out,
    right_out,
    lower_out,
    corner_a_out,
    corner_b_out,
    dpup,
    region,
    grads,
    win,
    left_hi,
    left_lo,
    right_hi,
    right_lo,
    cols_f32,
    rows_f32,
    dwin,
    amps,
    sems,
):
    side = pupil.shape[-1]
    short = side // RADIX
    tile_rows, tile_cols = tile_hbm.shape[1:]
    slots = amps_hbm.shape[0]
    lanes = 128
    wide = side + lanes

    half = side // 2

    def pieces(buffer):
        top, bottom = pl.ds(0, tile_rows), pl.ds(tile_rows, side)
        return (
            buffer.at[:, top, pl.ds(0, tile_cols)],
            buffer.at[:, top, pl.ds(tile_cols, side)],
            buffer.at[:, bottom, pl.ds(0, tile_cols)],
            buffer.at[:, bottom, pl.ds(tile_cols, half)],
            buffer.at[:, bottom, pl.ds(tile_cols + half, half)],
        )

    odd = meta[slots, 0]
    targets = pieces(region)
    sources = (tile_hbm, right_hbm, lower_hbm, corner_a_hbm)
    loads = [
        pltpu.make_async_copy(src, dst, sems.at[n])
        for n, (src, dst) in enumerate(zip(sources, targets))
    ]
    loads.append(pltpu.make_async_copy(amps_hbm, amps, sems.at[5]))
    for load in loads:
        load.start()
    from_side = pltpu.make_async_copy(corner_side_hbm, targets[4], sems.at[4])
    from_below = pltpu.make_async_copy(corner_up_hbm, targets[4], sems.at[4])
    pl.when(odd == 1)(from_side.start)
    pl.when(odd != 1)(from_below.start)
    loads.append(from_side)

    zero_rows = 16

    @pl.loop(0, grads.shape[1] // zero_rows)
    def _(step):
        rows = pl.ds(pl.multiple_of(step * zero_rows, zero_rows), zero_rows)
        grads[:, rows, :] = jnp.zeros((2, zero_rows, grads.shape[2]), jnp.float32)

    @pl.loop(0, side // zero_rows)
    def _(step):
        rows = pl.ds(pl.multiple_of(step * zero_rows, zero_rows), zero_rows)
        dpup[:, rows, :] = jnp.zeros((2, zero_rows, side), jnp.float32)

    for start in (0, side + 8):
        dwin[:, pl.ds(start, 8), :] = jnp.zeros((2, 8, side), jnp.float32)

    for load in loads:
        load.wait()

    def one_slot(slot):
        row = meta[slot, 0]
        col = meta[slot, 1]
        col_base = pl.multiple_of((col // lanes) * lanes, lanes)
        col_shift = col - col_base
        row_base = pl.multiple_of((row // 8) * 8, 8)
        row_shift = row - row_base

        @pl.loop(0, side // 32)
        def _(step):
            base = pl.multiple_of(step * 32, 32)
            for plane in range(2):
                tiles = []
                for i in range(5):
                    start = pl.multiple_of(row_base + base + 8 * i, 8)
                    tiles.append(region[plane, pl.ds(start, 8), pl.ds(col_base, wide)])
                tiles = [pull_lanes(tile, col_shift) for tile in tiles]
                for i, tile in enumerate(pull_rows(tiles, row_shift)):
                    win[plane, pl.ds(base + 8 * i, 8), :] = tile

        @pl.loop(0, short // 16)
        def _(step):
            base = pl.multiple_of(step * 16, 16)
            for part in range(RADIX):
                cols = pl.ds(part * short, short)
                values = []
                for q in range(RADIX):
                    rows = pl.ds(base + q * short, 16)
                    wr, wi = win[0, rows, cols], win[1, rows, cols]
                    pr, pi = pupil[0, rows, cols], pupil[1, rows, cols]
                    values.append((wr * pr - wi * pi, wr * pi + wi * pr))
                for p, (re, im) in enumerate(butterfly(values, 1)):
                    for offset, value in ((0, re), (short, im)):
                        hi, lo = split(value)
                        rows = pl.ds(base + offset, 16)
                        left_hi[p, rows, cols] = hi
                        left_lo[p, rows, cols] = lo

        for p in range(RADIX):
            for half in range(2):
                cols = pl.ds(half * (side // 2), side // 2)
                rows_f32[p, :, cols] = dot3(
                    mat_hi[p], mat_lo[p], left_hi[p, :, cols], left_lo[p, :, cols]
                )

        for p in range(RADIX):

            @pl.loop(0, short // 16)
            def _(step):
                base = pl.multiple_of(step * 16, 16)
                values = []
                for q in range(RADIX):
                    cols = pl.ds(q * short, short)
                    values.append(
                        (
                            rows_f32[p, pl.ds(base, 16), cols],
                            rows_f32[p, pl.ds(base + short, 16), cols],
                        )
                    )
                for t, (re, im) in enumerate(butterfly(values, 1)):
                    for offset, value in ((0, re), (short, im)):
                        hi, lo = split(value)
                        rows = pl.ds(base + p * short, 16)
                        right_hi[t, rows, pl.ds(offset, short)] = hi
                        right_lo[t, rows, pl.ds(offset, short)] = lo

        for t in range(RADIX):
            for half in range(2):
                rows = pl.ds(half * (side // 2), side // 2)
                field = dot3(right_hi[t, rows, :], right_lo[t, rows, :], mat_t_hi[t], mat_t_lo[t])
                fre, fim = field[:, :short], field[:, short:]
                measured = amps[slot, rows, pl.ds(t * short, short)]
                factor = 1.0 - measured * lax.rsqrt(fre * fre + fim * fim + 1.0)
                residual = jnp.concatenate([factor * fre, factor * fim], axis=1)
                hi, lo = split(residual)
                cols_f32[t, rows, :] = dot3(hi, lo, mat_hi[t], mat_lo[t])

        for p in range(RADIX):

            @pl.loop(0, short // 16)
            def _(step):
                base = pl.multiple_of(step * 16, 16)
                rows = pl.ds(base + p * short, 16)
                values = [
                    (cols_f32[t, rows, pl.ds(0, short)], cols_f32[t, rows, pl.ds(short, short)])
                    for t in range(RADIX)
                ]
                for q, (re, im) in enumerate(butterfly(values, -1)):
                    cols = pl.ds(q * short, short)
                    for offset, value in ((0, re), (short, im)):
                        hi, lo = split(value)
                        left_hi[p, pl.ds(base + offset, 16), cols] = hi
                        left_lo[p, pl.ds(base + offset, 16), cols] = lo

        for p in range(RADIX):
            for half in range(2):
                cols = pl.ds(half * (side // 2), side // 2)
                rows_f32[p, :, cols] = dot3(
                    mat_t_hi[p], mat_t_lo[p], left_hi[p, :, cols], left_lo[p, :, cols]
                )

        @pl.loop(0, short // 8)
        def _(step):
            base = pl.multiple_of(step * 8, 8)
            for part in range(RADIX):
                cols = pl.ds(part * short, short)
                values = [
                    (rows_f32[p, pl.ds(base, 8), cols], rows_f32[p, pl.ds(base + short, 8), cols])
                    for p in range(RADIX)
                ]
                for q, (re, im) in enumerate(butterfly(values, -1)):
                    rows = pl.ds(base + q * short, 8)
                    pr, pi = pupil[0, rows, cols], pupil[1, rows, cols]
                    padded = pl.ds(base + q * short + 8, 8)
                    dwin[0, padded, cols] = pr * re + pi * im
                    dwin[1, padded, cols] = pr * im - pi * re
                    wr, wi = win[0, rows, cols], win[1, rows, cols]
                    dpup[0, rows, cols] += wr * re + wi * im
                    dpup[1, rows, cols] += wr * im - wi * re

        @pl.loop(0, (side + 8) // 40)
        def _(step):
            base = pl.multiple_of(step * 40, 8)
            for plane in range(2):
                tiles = [dwin[plane, pl.ds(base + 8 * i, 8), :] for i in range(6)]
                tiles = [push_lanes(tile, col_shift) for tile in tiles]
                for i, tile in enumerate(push_rows(tiles, row_shift)):
                    start = pl.multiple_of(row_base + base + 8 * i, 8)
                    target = (plane, pl.ds(start, 8), pl.ds(col_base, wide))
                    grads[target] = grads[target] + tile

    @pl.loop(0, slots)
    def _(slot):
        pl.when(meta[slot, 2] != 0)(lambda: one_slot(slot))

    targets = (own_out, right_out, lower_out, corner_a_out, corner_b_out)
    stores = [
        pltpu.make_async_copy(src, dst, sems.at[n])
        for n, (src, dst) in enumerate(zip(pieces(grads), targets))
    ]
    for store in stores:
        store.start()
    for store in stores:
        store.wait()


def slots_call(meta, tile, right, lower, corner_a, corner_up, corner_side, amps, pupil):
    side = pupil.shape[-1]
    short = side // RADIX
    slots = amps.shape[0]
    tile_rows, tile_cols = tile.shape[1:]
    high, low = dft_blocks(side)
    tables = [jnp.asarray(x) for x in (high, low, high.transpose(0, 2, 1), low.transpose(0, 2, 1))]
    whole = pl.BlockSpec(memory_space=pltpu.VMEM)
    anywhere = pl.BlockSpec(memory_space=pl.ANY)
    f32, bf16 = jnp.float32, jnp.bfloat16
    region = (2, tile_rows + side, tile_cols + side)
    outs = (tile, right, lower, corner_a, corner_up, pupil)
    return pl.pallas_call(
        slots_kernel,
        out_shape=[jax.ShapeDtypeStruct(x.shape, f32) for x in outs],
        in_specs=[pl.BlockSpec(memory_space=pltpu.SMEM)] + [anywhere] * 7 + [whole] * 5,
        out_specs=[anywhere] * 5 + [whole],
        scratch_shapes=[
            pltpu.VMEM(region, f32),
            pltpu.VMEM(region, f32),
            pltpu.VMEM((2, side, side), f32),
            pltpu.VMEM((RADIX, 2 * short, side), bf16),
            pltpu.VMEM((RADIX, 2 * short, side), bf16),
            pltpu.VMEM((RADIX, side, 2 * short), bf16),
            pltpu.VMEM((RADIX, side, 2 * short), bf16),
            pltpu.VMEM((RADIX, side, 2 * short), f32),
            pltpu.VMEM((RADIX, 2 * short, side), f32),
            pltpu.VMEM((2, side + 16, side), f32),
            pltpu.VMEM(amps.shape, f32),
            pltpu.SemaphoreType.DMA((6,)),
        ],
        compiler_params=pltpu.CompilerParams(vmem_limit_bytes=56 * 1024 * 1024),
        cost_estimate=pl.CostEstimate(
            flops=slots * 48 * 2 * 4 * short * short * side,
            bytes_accessed=40 * 1024 * 1024,
            transcendentals=slots * side * side,
        ),
        name="slots",
    )(meta, tile, right, lower, corner_a, corner_up, corner_side, amps, pupil, *tables)


def exact_parts(value):
    hi, rest = split(value)
    rest = value - hi.astype(jnp.float32)
    return (hi, *split(rest))


def order_kernel(amps, perm_rows, perm_cols, out):
    value = sum(dot(part, perm_cols[...]) for part in exact_parts(amps[0]))
    out[0] = sum(dot(perm_rows[...], part) for part in exact_parts(value))


def ordered(amps):
    slots, side, _ = amps.shape
    index = np.arange(side)
    perm = np.zeros((side, side), ml_dtypes.bfloat16)
    perm[index, (index % RADIX) * (side // RADIX) + index // RADIX] = 1
    block = pl.BlockSpec((1, side, side), lambda s: (s, 0, 0))
    table = pl.BlockSpec((side, side), lambda s: (0, 0))
    return pl.pallas_call(
        order_kernel,
        grid=(slots,),
        out_shape=jax.ShapeDtypeStruct(amps.shape, amps.dtype),
        in_specs=[block, table, table],
        out_specs=block,
        cost_estimate=pl.CostEstimate(
            flops=slots * 12 * side**3, bytes_accessed=8 * slots * side**2, transcendentals=0
        ),
        name="ordered",
    )(amps, jnp.asarray(perm.T), jnp.asarray(perm))


def along(axis_pairs, members):
    n_ty, n_tx = members
    pairs = []
    for i in range(n_ty):
        for j in range(n_tx):
            target = axis_pairs(i, j)
            if target is not None and 0 <= target[0] < n_ty and 0 <= target[1] < n_tx:
                pairs.append((i * n_tx + j, target[0] * n_tx + target[1]))
    return pairs


def send(array, rule):
    sizes = (lax.axis_size("ty"), lax.axis_size("tx"))
    return lax.ppermute(array, ("ty", "tx"), along(rule, sizes))


def halve(value, bit):
    rows = value.shape[0] // 2
    mine = lax.axis_index("ty") // bit % 2
    kept = lax.dynamic_slice_in_dim(value, mine * rows, rows, 0)
    sent = lax.dynamic_slice_in_dim(value, (1 - mine) * rows, rows, 0)
    return kept + lax.ppermute(sent, "ty", [(i, i ^ bit) for i in range(lax.axis_size("ty"))])


def double(value, bit):
    mine = lax.axis_index("ty") // bit % 2
    other = lax.ppermute(value, "ty", [(i, i ^ bit) for i in range(lax.axis_size("ty"))])
    first = jnp.where(mine == 0, value, other)
    second = jnp.where(mine == 0, other, value)
    return jnp.concatenate([first, second], axis=0)


def ring_pairs(size, step):
    return [(i, (i + step) % size) for i in range(size)]


def scatter_tx(value):
    size, own = lax.axis_size("tx"), lax.axis_index("tx")
    rows = value.shape[0] // size
    total = lax.dynamic_slice_in_dim(value, own * rows, rows, 0)
    for step in range(1, size):
        piece = lax.dynamic_slice_in_dim(value, (own + step) % size * rows, rows, 0)
        total = total + lax.ppermute(piece, "tx", ring_pairs(size, step))
    return total


def gather_tx(value):
    size, own = lax.axis_size("tx"), lax.axis_index("tx")
    rows = value.shape[0]
    parts = [value]
    for step in range(1, size):
        parts.append(lax.ppermute(value, "tx", ring_pairs(size, step)))
    out = jnp.zeros((size * rows,) + value.shape[1:], value.dtype)
    for step, part in enumerate(parts):
        out = lax.dynamic_update_slice_in_dim(out, part, (own - step) % size * rows, 0)
    return out


def pupil_sum(dpup):
    n_ty, n_tx = lax.axis_size("ty"), lax.axis_size("tx")
    bits = [1]
    bit = n_ty // 2
    while bit > 1:
        bits.append(bit)
        bit //= 2
    part = dpup.reshape(-1, dpup.shape[-1])
    for bit in bits:
        part = halve(part, bit)
    part = scatter_tx(part) * (1.0 / math.sqrt(n_ty * n_tx))
    part = gather_tx(part)
    for bit in reversed(bits):
        part = double(part, bit)
    return part.reshape(dpup.shape)


def body(spectrum, pupil, amplitudes, offsets, live):
    side = pupil.shape[-1]
    half = side // 2
    tile_rows, tile_cols = spectrum.shape[1:]
    own_ty, own_tx = lax.axis_index("ty"), lax.axis_index("tx")
    rows_local = offsets[:, 0] - own_ty * tile_rows
    cols_local = offsets[:, 1] - own_tx * tile_cols
    meta = jnp.stack([rows_local, cols_local, live], axis=1)
    meta = jnp.concatenate([meta, jnp.full((1, 3), own_ty % 2, jnp.int32)], axis=0)

    right = send(spectrum[:, :, :side], lambda i, j: (i, j - 1))
    lower = send(spectrum[:, :side, :], lambda i, j: (i - 1, j))
    corner_a = send(right[:, :, :half], lambda i, j: (i - 1, j))
    corner_up = send(right[:, :, half:], lambda i, j: (i - 1, j) if i % 2 else None)
    corner_side = send(lower[:, :, half:side], lambda i, j: (i, j - 1) if i % 2 else None)

    own_g, right_g, lower_g, corner_a_g, corner_b_g, dpup = slots_call(
        meta, spectrum, right, lower, corner_a, corner_up, corner_side, ordered(amplitudes), pupil
    )

    back_a = send(corner_a_g, lambda i, j: (i + 1, j))
    back_down = send(corner_b_g, lambda i, j: None if i % 2 else (i + 1, j))
    back_side = send(corner_b_g, lambda i, j: (i, j + 1) if i % 2 else None)
    right_total = right_g + jnp.concatenate([back_a, back_down], axis=2)
    lower_total = lower_g.at[:, :, half:side].add(back_side)
    right_total, lower_total = lax.optimization_barrier((right_total, lower_total))
    right_back = send(right_total, lambda i, j: (i, j + 1))
    lower_back = send(lower_total, lambda i, j: (i + 1, j))
    spec_grad = (own_g + lower_back).at[:, :, :side].add(right_back)
    return spec_grad, pupil_sum(dpup)


def solution(mesh):
    return jax.shard_map(
        body,
        mesh=mesh,
        in_specs=(
            P(None, "ty", "tx"),
            P(),
            P(("ty", "tx"), None, None),
            P(("ty", "tx"), None),
            P(("ty", "tx")),
        ),
        out_specs=(P(None, "ty", "tx"), P()),
        check_vma=False,
    )
```

```python
import math

import jax
import jax.numpy as jnp
import ml_dtypes
import numpy as np
from jax import lax
from jax.experimental import pallas as pl
from jax.experimental.pallas import tpu as pltpu
from jax.sharding import PartitionSpec as P

RADIX = 4


def dft_blocks(length):
    short = length // RADIX
    out_idx = np.arange(short)[:, None]
    in_idx = np.arange(short)[None, :]
    blocks = []
    for p in range(RADIX):
        phase = (p * in_idx + RADIX * out_idx * in_idx) % length
        angle = phase * (2.0 * math.pi / length)
        cos = np.cos(angle) / math.sqrt(length)
        sin = np.sin(angle) / math.sqrt(length)
        blocks.append(np.block([[cos, -sin], [sin, cos]]))
    full = np.stack(blocks).astype(np.float32)
    high = full.astype(ml_dtypes.bfloat16)
    low = (full - high.astype(np.float32)).astype(ml_dtypes.bfloat16)
    return high, low


def split(value):
    high = value.astype(jnp.bfloat16)
    low = (value - high.astype(jnp.float32)).astype(jnp.bfloat16)
    return high, low


def dot(lhs, rhs):
    return jnp.dot(lhs, rhs, preferred_element_type=jnp.float32)


def left_dot(mat_hi, mat_lo, val_hi, val_lo):
    lhs = jnp.concatenate([mat_hi, mat_hi, mat_lo], axis=1)
    return dot(lhs, jnp.concatenate([val_hi, val_lo, val_hi], axis=0))


def right_dot(val_hi, val_lo, mat_hi, mat_lo):
    lhs = jnp.concatenate([val_hi, val_lo, val_hi], axis=1)
    return dot(lhs, jnp.concatenate([mat_hi, mat_hi, mat_lo], axis=0))


def butterfly(parts, sign):
    (r0, i0), (r1, i1), (r2, i2), (r3, i3) = parts
    sr, si, dr, di = r0 + r2, i0 + i2, r0 - r2, i0 - i2
    tr, ti, er, ei = r1 + r3, i1 + i3, r1 - r3, i1 - i3
    if sign < 0:
        er, ei = -er, -ei
    return [(sr + tr, si + ti), (dr - ei, di + er), (sr - tr, si - ti), (dr + ei, di - er)]


def row_index():
    return lax.broadcasted_iota(jnp.int32, (8, 128), 0)


def lane_index():
    return lax.broadcasted_iota(jnp.int32, (8, 128), 1)


def lane_tiles(tile):
    return [tile[:, i : i + 128] for i in range(0, tile.shape[1], 128)]


def pull_lanes(tile, shift):
    rolled = [pltpu.roll(part, (128 - shift) % 128, 1) for part in lane_tiles(tile)]
    keep = lane_index() < 128 - shift
    return [jnp.where(keep, a, b) for a, b in zip(rolled, rolled[1:])]


def pull_rows(tiles, shift):
    rolled = [[pltpu.roll(part, (8 - shift) % 8, 0) for part in tile] for tile in tiles]
    keep = row_index() < 8 - shift
    return [
        jnp.concatenate([jnp.where(keep, x, y) for x, y in zip(a, b)], axis=1)
        for a, b in zip(rolled, rolled[1:])
    ]


def push_lanes(tile, shift):
    rolled = [pltpu.roll(part, shift, 1) for part in lane_tiles(tile)]
    zero = jnp.zeros((8, 128), jnp.float32)
    keep = lane_index() >= shift
    return [jnp.where(keep, b, a) for a, b in zip([zero] + rolled, rolled + [zero])]


def push_rows(tiles, shift):
    rolled = [[pltpu.roll(part, shift, 0) for part in tile] for tile in tiles]
    keep = row_index() >= shift
    return [
        jnp.concatenate([jnp.where(keep, y, x) for x, y in zip(a, b)], axis=1)
        for a, b in zip(rolled, rolled[1:])
    ]


def slots_kernel(
    meta,
    tile_hbm,
    right_a_hbm,
    right_b_hbm,
    lower_a_hbm,
    lower_b_hbm,
    lower_c_hbm,
    corner_a_hbm,
    corner_up_hbm,
    corner_side_hbm,
    amps_hbm,
    pupil_hbm,
    mat_hi_hbm,
    mat_lo_hbm,
    mat_t_hi_hbm,
    mat_t_lo_hbm,
    own_out,
    right_a_out,
    right_b_out,
    lower_a_out,
    lower_b_out,
    lower_c_out,
    corner_a_out,
    corner_b_out,
    dpup_out,
    region,
    grads,
    win,
    left_hi,
    left_lo,
    right_hi,
    right_lo,
    cols_f32,
    rows_f32,
    dwin,
    dpup,
    amps,
    pupil,
    mat_hi,
    mat_lo,
    mat_t_hi,
    mat_t_lo,
    in_sems,
    out_sems,
):
    side = pupil.shape[-1]
    short = side // RADIX
    tile_rows, tile_cols = tile_hbm.shape[1:]
    slots = amps_hbm.shape[0]
    lanes = 128
    wide = side + lanes
    half = side // 2

    def pieces(buffer):
        top, bottom = pl.ds(0, tile_rows), pl.ds(tile_rows, side)
        return (
            buffer.at[:, top, pl.ds(0, tile_cols)],
            buffer.at[:, top, pl.ds(tile_cols, half)],
            buffer.at[:, top, pl.ds(tile_cols + half, half)],
            buffer.at[:, bottom, pl.ds(0, half)],
            buffer.at[:, bottom, pl.ds(half, half)],
            buffer.at[:, bottom, pl.ds(side, tile_cols - side)],
            buffer.at[:, bottom, pl.ds(tile_cols, half)],
            buffer.at[:, bottom, pl.ds(tile_cols + half, half)],
        )

    odd = meta[slots, 0]
    targets = pieces(region)
    sources = (
        tile_hbm,
        right_a_hbm,
        right_b_hbm,
        lower_a_hbm,
        lower_b_hbm,
        lower_c_hbm,
        corner_a_hbm,
    )
    loads = [
        pltpu.make_async_copy(src, dst, in_sems.at[n])
        for n, (src, dst) in enumerate(zip(sources, targets))
    ]
    for load in loads:
        load.start()
    from_side = pltpu.make_async_copy(corner_side_hbm, targets[7], in_sems.at[7])
    from_below = pltpu.make_async_copy(corner_up_hbm, targets[7], in_sems.at[7])
    pl.when(odd == 1)(from_side.start)
    pl.when(odd != 1)(from_below.start)
    loads.append(from_side)
    late = (
        (pupil_hbm, pupil),
        (mat_hi_hbm, mat_hi),
        (mat_lo_hbm, mat_lo),
        (mat_t_hi_hbm, mat_t_hi),
        (mat_t_lo_hbm, mat_t_lo),
        (amps_hbm, amps),
    )
    late_loads = [
        pltpu.make_async_copy(src, dst, in_sems.at[8 + n]) for n, (src, dst) in enumerate(late)
    ]
    for load in late_loads:
        load.start()

    outs = (
        own_out,
        right_a_out,
        right_b_out,
        lower_a_out,
        lower_b_out,
        lower_c_out,
        corner_a_out,
        corner_b_out,
    )
    stores = [
        pltpu.make_async_copy(src, dst, out_sems.at[n])
        for n, (src, dst) in enumerate(zip(pieces(grads), outs))
    ]
    dpup_store = pltpu.make_async_copy(dpup, dpup_out, out_sems.at[8])
    lower_stores = stores[3:]
    upper_stores = stores[:3]

    zero_rows = 16

    @pl.loop(0, grads.shape[1] // zero_rows)
    def _(step):
        rows = pl.ds(pl.multiple_of(step * zero_rows, zero_rows), zero_rows)
        grads[:, rows, :] = jnp.zeros((2, zero_rows, grads.shape[2]), jnp.float32)

    @pl.loop(0, side // zero_rows)
    def _(step):
        rows = pl.ds(pl.multiple_of(step * zero_rows, zero_rows), zero_rows)
        dpup[:, rows, :] = jnp.zeros((2, zero_rows, side), jnp.float32)

    for start in (0, side + 8):
        dwin[:, pl.ds(start, 8), :] = jnp.zeros((2, 8, side), jnp.float32)

    for load in loads:
        load.wait()

    count = meta[0, 2]
    for slot in range(1, slots):
        count = count + meta[slot, 2]

    def one_slot(slot):
        row = meta[slot, 0]
        col = meta[slot, 1]
        col_base = pl.multiple_of((col // lanes) * lanes, lanes)
        col_shift = col - col_base
        row_base = pl.multiple_of((row // 8) * 8, 8)
        row_shift = row - row_base

        @pl.loop(0, side // 32)
        def _(step):
            base = pl.multiple_of(step * 32, 32)
            for plane in range(2):
                tiles = []
                for i in range(5):
                    start = pl.multiple_of(row_base + base + 8 * i, 8)
                    tiles.append(region[plane, pl.ds(start, 8), pl.ds(col_base, wide)])
                tiles = [pull_lanes(tile, col_shift) for tile in tiles]
                for i, tile in enumerate(pull_rows(tiles, row_shift)):
                    win[plane, pl.ds(base + 8 * i, 8), :] = tile

        @pl.when(slot == 0)
        def _():
            for load in late_loads:
                load.wait()

        @pl.loop(0, short // 16)
        def _(step):
            base = pl.multiple_of(step * 16, 16)
            for part in range(RADIX):
                cols = pl.ds(part * short, short)
                values = []
                for q in range(RADIX):
                    rows = pl.ds(base + q * short, 16)
                    wr, wi = win[0, rows, cols], win[1, rows, cols]
                    pr, pi = pupil[0, rows, cols], pupil[1, rows, cols]
                    values.append((wr * pr - wi * pi, wr * pi + wi * pr))
                for p, (re, im) in enumerate(butterfly(values, 1)):
                    for offset, value in ((0, re), (short, im)):
                        hi, lo = split(value)
                        rows = pl.ds(base + offset, 16)
                        left_hi[p, rows, cols] = hi
                        left_lo[p, rows, cols] = lo

        for p in range(RADIX):
            for half in range(2):
                cols = pl.ds(half * (side // 2), side // 2)
                rows_f32[p, :, cols] = left_dot(
                    mat_hi[p], mat_lo[p], left_hi[p, :, cols], left_lo[p, :, cols]
                )

        for p in range(RADIX):

            @pl.loop(0, short // 16, unroll=2)
            def _(step):
                base = pl.multiple_of(step * 16, 16)
                values = []
                for q in range(RADIX):
                    cols = pl.ds(q * short, short)
                    values.append(
                        (
                            rows_f32[p, pl.ds(base, 16), cols],
                            rows_f32[p, pl.ds(base + short, 16), cols],
                        )
                    )
                for t, (re, im) in enumerate(butterfly(values, 1)):
                    for offset, value in ((0, re), (short, im)):
                        hi, lo = split(value)
                        rows = pl.ds(base + p * short, 16)
                        right_hi[t, rows, pl.ds(offset, short)] = hi
                        right_lo[t, rows, pl.ds(offset, short)] = lo

        for t in range(RADIX):
            for half in range(2):
                rows = pl.ds(half * (side // 2), side // 2)
                field = right_dot(
                    right_hi[t, rows, :], right_lo[t, rows, :], mat_t_hi[t], mat_t_lo[t]
                )
                fre, fim = field[:, :short], field[:, short:]
                measured = amps[slot, rows, pl.ds(t * short, short)]
                factor = 1.0 - measured * lax.rsqrt(fre * fre + fim * fim + 1.0)
                residual = jnp.concatenate([factor * fre, factor * fim], axis=1)
                hi, lo = split(residual)
                cols_f32[t, rows, :] = right_dot(hi, lo, mat_hi[t], mat_lo[t])

        for p in range(RADIX):

            @pl.loop(0, short // 16, unroll=2)
            def _(step):
                base = pl.multiple_of(step * 16, 16)
                rows = pl.ds(base + p * short, 16)
                values = [
                    (cols_f32[t, rows, pl.ds(0, short)], cols_f32[t, rows, pl.ds(short, short)])
                    for t in range(RADIX)
                ]
                for q, (re, im) in enumerate(butterfly(values, -1)):
                    cols = pl.ds(q * short, short)
                    for offset, value in ((0, re), (short, im)):
                        hi, lo = split(value)
                        left_hi[p, pl.ds(base + offset, 16), cols] = hi
                        left_lo[p, pl.ds(base + offset, 16), cols] = lo

        for p in range(RADIX):
            for half in range(2):
                cols = pl.ds(half * (side // 2), side // 2)
                rows_f32[p, :, cols] = left_dot(
                    mat_t_hi[p], mat_t_lo[p], left_hi[p, :, cols], left_lo[p, :, cols]
                )

        @pl.loop(0, short // 8)
        def _(step):
            base = pl.multiple_of(step * 8, 8)
            for part in range(RADIX):
                cols = pl.ds(part * short, short)
                values = [
                    (rows_f32[p, pl.ds(base, 8), cols], rows_f32[p, pl.ds(base + short, 8), cols])
                    for p in range(RADIX)
                ]
                for q, (re, im) in enumerate(butterfly(values, -1)):
                    rows = pl.ds(base + q * short, 8)
                    pr, pi = pupil[0, rows, cols], pupil[1, rows, cols]
                    padded = pl.ds(base + q * short + 8, 8)
                    dwin[0, padded, cols] = pr * re + pi * im
                    dwin[1, padded, cols] = pr * im - pi * re
                    wr, wi = win[0, rows, cols], win[1, rows, cols]
                    dpup[0, rows, cols] += wr * re + wi * im
                    dpup[1, rows, cols] += wr * im - wi * re

        last = slot == count - 1
        pl.when(last)(dpup_store.start)

        def place(step):
            base = pl.multiple_of(step * 40, 8)
            for plane in range(2):
                tiles = [dwin[plane, pl.ds(base + 8 * i, 8), :] for i in range(6)]
                tiles = [push_lanes(tile, col_shift) for tile in tiles]
                for i, tile in enumerate(push_rows(tiles, row_shift)):
                    start = pl.multiple_of(row_base + base + 8 * i, 8)
                    target = (plane, pl.ds(start, 8), pl.ds(col_base, wide))
                    grads[target] = grads[target] + tile

        steps = (side + 8) // 40
        above = (tile_rows - row_base) // 40
        pl.loop(above, steps)(place)

        @pl.when(last)
        def _():
            for store in lower_stores:
                store.start()

        pl.loop(0, above)(place)

    pl.loop(0, count)(one_slot)

    @pl.when(count == 0)
    def _():
        for store in [dpup_store] + lower_stores:
            store.start()
        for load in late_loads:
            load.wait()

    for store in upper_stores:
        store.start()
    for store in [dpup_store] + stores:
        store.wait()


def slots_call(meta, tile, parts, amps, pupil):
    side = pupil.shape[-1]
    short = side // RADIX
    slots = amps.shape[0]
    tile_rows, tile_cols = tile.shape[1:]
    high, low = dft_blocks(side)
    tables = [jnp.asarray(x) for x in (high, low, high.transpose(0, 2, 1), low.transpose(0, 2, 1))]
    anywhere = pl.BlockSpec(memory_space=pl.ANY)
    f32, bf16 = jnp.float32, jnp.bfloat16
    region = (2, tile_rows + side, tile_cols + side)
    outs = (tile, *parts[:-1], pupil)
    table = pltpu.VMEM(high.shape, bf16)
    return pl.pallas_call(
        slots_kernel,
        out_shape=[jax.ShapeDtypeStruct(x.shape, f32) for x in outs],
        in_specs=[pl.BlockSpec(memory_space=pltpu.SMEM)] + [anywhere] * (len(parts) + 7),
        out_specs=[anywhere] * len(outs),
        scratch_shapes=[
            pltpu.VMEM(region, f32),
            pltpu.VMEM(region, f32),
            pltpu.VMEM((2, side, side), f32),
            pltpu.VMEM((RADIX, 2 * short, side), bf16),
            pltpu.VMEM((RADIX, 2 * short, side), bf16),
            pltpu.VMEM((RADIX, side, 2 * short), bf16),
            pltpu.VMEM((RADIX, side, 2 * short), bf16),
            pltpu.VMEM((RADIX, side, 2 * short), f32),
            pltpu.VMEM((RADIX, 2 * short, side), f32),
            pltpu.VMEM((2, side + 16, side), f32),
            pltpu.VMEM((2, side, side), f32),
            pltpu.VMEM(amps.shape, f32),
            pltpu.VMEM(pupil.shape, f32),
            table,
            table,
            table,
            table,
            pltpu.SemaphoreType.DMA((14,)),
            pltpu.SemaphoreType.DMA((9,)),
        ],
        compiler_params=pltpu.CompilerParams(vmem_limit_bytes=56 * 1024 * 1024),
        cost_estimate=pl.CostEstimate(
            flops=slots * 48 * 2 * 4 * short * short * side,
            bytes_accessed=40 * 1024 * 1024,
            transcendentals=slots * side * side,
        ),
        name="slots",
    )(meta, tile, *parts, amps, pupil, *tables)


def exact_parts(value):
    hi, rest = split(value)
    rest = value - hi.astype(jnp.float32)
    return (hi, *split(rest))


def order_kernel(amps, perm_rows, perm_cols, out):
    value = sum(dot(part, perm_cols[...]) for part in exact_parts(amps[0]))
    out[0] = sum(dot(perm_rows[...], part) for part in exact_parts(value))


def ordered(amps):
    slots, side, _ = amps.shape
    index = np.arange(side)
    perm = np.zeros((side, side), ml_dtypes.bfloat16)
    perm[index, (index % RADIX) * (side // RADIX) + index // RADIX] = 1
    block = pl.BlockSpec((1, side, side), lambda s: (s, 0, 0))
    table = pl.BlockSpec((side, side), lambda s: (0, 0))
    return pl.pallas_call(
        order_kernel,
        grid=(slots,),
        out_shape=jax.ShapeDtypeStruct(amps.shape, amps.dtype),
        in_specs=[block, table, table],
        out_specs=block,
        cost_estimate=pl.CostEstimate(
            flops=slots * 12 * side**3, bytes_accessed=8 * slots * side**2, transcendentals=0
        ),
        name="ordered",
    )(amps, jnp.asarray(perm.T), jnp.asarray(perm))


def along(axis_pairs, members):
    n_ty, n_tx = members
    pairs = []
    for i in range(n_ty):
        for j in range(n_tx):
            target = axis_pairs(i, j)
            if target is not None and 0 <= target[0] < n_ty and 0 <= target[1] < n_tx:
                pairs.append((i * n_tx + j, target[0] * n_tx + target[1]))
    return pairs


def send(array, rule):
    sizes = (lax.axis_size("ty"), lax.axis_size("tx"))
    return lax.ppermute(array, ("ty", "tx"), along(rule, sizes))


def add_kernel(left, right, out):
    out[...] = left[...] + right[...]


def add_beside_transfers(left, right):
    return pl.pallas_call(
        add_kernel,
        out_shape=jax.ShapeDtypeStruct(left.shape, left.dtype),
        cost_estimate=pl.CostEstimate(flops=60 * 10**9, bytes_accessed=2**27, transcendentals=0),
        name="add_beside_transfers",
    )(left, right)


def halve(value, bit, beside=False):
    rows = value.shape[0] // 2
    mine = lax.axis_index("ty") // bit % 2
    kept = lax.dynamic_slice_in_dim(value, mine * rows, rows, 0)
    sent = lax.dynamic_slice_in_dim(value, (1 - mine) * rows, rows, 0)
    received = lax.ppermute(sent, "ty", [(i, i ^ bit) for i in range(lax.axis_size("ty"))])
    return add_beside_transfers(kept, received) if beside else kept + received


def double(value, bit):
    mine = lax.axis_index("ty") // bit % 2
    other = lax.ppermute(value, "ty", [(i, i ^ bit) for i in range(lax.axis_size("ty"))])
    first = jnp.where(mine == 0, value, other)
    second = jnp.where(mine == 0, other, value)
    return jnp.concatenate([first, second], axis=0)


def ring_pairs(size, step):
    return [(i, (i + step) % size) for i in range(size)]


def scatter_tx(value):
    size, own = lax.axis_size("tx"), lax.axis_index("tx")
    rows = value.shape[0] // size
    total = lax.dynamic_slice_in_dim(value, own * rows, rows, 0)
    for step in range(1, size):
        piece = lax.dynamic_slice_in_dim(value, (own + step) % size * rows, rows, 0)
        total = total + lax.ppermute(piece, "tx", ring_pairs(size, step))
    return total


def gather_tx(value):
    size, own = lax.axis_size("tx"), lax.axis_index("tx")
    rows = value.shape[0]
    parts = [value]
    for step in range(1, size):
        parts.append(lax.ppermute(value, "tx", ring_pairs(size, step)))
    out = jnp.zeros((size * rows,) + value.shape[1:], value.dtype)
    for step, part in enumerate(parts):
        out = lax.dynamic_update_slice_in_dim(out, part, (own - step) % size * rows, 0)
    return out


def pupil_sum(dpup):
    n_ty, n_tx = lax.axis_size("ty"), lax.axis_size("tx")
    bits = [1]
    bit = n_ty // 2
    while bit > 1:
        bits.append(bit)
        bit //= 2
    part = dpup.reshape(-1, dpup.shape[-1])
    for number, bit in enumerate(bits):
        part = halve(part, bit, number == 1)
    part = scatter_tx(part) * (1.0 / math.sqrt(n_ty * n_tx))
    part = gather_tx(part)
    for bit in reversed(bits):
        part = double(part, bit)
    return part.reshape(dpup.shape)


def body(spectrum, pupil, amplitudes, offsets, live):
    side = pupil.shape[-1]
    half = side // 2
    tile_rows, tile_cols = spectrum.shape[1:]
    own_ty, own_tx = lax.axis_index("ty"), lax.axis_index("tx")
    rows_local = offsets[:, 0] - own_ty * tile_rows
    cols_local = offsets[:, 1] - own_tx * tile_cols
    meta = jnp.stack([rows_local, cols_local, live], axis=1)
    meta = jnp.concatenate([meta, jnp.full((1, 3), own_ty % 2, jnp.int32)], axis=0)

    def left(i, j):
        return (i, j - 1)

    def up(i, j):
        return (i - 1, j)

    lower_b = send(spectrum[:, :side, half:side], up)
    right_a = send(spectrum[:, :, :half], left)
    right_b = send(spectrum[:, :, half:side], left)
    lower_a = send(spectrum[:, :side, :half], up)
    lower_c = send(spectrum[:, :side, side:], up)
    amps = ordered(amplitudes)
    lower_b, amps = lax.optimization_barrier((lower_b, amps))
    corner_side = send(lower_b, lambda i, j: (i, j - 1) if i % 2 else None)
    corner_a = send(right_a[:, :side], up)
    corner_up = send(right_b[:, :side], lambda i, j: (i - 1, j) if i % 2 else None)

    parts = (right_a, right_b, lower_a, lower_b, lower_c, corner_a, corner_up, corner_side)
    own_g, *grads, dpup = slots_call(meta, spectrum, parts, amps, pupil)
    right_a_g, right_b_g, lower_a_g, lower_b_g, lower_c_g, corner_a_g, corner_b_g = grads

    def down(i, j):
        return (i + 1, j)

    def right(i, j):
        return (i, j + 1)

    back_side = send(corner_b_g, lambda i, j: (i, j + 1) if i % 2 else None)
    back_a = send(corner_a_g, down)
    back_down = send(corner_b_g, lambda i, j: None if i % 2 else (i + 1, j))
    lower_a = send(lower_a_g, down)
    lower_c = send(lower_c_g, down)
    right_b = send(right_b_g + back_down, right)
    right_a = send(right_a_g + back_a, right)
    lower_b = send(lower_b_g + back_side, down)
    spec_grad = jnp.concatenate(
        [
            own_g[:, :, :half] + lower_a + right_a,
            own_g[:, :, half:side] + lower_b + right_b,
            own_g[:, :, side:] + lower_c,
        ],
        axis=2,
    )
    return spec_grad, pupil_sum(dpup)


def solution(mesh):
    return jax.shard_map(
        body,
        mesh=mesh,
        in_specs=(
            P(None, "ty", "tx"),
            P(),
            P(("ty", "tx"), None, None),
            P(("ty", "tx"), None),
            P(("ty", "tx")),
        ),
        out_specs=(P(None, "ty", "tx"), P()),
        check_vma=False,
    )
```

```python
import functools
import itertools
import math

import jax
import jax.numpy as jnp
import ml_dtypes
import numpy as np
from jax import lax
from jax.experimental import pallas as pl
from jax.experimental.pallas import tpu as pltpu
from jax.sharding import PartitionSpec as P

RADIX = 4


def dft_blocks(length):
    short = length // RADIX
    out_idx = np.arange(short)[:, None]
    in_idx = np.arange(short)[None, :]
    blocks = []
    for p in range(RADIX):
        phase = (p * in_idx + RADIX * out_idx * in_idx) % length
        angle = phase * (2.0 * math.pi / length)
        cos = np.cos(angle) / math.sqrt(length)
        sin = np.sin(angle) / math.sqrt(length)
        blocks.append(np.block([[cos, -sin], [sin, cos]]))
    full = np.stack(blocks).astype(np.float32)
    high = full.astype(ml_dtypes.bfloat16)
    low = (full - high.astype(np.float32)).astype(ml_dtypes.bfloat16)
    return high, low


def split(value):
    high = value.astype(jnp.bfloat16)
    low = (value - high.astype(jnp.float32)).astype(jnp.bfloat16)
    return high, low


def dot(lhs, rhs):
    return jnp.dot(lhs, rhs, preferred_element_type=jnp.float32)


def left_dot(mat_hi, mat_lo, val_hi, val_lo):
    lhs = jnp.concatenate([mat_hi, mat_hi, mat_lo], axis=1)
    return dot(lhs, jnp.concatenate([val_hi, val_lo, val_hi], axis=0))


def right_dot(val_hi, val_lo, mat_hi, mat_lo):
    lhs = jnp.concatenate([val_hi, val_lo, val_hi], axis=1)
    return dot(lhs, jnp.concatenate([mat_hi, mat_hi, mat_lo], axis=0))


def butterfly(parts, sign):
    (r0, i0), (r1, i1), (r2, i2), (r3, i3) = parts
    sr, si, dr, di = r0 + r2, i0 + i2, r0 - r2, i0 - i2
    tr, ti, er, ei = r1 + r3, i1 + i3, r1 - r3, i1 - i3
    if sign < 0:
        er, ei = -er, -ei
    return [(sr + tr, si + ti), (dr - ei, di + er), (sr - tr, si - ti), (dr + ei, di - er)]


def row_index():
    return lax.broadcasted_iota(jnp.int32, (8, 128), 0)


def lane_index():
    return lax.broadcasted_iota(jnp.int32, (8, 128), 1)


def lane_tiles(tile):
    return [tile[:, i : i + 128] for i in range(0, tile.shape[1], 128)]


def pull_lanes(tile, shift):
    rolled = [pltpu.roll(part, (128 - shift) % 128, 1) for part in lane_tiles(tile)]
    keep = lane_index() < 128 - shift
    return [jnp.where(keep, a, b) for a, b in zip(rolled, rolled[1:])]


def pull_rows(tiles, shift):
    rolled = [[pltpu.roll(part, (8 - shift) % 8, 0) for part in tile] for tile in tiles]
    keep = row_index() < 8 - shift
    return [
        jnp.concatenate([jnp.where(keep, x, y) for x, y in zip(a, b)], axis=1)
        for a, b in zip(rolled, rolled[1:])
    ]


def push_lanes(tile, shift):
    rolled = [pltpu.roll(part, shift, 1) for part in lane_tiles(tile)]
    zero = jnp.zeros((8, 128), jnp.float32)
    keep = lane_index() >= shift
    return [jnp.where(keep, b, a) for a, b in zip([zero] + rolled, rolled + [zero])]


def push_rows(tiles, shift):
    rolled = [[pltpu.roll(part, shift, 0) for part in tile] for tile in tiles]
    keep = row_index() >= shift
    return [
        jnp.concatenate([jnp.where(keep, y, x) for x, y in zip(a, b)], axis=1)
        for a, b in zip(rolled, rolled[1:])
    ]


def slots_kernel(
    meta,
    tile_hbm,
    right_a_hbm,
    right_b_hbm,
    lower_a_hbm,
    lower_b_hbm,
    lower_c_hbm,
    corner_a_hbm,
    corner_up_hbm,
    corner_side_hbm,
    amps_hbm,
    pupil_hbm,
    mat_hi_hbm,
    mat_lo_hbm,
    mat_t_hi_hbm,
    mat_t_lo_hbm,
    own_out,
    right_a_out,
    right_b_out,
    lower_a_out,
    lower_b_out,
    lower_c_out,
    corner_a_out,
    corner_b_out,
    dpup_out,
    region,
    grads,
    win,
    left_hi,
    left_lo,
    right_hi,
    right_lo,
    cols_f32,
    rows_f32,
    dwin,
    dpup,
    amps,
    pupil,
    mat_hi,
    mat_lo,
    mat_t_hi,
    mat_t_lo,
    in_sems,
    out_sems,
):
    side = pupil.shape[-1]
    short = side // RADIX
    tile_rows, tile_cols = tile_hbm.shape[1:]
    slots = amps_hbm.shape[0]
    lanes = 128
    wide = side + lanes
    half = side // 2

    def pieces(buffer):
        top, bottom = pl.ds(0, tile_rows), pl.ds(tile_rows, side)
        return (
            buffer.at[:, top, pl.ds(0, tile_cols)],
            buffer.at[:, top, pl.ds(tile_cols, half)],
            buffer.at[:, top, pl.ds(tile_cols + half, half)],
            buffer.at[:, bottom, pl.ds(0, half)],
            buffer.at[:, bottom, pl.ds(half, half)],
            buffer.at[:, bottom, pl.ds(side, tile_cols - side)],
            buffer.at[:, bottom, pl.ds(tile_cols, half)],
            buffer.at[:, bottom, pl.ds(tile_cols + half, half)],
        )

    odd = meta[slots, 0]
    targets = pieces(region)
    sources = (
        tile_hbm,
        right_a_hbm,
        right_b_hbm,
        lower_a_hbm,
        lower_b_hbm,
        lower_c_hbm,
        corner_a_hbm,
    )
    loads = [
        pltpu.make_async_copy(src, dst, in_sems.at[n])
        for n, (src, dst) in enumerate(zip(sources, targets))
    ]
    for load in loads:
        load.start()
    from_side = pltpu.make_async_copy(corner_side_hbm, targets[7], in_sems.at[7])
    from_below = pltpu.make_async_copy(corner_up_hbm, targets[7], in_sems.at[7])
    pl.when(odd == 1)(from_side.start)
    pl.when(odd != 1)(from_below.start)
    loads.append(from_side)
    late = (
        (pupil_hbm, pupil),
        (mat_hi_hbm, mat_hi),
        (mat_lo_hbm, mat_lo),
        (mat_t_hi_hbm, mat_t_hi),
        (mat_t_lo_hbm, mat_t_lo),
        (amps_hbm, amps),
    )
    late_loads = [
        pltpu.make_async_copy(src, dst, in_sems.at[8 + n]) for n, (src, dst) in enumerate(late)
    ]
    for load in late_loads:
        load.start()

    outs = (
        own_out,
        right_a_out,
        right_b_out,
        lower_a_out,
        lower_b_out,
        lower_c_out,
        corner_a_out,
        corner_b_out,
    )
    stores = [
        pltpu.make_async_copy(src, dst, out_sems.at[n])
        for n, (src, dst) in enumerate(zip(pieces(grads), outs))
    ]
    dpup_store = pltpu.make_async_copy(dpup, dpup_out, out_sems.at[8])
    lower_stores = stores[3:]
    upper_stores = stores[:3]

    zero_rows = 16

    @pl.loop(0, grads.shape[1] // zero_rows)
    def _(step):
        rows = pl.ds(pl.multiple_of(step * zero_rows, zero_rows), zero_rows)
        grads[:, rows, :] = jnp.zeros((2, zero_rows, grads.shape[2]), jnp.float32)

    @pl.loop(0, side // zero_rows)
    def _(step):
        rows = pl.ds(pl.multiple_of(step * zero_rows, zero_rows), zero_rows)
        dpup[:, rows, :] = jnp.zeros((2, zero_rows, side), jnp.float32)

    for start in (0, side + 8):
        dwin[:, pl.ds(start, 8), :] = jnp.zeros((2, 8, side), jnp.float32)

    for load in loads:
        load.wait()

    count = meta[0, 2]
    for slot in range(1, slots):
        count = count + meta[slot, 2]

    def one_slot(slot):
        row = meta[slot, 0]
        col = meta[slot, 1]
        col_base = pl.multiple_of((col // lanes) * lanes, lanes)
        col_shift = col - col_base
        row_base = pl.multiple_of((row // 8) * 8, 8)
        row_shift = row - row_base

        @pl.loop(0, side // 32, unroll=2)
        def _(step):
            base = pl.multiple_of(step * 32, 32)
            for plane in range(2):
                tiles = []
                for i in range(5):
                    start = pl.multiple_of(row_base + base + 8 * i, 8)
                    tiles.append(region[plane, pl.ds(start, 8), pl.ds(col_base, wide)])
                tiles = [pull_lanes(tile, col_shift) for tile in tiles]
                for i, tile in enumerate(pull_rows(tiles, row_shift)):
                    win[plane, pl.ds(base + 8 * i, 8), :] = tile

        @pl.when(slot == 0)
        def _():
            for load in late_loads:
                load.wait()

        @pl.loop(0, short // 16, unroll=2)
        def _(step):
            base = pl.multiple_of(step * 16, 16)
            for part in range(RADIX):
                cols = pl.ds(part * short, short)
                values = []
                for q in range(RADIX):
                    rows = pl.ds(base + q * short, 16)
                    wr, wi = win[0, rows, cols], win[1, rows, cols]
                    pr, pi = pupil[0, rows, cols], pupil[1, rows, cols]
                    values.append((wr * pr - wi * pi, wr * pi + wi * pr))
                for p, (re, im) in enumerate(butterfly(values, 1)):
                    for offset, value in ((0, re), (short, im)):
                        hi, lo = split(value)
                        rows = pl.ds(base + offset, 16)
                        left_hi[p, rows, cols] = hi
                        left_lo[p, rows, cols] = lo

        for p in range(RADIX):
            for half in range(2):
                cols = pl.ds(half * (side // 2), side // 2)
                rows_f32[p, :, cols] = left_dot(
                    mat_hi[p], mat_lo[p], left_hi[p, :, cols], left_lo[p, :, cols]
                )
            for base in range(0, short, 16):
                values = []
                for q in range(RADIX):
                    cols = pl.ds(q * short, short)
                    values.append(
                        (
                            rows_f32[p, pl.ds(base, 16), cols],
                            rows_f32[p, pl.ds(base + short, 16), cols],
                        )
                    )
                for t, (re, im) in enumerate(butterfly(values, 1)):
                    for offset, value in ((0, re), (short, im)):
                        hi, lo = split(value)
                        rows = pl.ds(base + p * short, 16)
                        right_hi[t, rows, pl.ds(offset, short)] = hi
                        right_lo[t, rows, pl.ds(offset, short)] = lo

        for t in range(RADIX):
            for half in range(2):
                rows = pl.ds(half * (side // 2), side // 2)
                field = right_dot(
                    right_hi[t, rows, :], right_lo[t, rows, :], mat_t_hi[t], mat_t_lo[t]
                )
                fre, fim = field[:, :short], field[:, short:]
                measured = amps[slot, rows, pl.ds(t * short, short)]
                factor = 1.0 - measured * lax.rsqrt(fre * fre + fim * fim + 1.0)
                residual = jnp.concatenate([factor * fre, factor * fim], axis=1)
                hi, lo = split(residual)
                cols_f32[t, rows, :] = right_dot(hi, lo, mat_hi[t], mat_lo[t])

        for p in range(RADIX):
            for base in range(0, short, 16):
                rows = pl.ds(base + p * short, 16)
                values = [
                    (cols_f32[t, rows, pl.ds(0, short)], cols_f32[t, rows, pl.ds(short, short)])
                    for t in range(RADIX)
                ]
                for q, (re, im) in enumerate(butterfly(values, -1)):
                    cols = pl.ds(q * short, short)
                    for offset, value in ((0, re), (short, im)):
                        hi, lo = split(value)
                        left_hi[p, pl.ds(base + offset, 16), cols] = hi
                        left_lo[p, pl.ds(base + offset, 16), cols] = lo
            for half in range(2):
                cols = pl.ds(half * (side // 2), side // 2)
                rows_f32[p, :, cols] = left_dot(
                    mat_t_hi[p], mat_t_lo[p], left_hi[p, :, cols], left_lo[p, :, cols]
                )

        @pl.loop(0, short // 8, unroll=2)
        def _(step):
            base = pl.multiple_of(step * 8, 8)
            for part in range(RADIX):
                cols = pl.ds(part * short, short)
                values = [
                    (rows_f32[p, pl.ds(base, 8), cols], rows_f32[p, pl.ds(base + short, 8), cols])
                    for p in range(RADIX)
                ]
                for q, (re, im) in enumerate(butterfly(values, -1)):
                    rows = pl.ds(base + q * short, 8)
                    pr, pi = pupil[0, rows, cols], pupil[1, rows, cols]
                    padded = pl.ds(base + q * short + 8, 8)
                    dwin[0, padded, cols] = pr * re + pi * im
                    dwin[1, padded, cols] = pr * im - pi * re
                    wr, wi = win[0, rows, cols], win[1, rows, cols]
                    dpup[0, rows, cols] += wr * re + wi * im
                    dpup[1, rows, cols] += wr * im - wi * re

        last = slot == count - 1
        pl.when(last)(dpup_store.start)

        def place(step):
            base = pl.multiple_of(step * 40, 8)
            for plane in range(2):
                tiles = [dwin[plane, pl.ds(base + 8 * i, 8), :] for i in range(6)]
                tiles = [push_lanes(tile, col_shift) for tile in tiles]
                for i, tile in enumerate(push_rows(tiles, row_shift)):
                    start = pl.multiple_of(row_base + base + 8 * i, 8)
                    target = (plane, pl.ds(start, 8), pl.ds(col_base, wide))
                    grads[target] = grads[target] + tile

        steps = (side + 8) // 40
        above = (tile_rows - row_base) // 40
        pl.loop(above, steps)(place)

        @pl.when(last)
        def _():
            for store in lower_stores:
                store.start()

        pl.loop(0, above)(place)

    pl.loop(0, count)(one_slot)

    @pl.when(count == 0)
    def _():
        for store in [dpup_store] + lower_stores:
            store.start()
        for load in late_loads:
            load.wait()

    for store in upper_stores:
        store.start()
    for store in [dpup_store] + stores:
        store.wait()


def slots_call(meta, tile, parts, amps, pupil):
    side = pupil.shape[-1]
    short = side // RADIX
    slots = amps.shape[0]
    tile_rows, tile_cols = tile.shape[1:]
    high, low = dft_blocks(side)
    tables = [jnp.asarray(x) for x in (high, low, high.transpose(0, 2, 1), low.transpose(0, 2, 1))]
    anywhere = pl.BlockSpec(memory_space=pl.ANY)
    f32, bf16 = jnp.float32, jnp.bfloat16
    region = (2, tile_rows + side, tile_cols + side)
    outs = (tile, *parts[:-1], pupil)
    table = pltpu.VMEM(high.shape, bf16)
    return pl.pallas_call(
        slots_kernel,
        out_shape=[jax.ShapeDtypeStruct(x.shape, f32) for x in outs],
        in_specs=[pl.BlockSpec(memory_space=pltpu.SMEM)] + [anywhere] * (len(parts) + 7),
        out_specs=[anywhere] * len(outs),
        scratch_shapes=[
            pltpu.VMEM(region, f32),
            pltpu.VMEM(region, f32),
            pltpu.VMEM((2, side, side), f32),
            pltpu.VMEM((RADIX, 2 * short, side), bf16),
            pltpu.VMEM((RADIX, 2 * short, side), bf16),
            pltpu.VMEM((RADIX, side, 2 * short), bf16),
            pltpu.VMEM((RADIX, side, 2 * short), bf16),
            pltpu.VMEM((RADIX, side, 2 * short), f32),
            pltpu.VMEM((RADIX, 2 * short, side), f32),
            pltpu.VMEM((2, side + 16, side), f32),
            pltpu.VMEM((2, side, side), f32),
            pltpu.VMEM(amps.shape, f32),
            pltpu.VMEM(pupil.shape, f32),
            table,
            table,
            table,
            table,
            pltpu.SemaphoreType.DMA((14,)),
            pltpu.SemaphoreType.DMA((9,)),
        ],
        compiler_params=pltpu.CompilerParams(vmem_limit_bytes=56 * 1024 * 1024),
        cost_estimate=pl.CostEstimate(
            flops=slots * 48 * 2 * 4 * short * short * side,
            bytes_accessed=40 * 1024 * 1024,
            transcendentals=slots * side * side,
        ),
        name="slots",
    )(meta, tile, *parts, amps, pupil, *tables)


def exact_parts(value):
    hi, rest = split(value)
    rest = value - hi.astype(jnp.float32)
    return (hi, *split(rest))


def order_kernel(amps, perm_rows, perm_cols, out):
    value = sum(dot(part, perm_cols[...]) for part in exact_parts(amps[0]))
    out[0] = sum(dot(perm_rows[...], part) for part in exact_parts(value))


def ordered(amps):
    slots, side, _ = amps.shape
    index = np.arange(side)
    perm = np.zeros((side, side), ml_dtypes.bfloat16)
    perm[index, (index % RADIX) * (side // RADIX) + index // RADIX] = 1
    block = pl.BlockSpec((1, side, side), lambda s: (s, 0, 0))
    table = pl.BlockSpec((side, side), lambda s: (0, 0))
    return pl.pallas_call(
        order_kernel,
        grid=(slots,),
        out_shape=jax.ShapeDtypeStruct(amps.shape, amps.dtype),
        in_specs=[block, table, table],
        out_specs=block,
        cost_estimate=pl.CostEstimate(
            flops=slots * 12 * side**3, bytes_accessed=8 * slots * side**2, transcendentals=0
        ),
        name="ordered",
    )(amps, jnp.asarray(perm.T), jnp.asarray(perm))


def along(axis_pairs, members):
    n_ty, n_tx = members
    pairs = []
    for i in range(n_ty):
        for j in range(n_tx):
            target = axis_pairs(i, j)
            if target is not None and 0 <= target[0] < n_ty and 0 <= target[1] < n_tx:
                pairs.append((i * n_tx + j, target[0] * n_tx + target[1]))
    return pairs


def send(array, rule):
    sizes = (lax.axis_size("ty"), lax.axis_size("tx"))
    return lax.ppermute(array, ("ty", "tx"), along(rule, sizes))


def halve(value, bit):
    rows = value.shape[0] // 2
    mine = lax.axis_index("ty") // bit % 2
    kept = lax.dynamic_slice_in_dim(value, mine * rows, rows, 0)
    sent = lax.dynamic_slice_in_dim(value, (1 - mine) * rows, rows, 0)
    received = lax.ppermute(sent, "ty", [(i, i ^ bit) for i in range(lax.axis_size("ty"))])
    return kept + received


def double(value, bit):
    mine = lax.axis_index("ty") // bit % 2
    other = lax.ppermute(value, "ty", [(i, i ^ bit) for i in range(lax.axis_size("ty"))])
    first = jnp.where(mine == 0, value, other)
    second = jnp.where(mine == 0, other, value)
    return jnp.concatenate([first, second], axis=0)


def ring_pairs(size, step):
    return [(i, (i + step) % size) for i in range(size)]


def scatter_tx(value):
    size, own = lax.axis_size("tx"), lax.axis_index("tx")
    rows = value.shape[0] // size
    total = lax.dynamic_slice_in_dim(value, own * rows, rows, 0)
    for step in range(1, size):
        piece = lax.dynamic_slice_in_dim(value, (own + step) % size * rows, rows, 0)
        total = total + lax.ppermute(piece, "tx", ring_pairs(size, step))
    return total


def gather_tx(value):
    size, own = lax.axis_size("tx"), lax.axis_index("tx")
    rows = value.shape[0]
    parts = [value]
    for step in range(1, size):
        parts.append(lax.ppermute(value, "tx", ring_pairs(size, step)))
    out = jnp.zeros((size * rows,) + value.shape[1:], value.dtype)
    for step, part in enumerate(parts):
        out = lax.dynamic_update_slice_in_dim(out, part, (own - step) % size * rows, 0)
    return out


def after(value, *arrivals):
    return lax.optimization_barrier((value, *arrivals))[0]


def pupil_sum(dpup, arrivals):
    n_ty, n_tx = lax.axis_size("ty"), lax.axis_size("tx")
    bits = [1]
    bit = n_ty // 2
    while bit > 1:
        bits.append(bit)
        bit //= 2
    steps = [functools.partial(halve, bit=bit) for bit in bits]
    steps.append(lambda part: scatter_tx(part) * (1.0 / math.sqrt(n_ty * n_tx)))
    steps.append(gather_tx)
    steps += [functools.partial(double, bit=bit) for bit in reversed(bits)]
    part = dpup.reshape(-1, dpup.shape[-1])
    for step, before in itertools.zip_longest(steps, arrivals, fillvalue=()):
        if before:
            part = after(part, *before)
        part = step(part)
    return part.reshape(dpup.shape)


def body(spectrum, pupil, amplitudes, offsets, live):
    side = pupil.shape[-1]
    half = side // 2
    tile_rows, tile_cols = spectrum.shape[1:]
    own_ty, own_tx = lax.axis_index("ty"), lax.axis_index("tx")
    rows_local = offsets[:, 0] - own_ty * tile_rows
    cols_local = offsets[:, 1] - own_tx * tile_cols
    meta = jnp.stack([rows_local, cols_local, live], axis=1)
    meta = jnp.concatenate([meta, jnp.full((1, 3), own_ty % 2, jnp.int32)], axis=0)

    def left(i, j):
        return (i, j - 1)

    def up(i, j):
        return (i - 1, j)

    lower_b = send(spectrum[:, :side, half:side], up)
    right_a = send(spectrum[:, :, :half], left)
    right_b = send(spectrum[:, :, half:side], left)
    lower_a = send(spectrum[:, :side, :half], up)
    lower_c = send(spectrum[:, :side, side:], up)
    amps = ordered(amplitudes)
    lower_b, amps = lax.optimization_barrier((lower_b, amps))
    corner_side = send(lower_b, lambda i, j: (i, j - 1) if i % 2 else None)
    corner_a = send(right_a[:, :side], up)
    right_b_again = after(right_b, corner_side)
    corner_up = send(right_b_again[:, :side], lambda i, j: (i - 1, j) if i % 2 else None)

    parts = (right_a, right_b, lower_a, lower_b, lower_c, corner_a, corner_up, corner_side)
    own_g, *grads, dpup = slots_call(meta, spectrum, parts, amps, pupil)
    right_a_g, right_b_g, lower_a_g, lower_b_g, lower_c_g, corner_a_g, corner_b_g = grads

    def down(i, j):
        return (i + 1, j)

    def right(i, j):
        return (i, j + 1)

    back_side = send(corner_b_g, lambda i, j: (i, j + 1) if i % 2 else None)
    back_a = send(corner_a_g, down)
    back_down = send(corner_b_g, lambda i, j: None if i % 2 else (i + 1, j))
    lower_a = send(lower_a_g, down)
    lower_c = send(lower_c_g, down)
    right_b = send(right_b_g + back_down, right)
    right_a = send(right_a_g + back_a, right)
    lower_b = send(lower_b_g + back_side, down)
    spec_grad = jnp.concatenate(
        [
            own_g[:, :, :half] + lower_a + right_a,
            own_g[:, :, half:side] + lower_b + right_b,
            own_g[:, :, side:] + lower_c,
        ],
        axis=2,
    )
    arrivals = [
        (),
        (),
        (back_a, back_side, back_down),
        (),
        (right_b,),
        (lower_c,),
        (right_a, lower_b),
        (lower_a,),
    ]
    return spec_grad, pupil_sum(dpup, arrivals)


def solution(mesh):
    return jax.shard_map(
        body,
        mesh=mesh,
        in_specs=(
            P(None, "ty", "tx"),
            P(),
            P(("ty", "tx"), None, None),
            P(("ty", "tx"), None),
            P(("ty", "tx")),
        ),
        out_specs=(P(None, "ty", "tx"), P()),
        check_vma=False,
    )
```

```python
import math

import jax
import jax.numpy as jnp
import ml_dtypes
import numpy as np
from jax import lax
from jax.experimental import pallas as pl
from jax.experimental.pallas import tpu as pltpu
from jax.sharding import PartitionSpec as P

RADIX = 4


def dft_blocks(length):
    short = length // RADIX
    out_idx = np.arange(short)[:, None]
    in_idx = np.arange(short)[None, :]
    blocks = []
    for p in range(RADIX):
        phase = (p * in_idx + RADIX * out_idx * in_idx) % length
        angle = phase * (2.0 * math.pi / length)
        cos = np.cos(angle) / math.sqrt(length)
        sin = np.sin(angle) / math.sqrt(length)
        blocks.append(np.block([[cos, -sin], [sin, cos]]))
    full = np.stack(blocks).astype(np.float32)
    high = full.astype(ml_dtypes.bfloat16)
    low = (full - high.astype(np.float32)).astype(ml_dtypes.bfloat16)
    return high, low


def split(value):
    high = value.astype(jnp.bfloat16)
    low = (value - high.astype(jnp.float32)).astype(jnp.bfloat16)
    return high, low


def dot(lhs, rhs):
    return jnp.dot(lhs, rhs, preferred_element_type=jnp.float32)


def left_dot(mat_hi, mat_lo, val_hi, val_lo):
    lhs = jnp.concatenate([mat_hi, mat_hi, mat_lo], axis=1)
    return dot(lhs, jnp.concatenate([val_hi, val_lo, val_hi], axis=0))


def right_dot(val_hi, val_lo, mat_hi, mat_lo):
    lhs = jnp.concatenate([val_hi, val_lo, val_hi], axis=1)
    return dot(lhs, jnp.concatenate([mat_hi, mat_hi, mat_lo], axis=0))


def butterfly(parts, sign):
    (r0, i0), (r1, i1), (r2, i2), (r3, i3) = parts
    sr, si, dr, di = r0 + r2, i0 + i2, r0 - r2, i0 - i2
    tr, ti, er, ei = r1 + r3, i1 + i3, r1 - r3, i1 - i3
    if sign < 0:
        er, ei = -er, -ei
    return [(sr + tr, si + ti), (dr - ei, di + er), (sr - tr, si - ti), (dr + ei, di - er)]


def row_index():
    return lax.broadcasted_iota(jnp.int32, (8, 128), 0)


def lane_index():
    return lax.broadcasted_iota(jnp.int32, (8, 128), 1)


def lane_tiles(tile):
    return [tile[:, i : i + 128] for i in range(0, tile.shape[1], 128)]


def pull_lanes(tile, shift):
    rolled = [pltpu.roll(part, (128 - shift) % 128, 1) for part in lane_tiles(tile)]
    keep = lane_index() < 128 - shift
    return [jnp.where(keep, a, b) for a, b in zip(rolled, rolled[1:])]


def pull_rows(tiles, shift):
    rolled = [[pltpu.roll(part, (8 - shift) % 8, 0) for part in tile] for tile in tiles]
    keep = row_index() < 8 - shift
    return [
        jnp.concatenate([jnp.where(keep, x, y) for x, y in zip(a, b)], axis=1)
        for a, b in zip(rolled, rolled[1:])
    ]


def push_lanes(tile, shift):
    rolled = [pltpu.roll(part, shift, 1) for part in lane_tiles(tile)]
    zero = jnp.zeros((8, 128), jnp.float32)
    keep = lane_index() >= shift
    return [jnp.where(keep, b, a) for a, b in zip([zero] + rolled, rolled + [zero])]


def push_rows(tiles, shift):
    rolled = [[pltpu.roll(part, shift, 0) for part in tile] for tile in tiles]
    keep = row_index() >= shift
    return [
        jnp.concatenate([jnp.where(keep, y, x) for x, y in zip(a, b)], axis=1)
        for a, b in zip(rolled, rolled[1:])
    ]


def slots_kernel(
    meta,
    tile_hbm,
    right_a_hbm,
    right_b_hbm,
    lower_a_hbm,
    lower_b_hbm,
    lower_c_hbm,
    corner_a_hbm,
    corner_up_hbm,
    corner_side_hbm,
    amps_hbm,
    pupil_hbm,
    mat_hi_hbm,
    mat_lo_hbm,
    mat_t_hi_hbm,
    mat_t_lo_hbm,
    own_out,
    right_out,
    lower_ab_out,
    lower_c_out,
    corner_a_out,
    corner_b_out,
    dpup_out,
    region,
    grads,
    win,
    left_hi,
    left_lo,
    right_hi,
    right_lo,
    cols_f32,
    rows_f32,
    dwin,
    dpup,
    amps,
    pupil,
    mat_hi,
    mat_lo,
    mat_t_hi,
    mat_t_lo,
    in_sems,
    out_sems,
):
    side = pupil.shape[-1]
    short = side // RADIX
    tile_rows, tile_cols = tile_hbm.shape[1:]
    slots = amps_hbm.shape[0]
    lanes = 128
    wide = side + lanes
    half = side // 2

    def pieces(buffer):
        top, bottom = pl.ds(0, tile_rows), pl.ds(tile_rows, side)
        return (
            buffer.at[:, top, pl.ds(0, tile_cols)],
            buffer.at[:, top, pl.ds(tile_cols, half)],
            buffer.at[:, top, pl.ds(tile_cols + half, half)],
            buffer.at[:, bottom, pl.ds(0, half)],
            buffer.at[:, bottom, pl.ds(half, half)],
            buffer.at[:, bottom, pl.ds(side, tile_cols - side)],
            buffer.at[:, bottom, pl.ds(tile_cols, half)],
            buffer.at[:, bottom, pl.ds(tile_cols + half, half)],
        )

    odd = meta[slots, 0]
    targets = pieces(region)
    sources = (
        tile_hbm,
        right_a_hbm,
        right_b_hbm,
        lower_a_hbm,
        lower_b_hbm,
        lower_c_hbm,
        corner_a_hbm,
    )
    loads = [
        pltpu.make_async_copy(src, dst, in_sems.at[n])
        for n, (src, dst) in enumerate(zip(sources, targets))
    ]
    for load in loads:
        load.start()
    from_side = pltpu.make_async_copy(corner_side_hbm, targets[7], in_sems.at[7])
    from_below = pltpu.make_async_copy(corner_up_hbm, targets[7], in_sems.at[7])
    pl.when(odd == 1)(from_side.start)
    pl.when(odd != 1)(from_below.start)
    loads.append(from_side)
    late = (
        (pupil_hbm, pupil),
        (mat_hi_hbm, mat_hi),
        (mat_lo_hbm, mat_lo),
        (mat_t_hi_hbm, mat_t_hi),
        (mat_t_lo_hbm, mat_t_lo),
        (amps_hbm, amps),
    )
    late_loads = [
        pltpu.make_async_copy(src, dst, in_sems.at[8 + n]) for n, (src, dst) in enumerate(late)
    ]
    for load in late_loads:
        load.start()

    top, bottom = pl.ds(0, tile_rows), pl.ds(tile_rows, side)
    outs = (
        (corner_a_out, bottom, pl.ds(tile_cols, half)),
        (corner_b_out, bottom, pl.ds(tile_cols + half, half)),
        (lower_c_out, bottom, pl.ds(side, tile_cols - side)),
        (lower_ab_out, bottom, pl.ds(0, side)),
        (right_out, top, pl.ds(tile_cols, side)),
        (own_out, top, pl.ds(0, tile_cols)),
    )
    stores = [
        pltpu.make_async_copy(grads.at[:, rows, cols], dst, out_sems.at[n])
        for n, (dst, rows, cols) in enumerate(outs)
    ]
    dpup_store = pltpu.make_async_copy(dpup, dpup_out, out_sems.at[6])
    lower_stores = stores[:4]
    upper_stores = stores[4:]

    zero_rows = 16

    @pl.loop(0, grads.shape[1] // zero_rows)
    def _(step):
        rows = pl.ds(pl.multiple_of(step * zero_rows, zero_rows), zero_rows)
        grads[:, rows, :] = jnp.zeros((2, zero_rows, grads.shape[2]), jnp.float32)

    @pl.loop(0, side // zero_rows)
    def _(step):
        rows = pl.ds(pl.multiple_of(step * zero_rows, zero_rows), zero_rows)
        dpup[:, rows, :] = jnp.zeros((2, zero_rows, side), jnp.float32)

    for start in (0, side + 8):
        dwin[:, pl.ds(start, 8), :] = jnp.zeros((2, 8, side), jnp.float32)

    for load in loads:
        load.wait()

    count = meta[0, 2]
    for slot in range(1, slots):
        count = count + meta[slot, 2]

    def one_slot(slot):
        row = meta[slot, 0]
        col = meta[slot, 1]
        col_base = pl.multiple_of((col // lanes) * lanes, lanes)
        col_shift = col - col_base
        row_base = pl.multiple_of((row // 8) * 8, 8)
        row_shift = row - row_base

        @pl.loop(0, side // 32, unroll=2)
        def _(step):
            base = pl.multiple_of(step * 32, 32)
            for plane in range(2):
                tiles = []
                for i in range(5):
                    start = pl.multiple_of(row_base + base + 8 * i, 8)
                    tiles.append(region[plane, pl.ds(start, 8), pl.ds(col_base, wide)])
                tiles = [pull_lanes(tile, col_shift) for tile in tiles]
                for i, tile in enumerate(pull_rows(tiles, row_shift)):
                    win[plane, pl.ds(base + 8 * i, 8), :] = tile

        @pl.when(slot == 0)
        def _():
            for load in late_loads:
                load.wait()

        for start in (0, half):
            for base in range(0, short, 16):
                for col0 in range(start, start + half, short):
                    cols = pl.ds(col0, short)
                    values = []
                    for q in range(RADIX):
                        rows = pl.ds(base + q * short, 16)
                        wr, wi = win[0, rows, cols], win[1, rows, cols]
                        pr, pi = pupil[0, rows, cols], pupil[1, rows, cols]
                        values.append((wr * pr - wi * pi, wr * pi + wi * pr))
                    for p, (re, im) in enumerate(butterfly(values, 1)):
                        for offset, value in ((0, re), (short, im)):
                            hi, lo = split(value)
                            rows = pl.ds(base + offset, 16)
                            left_hi[p, rows, cols] = hi
                            left_lo[p, rows, cols] = lo
            cols = pl.ds(start, half)
            for p in range(RADIX):
                rows_f32[p, :, cols] = left_dot(
                    mat_hi[p], mat_lo[p], left_hi[p, :, cols], left_lo[p, :, cols]
                )

        for p in range(RADIX):
            for base in range(0, short, 16):
                values = []
                for q in range(RADIX):
                    cols = pl.ds(q * short, short)
                    values.append(
                        (
                            rows_f32[p, pl.ds(base, 16), cols],
                            rows_f32[p, pl.ds(base + short, 16), cols],
                        )
                    )
                for t, (re, im) in enumerate(butterfly(values, 1)):
                    for offset, value in ((0, re), (short, im)):
                        hi, lo = split(value)
                        rows = pl.ds(base + p * short, 16)
                        right_hi[t, rows, pl.ds(offset, short)] = hi
                        right_lo[t, rows, pl.ds(offset, short)] = lo

        for t in range(RADIX):
            for start in (0, half):
                rows = pl.ds(start, half)
                field = right_dot(
                    right_hi[t, rows, :], right_lo[t, rows, :], mat_t_hi[t], mat_t_lo[t]
                )
                fre, fim = field[:, :short], field[:, short:]
                measured = amps[slot, rows, pl.ds(t * short, short)]
                factor = 1.0 - measured * lax.rsqrt(fre * fre + fim * fim + 1.0)
                residual = jnp.concatenate([factor * fre, factor * fim], axis=1)
                hi, lo = split(residual)
                cols_f32[t, rows, :] = right_dot(hi, lo, mat_hi[t], mat_lo[t])

        for p in range(RADIX):
            for base in range(0, short, 16):
                rows = pl.ds(base + p * short, 16)
                values = [
                    (cols_f32[t, rows, pl.ds(0, short)], cols_f32[t, rows, pl.ds(short, short)])
                    for t in range(RADIX)
                ]
                for q, (re, im) in enumerate(butterfly(values, -1)):
                    cols = pl.ds(q * short, short)
                    for offset, value in ((0, re), (short, im)):
                        hi, lo = split(value)
                        left_hi[p, pl.ds(base + offset, 16), cols] = hi
                        left_lo[p, pl.ds(base + offset, 16), cols] = lo

        for start in (0, half):
            cols = pl.ds(start, half)
            for p in range(RADIX):
                rows_f32[p, :, cols] = left_dot(
                    mat_t_hi[p], mat_t_lo[p], left_hi[p, :, cols], left_lo[p, :, cols]
                )
            for base in range(0, short, 8):
                for col0 in range(start, start + half, short):
                    cols = pl.ds(col0, short)
                    values = [
                        (
                            rows_f32[p, pl.ds(base, 8), cols],
                            rows_f32[p, pl.ds(base + short, 8), cols],
                        )
                        for p in range(RADIX)
                    ]
                    for q, (re, im) in enumerate(butterfly(values, -1)):
                        rows = pl.ds(base + q * short, 8)
                        pr, pi = pupil[0, rows, cols], pupil[1, rows, cols]
                        padded = pl.ds(base + q * short + 8, 8)
                        dwin[0, padded, cols] = pr * re + pi * im
                        dwin[1, padded, cols] = pr * im - pi * re
                        wr, wi = win[0, rows, cols], win[1, rows, cols]
                        dpup[0, rows, cols] += wr * re + wi * im
                        dpup[1, rows, cols] += wr * im - wi * re

        last = slot == count - 1
        pl.when(last)(dpup_store.start)

        def place(step):
            base = pl.multiple_of(step * 40, 8)
            for plane in range(2):
                tiles = [dwin[plane, pl.ds(base + 8 * i, 8), :] for i in range(6)]
                tiles = [push_lanes(tile, col_shift) for tile in tiles]
                for i, tile in enumerate(push_rows(tiles, row_shift)):
                    start = pl.multiple_of(row_base + base + 8 * i, 8)
                    target = (plane, pl.ds(start, 8), pl.ds(col_base, wide))
                    grads[target] = grads[target] + tile

        steps = (side + 8) // 40
        above = (tile_rows - row_base) // 40
        pl.loop(above, steps)(place)

        @pl.when(last)
        def _():
            for store in lower_stores:
                store.start()

        pl.loop(0, above)(place)

    pl.loop(0, count)(one_slot)

    @pl.when(count == 0)
    def _():
        for store in [dpup_store] + lower_stores:
            store.start()
        for load in late_loads:
            load.wait()

    for store in upper_stores:
        store.start()
    for store in [dpup_store] + stores:
        store.wait()


def slots_call(meta, tile, parts, amps, pupil):
    side = pupil.shape[-1]
    short = side // RADIX
    slots = amps.shape[0]
    tile_rows, tile_cols = tile.shape[1:]
    high, low = dft_blocks(side)
    tables = [jnp.asarray(x) for x in (high, low, high.transpose(0, 2, 1), low.transpose(0, 2, 1))]
    anywhere = pl.BlockSpec(memory_space=pl.ANY)
    f32, bf16 = jnp.float32, jnp.bfloat16
    region = (2, tile_rows + side, tile_cols + side)
    _, _, _, _, lower_c, corner_a, corner_b, _ = parts
    right = jax.ShapeDtypeStruct((2, tile_rows, side), f32)
    lower_ab = jax.ShapeDtypeStruct((2, side, side), f32)
    outs = (tile, right, lower_ab, lower_c, corner_a, corner_b, pupil)
    table = pltpu.VMEM(high.shape, bf16)
    return pl.pallas_call(
        slots_kernel,
        out_shape=[jax.ShapeDtypeStruct(x.shape, f32) for x in outs],
        in_specs=[pl.BlockSpec(memory_space=pltpu.SMEM)] + [anywhere] * (len(parts) + 7),
        out_specs=[anywhere] * len(outs),
        scratch_shapes=[
            pltpu.VMEM(region, f32),
            pltpu.VMEM(region, f32),
            pltpu.VMEM((2, side, side), f32),
            pltpu.VMEM((RADIX, 2 * short, side), bf16),
            pltpu.VMEM((RADIX, 2 * short, side), bf16),
            pltpu.VMEM((RADIX, side, 2 * short), bf16),
            pltpu.VMEM((RADIX, side, 2 * short), bf16),
            pltpu.VMEM((RADIX, side, 2 * short), f32),
            pltpu.VMEM((RADIX, 2 * short, side), f32),
            pltpu.VMEM((2, side + 16, side), f32),
            pltpu.VMEM((2, side, side), f32),
            pltpu.VMEM(amps.shape, f32),
            pltpu.VMEM(pupil.shape, f32),
            table,
            table,
            table,
            table,
            pltpu.SemaphoreType.DMA((14,)),
            pltpu.SemaphoreType.DMA((7,)),
        ],
        compiler_params=pltpu.CompilerParams(vmem_limit_bytes=56 * 1024 * 1024),
        cost_estimate=pl.CostEstimate(
            flops=slots * 48 * 2 * 4 * short * short * side,
            bytes_accessed=40 * 1024 * 1024,
            transcendentals=slots * side * side,
        ),
        name="slots",
    )(meta, tile, *parts, amps, pupil, *tables)


def exact_parts(value):
    hi, rest = split(value)
    rest = value - hi.astype(jnp.float32)
    return (hi, *split(rest))


def order_kernel(amps, perm_rows, perm_cols, out):
    value = sum(dot(part, perm_cols[...]) for part in exact_parts(amps[0]))
    out[0] = sum(dot(perm_rows[...], part) for part in exact_parts(value))


def ordered(amps):
    slots, side, _ = amps.shape
    index = np.arange(side)
    perm = np.zeros((side, side), ml_dtypes.bfloat16)
    perm[index, (index % RADIX) * (side // RADIX) + index // RADIX] = 1
    block = pl.BlockSpec((1, side, side), lambda s: (s, 0, 0))
    table = pl.BlockSpec((side, side), lambda s: (0, 0))
    return pl.pallas_call(
        order_kernel,
        grid=(slots,),
        out_shape=jax.ShapeDtypeStruct(amps.shape, amps.dtype),
        in_specs=[block, table, table],
        out_specs=block,
        cost_estimate=pl.CostEstimate(
            flops=slots * 12 * side**3, bytes_accessed=8 * slots * side**2, transcendentals=0
        ),
        name="ordered",
    )(amps, jnp.asarray(perm.T), jnp.asarray(perm))


def along(axis_pairs, members):
    n_ty, n_tx = members
    pairs = []
    for i in range(n_ty):
        for j in range(n_tx):
            target = axis_pairs(i, j)
            if target is not None and 0 <= target[0] < n_ty and 0 <= target[1] < n_tx:
                pairs.append((i * n_tx + j, target[0] * n_tx + target[1]))
    return pairs


def send(array, rule):
    sizes = (lax.axis_size("ty"), lax.axis_size("tx"))
    return lax.ppermute(array, ("ty", "tx"), along(rule, sizes))


def halve(value, bit):
    rows = value.shape[0] // 2
    mine = lax.axis_index("ty") // bit % 2
    kept = lax.dynamic_slice_in_dim(value, mine * rows, rows, 0)
    sent = lax.dynamic_slice_in_dim(value, (1 - mine) * rows, rows, 0)
    received = lax.ppermute(sent, "ty", [(i, i ^ bit) for i in range(lax.axis_size("ty"))])
    return kept + received


def double(value, bit):
    mine = lax.axis_index("ty") // bit % 2
    other = lax.ppermute(value, "ty", [(i, i ^ bit) for i in range(lax.axis_size("ty"))])
    first = jnp.where(mine == 0, value, other)
    second = jnp.where(mine == 0, other, value)
    return jnp.concatenate([first, second], axis=0)


def ring_pairs(size, step):
    return [(i, (i + step) % size) for i in range(size)]


def scatter_tx(value):
    size, own = lax.axis_size("tx"), lax.axis_index("tx")
    rows = value.shape[0] // size
    total = lax.dynamic_slice_in_dim(value, own * rows, rows, 0)
    for step in range(1, size):
        piece = lax.dynamic_slice_in_dim(value, (own + step) % size * rows, rows, 0)
        total = total + lax.ppermute(piece, "tx", ring_pairs(size, step))
    return total


def gather_tx(value):
    size, own = lax.axis_size("tx"), lax.axis_index("tx")
    rows = value.shape[0]
    parts = [value]
    for step in range(1, size):
        parts.append(lax.ppermute(value, "tx", ring_pairs(size, step)))
    out = jnp.zeros((size * rows,) + value.shape[1:], value.dtype)
    for step, part in enumerate(parts):
        out = lax.dynamic_update_slice_in_dim(out, part, (own - step) % size * rows, 0)
    return out


def after(value, *arrivals):
    return lax.optimization_barrier((value, *arrivals))[0]


def pupil_sum(part, first, middle, last):
    n_ty, n_tx = lax.axis_size("ty"), lax.axis_size("tx")
    bits = []
    bit = n_ty // 2
    while bit > 1:
        bits.append(bit)
        bit //= 2
    part = after(part, *first)
    for bit in bits[1:]:
        part = halve(part, bit)
    part = scatter_tx(part) * (1.0 / math.sqrt(n_ty * n_tx))
    part = gather_tx(part)
    for bit in reversed(bits[1:]):
        part = double(part, bit)
    part = double(after(part, *middle), bits[0])
    return double(after(part, *last), 1)


def body(spectrum, pupil, amplitudes, offsets, live):
    side = pupil.shape[-1]
    half = side // 2
    tile_rows, tile_cols = spectrum.shape[1:]
    own_ty, own_tx = lax.axis_index("ty"), lax.axis_index("tx")
    rows_local = offsets[:, 0] - own_ty * tile_rows
    cols_local = offsets[:, 1] - own_tx * tile_cols
    meta = jnp.stack([rows_local, cols_local, live], axis=1)
    meta = jnp.concatenate([meta, jnp.full((1, 3), own_ty % 2, jnp.int32)], axis=0)

    def left(i, j):
        return (i, j - 1)

    def up(i, j):
        return (i - 1, j)

    lower_b = send(spectrum[:, :side, half:side], up)
    right_a = send(spectrum[:, :, :half], left)
    right_b = send(after(spectrum[:, :, half:side], lower_b), left)
    lower_a = send(spectrum[:, :side, :half], up)
    lower_c = send(spectrum[:, :side, side:], up)
    amps = ordered(amplitudes)
    lower_b, amps = lax.optimization_barrier((lower_b, amps))
    corner_side = send(lower_b, lambda i, j: (i, j - 1) if i % 2 else None)
    corner_a = send(right_a[:, :side], up)
    right_b_again = after(right_b, corner_side)
    corner_up = send(right_b_again[:, :side], lambda i, j: (i - 1, j) if i % 2 else None)

    parts = (right_a, right_b, lower_a, lower_b, lower_c, corner_a, corner_up, corner_side)
    own_g, right_g, lower_ab_g, lower_c_g, corner_a_g, corner_b_g, dpup = slots_call(
        meta, spectrum, parts, amps, pupil
    )

    def down(i, j):
        return (i + 1, j)

    def right(i, j):
        return (i, j + 1)

    back_side = send(corner_b_g, lambda i, j: (i, j + 1) if i % 2 else None)
    back_a = send(corner_a_g, down)
    back_down = send(corner_b_g, lambda i, j: None if i % 2 else (i + 1, j))
    halved = halve(halve(dpup.reshape(-1, side), 1), lax.axis_size("ty") // 2)
    lower_c = send(after(lower_c_g, halved), down)
    right_back = send(right_g + jnp.concatenate([back_a, back_down], axis=2), right)
    lower_ab = send(lower_ab_g.at[:, :, half:].add(back_side), down)
    spec_grad = jnp.concatenate(
        [
            own_g[:, :, :side] + lower_ab + right_back,
            own_g[:, :, side:] + lower_c,
        ],
        axis=2,
    )
    pupil_grad = pupil_sum(
        halved, (back_a, back_down, back_side), (lower_c,), (right_back, lower_ab)
    )
    return spec_grad, pupil_grad.reshape(pupil.shape)


def solution(mesh):
    return jax.shard_map(
        body,
        mesh=mesh,
        in_specs=(
            P(None, "ty", "tx"),
            P(),
            P(("ty", "tx"), None, None),
            P(("ty", "tx"), None),
            P(("ty", "tx")),
        ),
        out_specs=(P(None, "ty", "tx"), P()),
        check_vma=False,
    )
```

```python
import math

import jax
import jax.numpy as jnp
import ml_dtypes
import numpy as np
from jax import lax
from jax.experimental import pallas as pl
from jax.experimental.pallas import tpu as pltpu
from jax.sharding import PartitionSpec as P

RADIX = 4


def dft_blocks(length):
    short = length // RADIX
    out_idx = np.arange(short)[:, None]
    in_idx = np.arange(short)[None, :]
    blocks = []
    for p in range(RADIX):
        phase = (p * in_idx + RADIX * out_idx * in_idx) % length
        angle = phase * (2.0 * math.pi / length)
        cos = np.cos(angle) / math.sqrt(length)
        sin = np.sin(angle) / math.sqrt(length)
        blocks.append(np.block([[cos, -sin], [sin, cos]]))
    full = np.stack(blocks).astype(np.float32)
    high = full.astype(ml_dtypes.bfloat16)
    low = (full - high.astype(np.float32)).astype(ml_dtypes.bfloat16)
    return high, low


def split(value):
    high = value.astype(jnp.bfloat16)
    low = (value - high.astype(jnp.float32)).astype(jnp.bfloat16)
    return high, low


def dot(lhs, rhs):
    return jnp.dot(lhs, rhs, preferred_element_type=jnp.float32)


def left_dot(mats, val_hi, val_lo):
    rows = mats.shape[0] // 2
    both = dot(mats, val_hi)
    return both[:rows] + (both[rows:] + dot(mats[:rows], val_lo))


def right_dot(val_hi, val_lo, mat_hi, mat_lo):
    rows = val_hi.shape[0]
    both = dot(jnp.concatenate([val_hi, val_lo], axis=0), mat_hi)
    return both[:rows] + (both[rows:] + dot(val_hi, mat_lo))


def butterfly(parts, sign):
    (r0, i0), (r1, i1), (r2, i2), (r3, i3) = parts
    sr, si, dr, di = r0 + r2, i0 + i2, r0 - r2, i0 - i2
    tr, ti, er, ei = r1 + r3, i1 + i3, r1 - r3, i1 - i3
    if sign < 0:
        er, ei = -er, -ei
    return [(sr + tr, si + ti), (dr - ei, di + er), (sr - tr, si - ti), (dr + ei, di - er)]


def row_index():
    return lax.broadcasted_iota(jnp.int32, (8, 128), 0)


def lane_index():
    return lax.broadcasted_iota(jnp.int32, (8, 128), 1)


def lane_tiles(tile):
    return [tile[:, i : i + 128] for i in range(0, tile.shape[1], 128)]


def pull_lanes(tile, shift):
    rolled = [pltpu.roll(part, (128 - shift) % 128, 1) for part in lane_tiles(tile)]
    keep = lane_index() < 128 - shift
    return [jnp.where(keep, a, b) for a, b in zip(rolled, rolled[1:])]


def pull_rows(tiles, shift):
    rolled = [[pltpu.roll(part, (8 - shift) % 8, 0) for part in tile] for tile in tiles]
    keep = row_index() < 8 - shift
    return [
        jnp.concatenate([jnp.where(keep, x, y) for x, y in zip(a, b)], axis=1)
        for a, b in zip(rolled, rolled[1:])
    ]


def push_lanes(tile, shift):
    rolled = [pltpu.roll(part, shift, 1) for part in lane_tiles(tile)]
    zero = jnp.zeros((8, 128), jnp.float32)
    keep = lane_index() >= shift
    return [jnp.where(keep, b, a) for a, b in zip([zero] + rolled, rolled + [zero])]


def push_rows(tiles, shift):
    rolled = [[pltpu.roll(part, shift, 0) for part in tile] for tile in tiles]
    keep = row_index() >= shift
    return [
        jnp.concatenate([jnp.where(keep, y, x) for x, y in zip(a, b)], axis=1)
        for a, b in zip(rolled, rolled[1:])
    ]


def slots_kernel(
    meta,
    tile_hbm,
    right_a_hbm,
    right_b_hbm,
    lower_a_hbm,
    lower_b_hbm,
    lower_c_hbm,
    corner_a_hbm,
    corner_up_hbm,
    corner_side_hbm,
    amps_hbm,
    pupil_hbm,
    mat_hi_hbm,
    mat_lo_hbm,
    mat_t_hi_hbm,
    mat_t_lo_hbm,
    own_out,
    right_out,
    lower_ab_out,
    lower_c_out,
    corner_a_out,
    corner_b_out,
    dpup_out,
    region,
    grads,
    win,
    left_hi,
    left_lo,
    right_hi,
    right_lo,
    cols_f32,
    rows_f32,
    dwin,
    dpup,
    amps,
    pupil,
    mat_hi,
    mat_lo,
    mat_t_hi,
    mat_t_lo,
    in_sems,
    out_sems,
):
    side = pupil.shape[-1]
    short = side // RADIX
    tile_rows, tile_cols = tile_hbm.shape[1:]
    slots = amps_hbm.shape[0]
    lanes = 128
    wide = side + lanes
    half = side // 2

    def pieces(buffer):
        top, bottom = pl.ds(0, tile_rows), pl.ds(tile_rows, side)
        return (
            buffer.at[:, top, pl.ds(0, tile_cols)],
            buffer.at[:, top, pl.ds(tile_cols, half)],
            buffer.at[:, top, pl.ds(tile_cols + half, half)],
            buffer.at[:, bottom, pl.ds(0, half)],
            buffer.at[:, bottom, pl.ds(half, half)],
            buffer.at[:, bottom, pl.ds(side, tile_cols - side)],
            buffer.at[:, bottom, pl.ds(tile_cols, half)],
            buffer.at[:, bottom, pl.ds(tile_cols + half, half)],
        )

    odd = meta[slots, 0]
    targets = pieces(region)
    sources = (
        tile_hbm,
        right_a_hbm,
        right_b_hbm,
        lower_a_hbm,
        lower_b_hbm,
        lower_c_hbm,
        corner_a_hbm,
    )
    loads = [
        pltpu.make_async_copy(src, dst, in_sems.at[n])
        for n, (src, dst) in enumerate(zip(sources, targets))
    ]
    for load in loads:
        load.start()
    from_side = pltpu.make_async_copy(corner_side_hbm, targets[7], in_sems.at[7])
    from_below = pltpu.make_async_copy(corner_up_hbm, targets[7], in_sems.at[7])
    pl.when(odd == 1)(from_side.start)
    pl.when(odd != 1)(from_below.start)
    loads.append(from_side)
    late = (
        (pupil_hbm, pupil),
        (mat_hi_hbm, mat_hi),
        (mat_lo_hbm, mat_lo),
        (mat_t_hi_hbm, mat_t_hi),
        (mat_t_lo_hbm, mat_t_lo),
        (amps_hbm, amps),
    )
    late_loads = [
        pltpu.make_async_copy(src, dst, in_sems.at[8 + n]) for n, (src, dst) in enumerate(late)
    ]
    for load in late_loads:
        load.start()

    top, bottom = pl.ds(0, tile_rows), pl.ds(tile_rows, side)
    outs = (
        (corner_a_out, bottom, pl.ds(tile_cols, half)),
        (corner_b_out, bottom, pl.ds(tile_cols + half, half)),
        (lower_c_out, bottom, pl.ds(side, tile_cols - side)),
        (lower_ab_out, bottom, pl.ds(0, side)),
        (right_out, top, pl.ds(tile_cols, side)),
        (own_out, top, pl.ds(0, tile_cols)),
    )
    stores = [
        pltpu.make_async_copy(grads.at[:, rows, cols], dst, out_sems.at[n])
        for n, (dst, rows, cols) in enumerate(outs)
    ]
    dpup_store = pltpu.make_async_copy(dpup, dpup_out, out_sems.at[6])
    lower_stores = stores[:4]
    upper_stores = stores[4:]

    zero_rows = 16

    @pl.loop(0, grads.shape[1] // zero_rows)
    def _(step):
        rows = pl.ds(pl.multiple_of(step * zero_rows, zero_rows), zero_rows)
        grads[:, rows, :] = jnp.zeros((2, zero_rows, grads.shape[2]), jnp.float32)

    @pl.loop(0, side // zero_rows)
    def _(step):
        rows = pl.ds(pl.multiple_of(step * zero_rows, zero_rows), zero_rows)
        dpup[:, rows, :] = jnp.zeros((2, zero_rows, side), jnp.float32)

    for start in (0, side + 8):
        dwin[:, pl.ds(start, 8), :] = jnp.zeros((2, 8, side), jnp.float32)

    for load in loads:
        load.wait()

    count = meta[0, 2]
    for slot in range(1, slots):
        count = count + meta[slot, 2]

    def one_slot(slot):
        row = meta[slot, 0]
        col = meta[slot, 1]
        col_base = pl.multiple_of((col // lanes) * lanes, lanes)
        col_shift = col - col_base
        row_base = pl.multiple_of((row // 8) * 8, 8)
        row_shift = row - row_base

        @pl.loop(0, side // 32, unroll=2)
        def _(step):
            base = pl.multiple_of(step * 32, 32)
            for plane in range(2):
                tiles = []
                for i in range(5):
                    start = pl.multiple_of(row_base + base + 8 * i, 8)
                    tiles.append(region[plane, pl.ds(start, 8), pl.ds(col_base, wide)])
                tiles = [pull_lanes(tile, col_shift) for tile in tiles]
                for i, tile in enumerate(pull_rows(tiles, row_shift)):
                    win[plane, pl.ds(base + 8 * i, 8), :] = tile

        @pl.when(slot == 0)
        def _():
            for load in late_loads:
                load.wait()

        for start in (0, half):
            for base in range(0, short, 16):
                for col0 in range(start, start + half, short):
                    cols = pl.ds(col0, short)
                    values = []
                    for q in range(RADIX):
                        rows = pl.ds(base + q * short, 16)
                        wr, wi = win[0, rows, cols], win[1, rows, cols]
                        pr, pi = pupil[0, rows, cols], pupil[1, rows, cols]
                        values.append((wr * pr - wi * pi, wr * pi + wi * pr))
                    for p, (re, im) in enumerate(butterfly(values, 1)):
                        for offset, value in ((0, re), (short, im)):
                            hi, lo = split(value)
                            rows = pl.ds(base + offset, 16)
                            left_hi[p, rows, cols] = hi
                            left_lo[p, rows, cols] = lo
            cols = pl.ds(start, half)
            for p in range(RADIX):
                rows_f32[p, :, cols] = left_dot(
                    jnp.concatenate([mat_hi[p], mat_lo[p]], axis=0),
                    left_hi[p, :, cols],
                    left_lo[p, :, cols],
                )

        for p in range(RADIX):
            for base in range(0, short, 16):
                values = []
                for q in range(RADIX):
                    cols = pl.ds(q * short, short)
                    values.append(
                        (
                            rows_f32[p, pl.ds(base, 16), cols],
                            rows_f32[p, pl.ds(base + short, 16), cols],
                        )
                    )
                for t, (re, im) in enumerate(butterfly(values, 1)):
                    for offset, value in ((0, re), (short, im)):
                        hi, lo = split(value)
                        rows = pl.ds(base + p * short, 16)
                        right_hi[t, rows, pl.ds(offset, short)] = hi
                        right_lo[t, rows, pl.ds(offset, short)] = lo

        for t in range(RADIX):
            field = right_dot(right_hi[t], right_lo[t], mat_t_hi[t], mat_t_lo[t])
            fre, fim = field[:, :short], field[:, short:]
            measured = amps[slot, :, pl.ds(t * short, short)]
            factor = 1.0 - measured * lax.rsqrt(fre * fre + fim * fim + 1.0)
            residual = jnp.concatenate([factor * fre, factor * fim], axis=1)
            hi, lo = split(residual)
            cols_f32[t] = right_dot(hi, lo, mat_hi[t], mat_lo[t])

        for p in range(RADIX):
            for base in range(0, short, 16):
                rows = pl.ds(base + p * short, 16)
                values = [
                    (cols_f32[t, rows, pl.ds(0, short)], cols_f32[t, rows, pl.ds(short, short)])
                    for t in range(RADIX)
                ]
                for q, (re, im) in enumerate(butterfly(values, -1)):
                    cols = pl.ds(q * short, short)
                    for offset, value in ((0, re), (short, im)):
                        hi, lo = split(value)
                        left_hi[p, pl.ds(base + offset, 16), cols] = hi
                        left_lo[p, pl.ds(base + offset, 16), cols] = lo

        for start in (0, half):
            cols = pl.ds(start, half)
            for p in range(RADIX):
                rows_f32[p, :, cols] = left_dot(
                    jnp.concatenate([mat_t_hi[p], mat_t_lo[p]], axis=0),
                    left_hi[p, :, cols],
                    left_lo[p, :, cols],
                )
            for base in range(0, short, 8):
                for col0 in range(start, start + half, short):
                    cols = pl.ds(col0, short)
                    values = [
                        (
                            rows_f32[p, pl.ds(base, 8), cols],
                            rows_f32[p, pl.ds(base + short, 8), cols],
                        )
                        for p in range(RADIX)
                    ]
                    for q, (re, im) in enumerate(butterfly(values, -1)):
                        rows = pl.ds(base + q * short, 8)
                        pr, pi = pupil[0, rows, cols], pupil[1, rows, cols]
                        padded = pl.ds(base + q * short + 8, 8)
                        dwin[0, padded, cols] = pr * re + pi * im
                        dwin[1, padded, cols] = pr * im - pi * re
                        wr, wi = win[0, rows, cols], win[1, rows, cols]
                        dpup[0, rows, cols] += wr * re + wi * im
                        dpup[1, rows, cols] += wr * im - wi * re

        last = slot == count - 1
        pl.when(last)(dpup_store.start)

        def place(step):
            base = pl.multiple_of(step * 40, 8)
            for plane in range(2):
                tiles = [dwin[plane, pl.ds(base + 8 * i, 8), :] for i in range(6)]
                tiles = [push_lanes(tile, col_shift) for tile in tiles]
                for i, tile in enumerate(push_rows(tiles, row_shift)):
                    start = pl.multiple_of(row_base + base + 8 * i, 8)
                    target = (plane, pl.ds(start, 8), pl.ds(col_base, wide))
                    grads[target] = grads[target] + tile

        steps = (side + 8) // 40
        above = (tile_rows - row_base) // 40
        pl.loop(above, steps)(place)

        @pl.when(last)
        def _():
            for store in lower_stores:
                store.start()

        pl.loop(0, above)(place)

    pl.loop(0, count)(one_slot)

    @pl.when(count == 0)
    def _():
        for store in [dpup_store] + lower_stores:
            store.start()
        for load in late_loads:
            load.wait()

    for store in upper_stores:
        store.start()
    for store in [dpup_store] + stores:
        store.wait()


def slots_call(meta, tile, parts, amps, pupil):
    side = pupil.shape[-1]
    short = side // RADIX
    slots = amps.shape[0]
    tile_rows, tile_cols = tile.shape[1:]
    high, low = dft_blocks(side)
    tables = [jnp.asarray(x) for x in (high, low, high.transpose(0, 2, 1), low.transpose(0, 2, 1))]
    anywhere = pl.BlockSpec(memory_space=pl.ANY)
    f32, bf16 = jnp.float32, jnp.bfloat16
    region = (2, tile_rows + side, tile_cols + side)
    _, _, _, _, lower_c, corner_a, corner_b, _ = parts
    right = jax.ShapeDtypeStruct((2, tile_rows, side), f32)
    lower_ab = jax.ShapeDtypeStruct((2, side, side), f32)
    outs = (tile, right, lower_ab, lower_c, corner_a, corner_b, pupil)
    table = pltpu.VMEM(high.shape, bf16)
    return pl.pallas_call(
        slots_kernel,
        out_shape=[jax.ShapeDtypeStruct(x.shape, f32) for x in outs],
        in_specs=[pl.BlockSpec(memory_space=pltpu.SMEM)] + [anywhere] * (len(parts) + 7),
        out_specs=[anywhere] * len(outs),
        scratch_shapes=[
            pltpu.VMEM(region, f32),
            pltpu.VMEM(region, f32),
            pltpu.VMEM((2, side, side), f32),
            pltpu.VMEM((RADIX, 2 * short, side), bf16),
            pltpu.VMEM((RADIX, 2 * short, side), bf16),
            pltpu.VMEM((RADIX, side, 2 * short), bf16),
            pltpu.VMEM((RADIX, side, 2 * short), bf16),
            pltpu.VMEM((RADIX, side, 2 * short), f32),
            pltpu.VMEM((RADIX, 2 * short, side), f32),
            pltpu.VMEM((2, side + 16, side), f32),
            pltpu.VMEM((2, side, side), f32),
            pltpu.VMEM(amps.shape, f32),
            pltpu.VMEM(pupil.shape, f32),
            table,
            table,
            table,
            table,
            pltpu.SemaphoreType.DMA((14,)),
            pltpu.SemaphoreType.DMA((7,)),
        ],
        compiler_params=pltpu.CompilerParams(vmem_limit_bytes=56 * 1024 * 1024),
        cost_estimate=pl.CostEstimate(
            flops=slots * 48 * 2 * 4 * short * short * side,
            bytes_accessed=40 * 1024 * 1024,
            transcendentals=slots * side * side,
        ),
        name="slots",
    )(meta, tile, *parts, amps, pupil, *tables)


def exact_parts(value):
    hi, rest = split(value)
    rest = value - hi.astype(jnp.float32)
    return (hi, *split(rest))


def order_kernel(amps, perm_rows, perm_cols, out):
    value = sum(dot(part, perm_cols[...]) for part in exact_parts(amps[0]))
    out[0] = sum(dot(perm_rows[...], part) for part in exact_parts(value))


def ordered(amps):
    slots, side, _ = amps.shape
    index = np.arange(side)
    perm = np.zeros((side, side), ml_dtypes.bfloat16)
    perm[index, (index % RADIX) * (side // RADIX) + index // RADIX] = 1
    block = pl.BlockSpec((1, side, side), lambda s: (s, 0, 0))
    table = pl.BlockSpec((side, side), lambda s: (0, 0))
    return pl.pallas_call(
        order_kernel,
        grid=(slots,),
        out_shape=jax.ShapeDtypeStruct(amps.shape, amps.dtype),
        in_specs=[block, table, table],
        out_specs=block,
        cost_estimate=pl.CostEstimate(
            flops=slots * 12 * side**3, bytes_accessed=8 * slots * side**2, transcendentals=0
        ),
        name="ordered",
    )(amps, jnp.asarray(perm.T), jnp.asarray(perm))


def along(axis_pairs, members):
    n_ty, n_tx = members
    pairs = []
    for i in range(n_ty):
        for j in range(n_tx):
            target = axis_pairs(i, j)
            if target is not None and 0 <= target[0] < n_ty and 0 <= target[1] < n_tx:
                pairs.append((i * n_tx + j, target[0] * n_tx + target[1]))
    return pairs


def send(array, rule):
    sizes = (lax.axis_size("ty"), lax.axis_size("tx"))
    return lax.ppermute(array, ("ty", "tx"), along(rule, sizes))


def after(value, *arrivals):
    return lax.optimization_barrier((value, *arrivals))[0]


def pupil_sum(dpup):
    axes = ("ty", "tx")
    flat = dpup.reshape(-1, dpup.shape[-1])
    part = lax.psum_scatter(flat, axes, scatter_dimension=0, tiled=True)
    part = part * (1.0 / math.sqrt(lax.axis_size("ty") * lax.axis_size("tx")))
    return lax.all_gather(part, axes, axis=0, tiled=True).reshape(dpup.shape)


def body(spectrum, pupil, amplitudes, offsets, live):
    side = pupil.shape[-1]
    half = side // 2
    tile_rows, tile_cols = spectrum.shape[1:]
    own_ty, own_tx = lax.axis_index("ty"), lax.axis_index("tx")
    rows_local = offsets[:, 0] - own_ty * tile_rows
    cols_local = offsets[:, 1] - own_tx * tile_cols
    meta = jnp.stack([rows_local, cols_local, live], axis=1)
    meta = jnp.concatenate([meta, jnp.full((1, 3), own_ty % 2, jnp.int32)], axis=0)

    def left(i, j):
        return (i, j - 1)

    def up(i, j):
        return (i - 1, j)

    lower_b = send(spectrum[:, :side, half:side], up)
    right_a = send(spectrum[:, :, :half], left)
    right_b = send(after(spectrum[:, :, half:side], lower_b), left)
    lower_a = send(spectrum[:, :side, :half], up)
    lower_c = send(spectrum[:, :side, side:], up)
    amps = ordered(amplitudes)
    lower_b, amps = lax.optimization_barrier((lower_b, amps))
    corner_side = send(lower_b, lambda i, j: (i, j - 1) if i % 2 else None)
    corner_a = send(right_a[:, :side], up)
    right_b_again = after(right_b, corner_side)
    corner_up = send(right_b_again[:, :side], lambda i, j: (i - 1, j) if i % 2 else None)

    parts = (right_a, right_b, lower_a, lower_b, lower_c, corner_a, corner_up, corner_side)
    own_g, right_g, lower_ab_g, lower_c_g, corner_a_g, corner_b_g, dpup = slots_call(
        meta, spectrum, parts, amps, pupil
    )

    def down(i, j):
        return (i + 1, j)

    def right(i, j):
        return (i, j + 1)

    back_side = send(corner_b_g, lambda i, j: (i, j + 1) if i % 2 else None)
    back_a = send(corner_a_g, down)
    back_down = send(corner_b_g, lambda i, j: None if i % 2 else (i + 1, j))
    lower_c = send(lower_c_g, down)
    right_back = send(right_g + jnp.concatenate([back_a, back_down], axis=2), right)
    lower_ab = send(lower_ab_g.at[:, :, half:].add(back_side), down)
    spec_grad = jnp.concatenate(
        [
            own_g[:, :, :side] + lower_ab + right_back,
            own_g[:, :, side:] + lower_c,
        ],
        axis=2,
    )
    return spec_grad, pupil_sum(dpup)


def solution(mesh):
    return jax.shard_map(
        body,
        mesh=mesh,
        in_specs=(
            P(None, "ty", "tx"),
            P(),
            P(("ty", "tx"), None, None),
            P(("ty", "tx"), None),
            P(("ty", "tx")),
        ),
        out_specs=(P(None, "ty", "tx"), P()),
        check_vma=False,
    )
```

```python
import math

import jax
import jax.numpy as jnp
import ml_dtypes
import numpy as np
from jax import lax
from jax.experimental import pallas as pl
from jax.experimental.pallas import tpu as pltpu
from jax.sharding import PartitionSpec as P

RADIX = 4


def dft_blocks(length):
    short = length // RADIX
    out_idx = np.arange(short)[:, None]
    in_idx = np.arange(short)[None, :]
    blocks = []
    for p in range(RADIX):
        phase = (p * in_idx + RADIX * out_idx * in_idx) % length
        angle = phase * (2.0 * math.pi / length)
        cos = np.cos(angle) / math.sqrt(length)
        sin = np.sin(angle) / math.sqrt(length)
        blocks.append(np.block([[cos, -sin], [sin, cos]]))
    full = np.stack(blocks).astype(np.float32)
    high = full.astype(ml_dtypes.bfloat16)
    low = (full - high.astype(np.float32)).astype(ml_dtypes.bfloat16)
    return high, low


def split(value):
    high = value.astype(jnp.bfloat16)
    low = (value - high.astype(jnp.float32)).astype(jnp.bfloat16)
    return high, low


def dot(lhs, rhs):
    return jnp.dot(lhs, rhs, preferred_element_type=jnp.float32)


def left_dot(mat_hi, mat_lo, val_hi, val_lo):
    lhs = jnp.concatenate([mat_hi, mat_hi, mat_lo], axis=1)
    return dot(lhs, jnp.concatenate([val_hi, val_lo, val_hi], axis=0))


def right_dot(val_hi, val_lo, mat_hi, mat_lo):
    lhs = jnp.concatenate([val_hi, val_lo, val_hi], axis=1)
    return dot(lhs, jnp.concatenate([mat_hi, mat_hi, mat_lo], axis=0))


def butterfly(parts, sign):
    (r0, i0), (r1, i1), (r2, i2), (r3, i3) = parts
    sr, si, dr, di = r0 + r2, i0 + i2, r0 - r2, i0 - i2
    tr, ti, er, ei = r1 + r3, i1 + i3, r1 - r3, i1 - i3
    if sign < 0:
        er, ei = -er, -ei
    return [(sr + tr, si + ti), (dr - ei, di + er), (sr - tr, si - ti), (dr + ei, di - er)]


def row_index():
    return lax.broadcasted_iota(jnp.int32, (8, 128), 0)


def lane_index():
    return lax.broadcasted_iota(jnp.int32, (8, 128), 1)


def lane_tiles(tile):
    return [tile[:, i : i + 128] for i in range(0, tile.shape[1], 128)]


def rolled(tiles, amount, axis):
    return [[pltpu.roll(part, amount, axis) for part in tile] for tile in tiles]


def shift_on(tiles, row_shift, col_shift):
    keep = lane_index() >= col_shift
    tiles = rolled([lane_tiles(tile) for tile in tiles], col_shift, 1)
    tiles = [[jnp.where(keep, x, y) for x, y in zip(t, t[-1:] + t[:-1])] for t in tiles]
    keep = row_index() >= row_shift
    tiles = rolled(tiles, row_shift, 0)
    return [
        jnp.concatenate([jnp.where(keep, y, x) for x, y in zip(a, b)], axis=1)
        for a, b in zip(tiles, tiles[1:])
    ]


def shift_back(tiles, row_shift, col_shift):
    keep = lane_index() < 128 - col_shift
    tiles = rolled([lane_tiles(tile) for tile in tiles], (128 - col_shift) % 128, 1)
    tiles = [[jnp.where(keep, x, y) for x, y in zip(t, t[1:] + t[:1])] for t in tiles]
    keep = row_index() < 8 - row_shift
    tiles = rolled(tiles, (8 - row_shift) % 8, 0)
    return [
        jnp.concatenate([jnp.where(keep, x, y) for x, y in zip(a, b)], axis=1)
        for a, b in zip(tiles, tiles[1:])
    ]


def wrap_lanes(block, col_shift):
    rows = block.shape[0]
    keep = lax.broadcasted_iota(jnp.int32, (rows, 128), 1) >= col_shift
    first = jnp.where(keep, block[:, :128], block[:, -128:])
    return jnp.concatenate([first, block[:, 128:-128]], axis=1)


def unwrap_lanes(block, col_shift):
    rows = block.shape[0]
    keep = lax.broadcasted_iota(jnp.int32, (rows, 128), 1) >= col_shift
    zero = jnp.zeros((rows, 128), jnp.float32)
    first = jnp.where(keep, block[:, :128], zero)
    last = jnp.where(keep, zero, block[:, :128])
    return jnp.concatenate([first, block[:, 128:], last], axis=1)


def slots_kernel(
    meta,
    tile_hbm,
    right_a_hbm,
    right_b_hbm,
    lower_a_hbm,
    lower_b_hbm,
    lower_c_hbm,
    corner_a_hbm,
    corner_up_hbm,
    corner_side_hbm,
    amps_hbm,
    pupil_hbm,
    mat_hi_hbm,
    mat_lo_hbm,
    mat_t_hi_hbm,
    mat_t_lo_hbm,
    own_out,
    right_out,
    lower_ab_out,
    lower_c_out,
    corner_a_out,
    corner_b_out,
    dpup_out,
    region,
    grads,
    win,
    left_hi,
    left_lo,
    right_hi,
    right_lo,
    cols_f32,
    rows_f32,
    dwin,
    dpup,
    amps,
    pupil,
    mat_hi,
    mat_lo,
    mat_t_hi,
    mat_t_lo,
    in_sems,
    out_sems,
):
    side = pupil.shape[-1]
    short = side // RADIX
    tile_rows, tile_cols = tile_hbm.shape[1:]
    slots = amps_hbm.shape[0]
    lanes = 128
    wide = side + lanes
    half = side // 2

    def pieces(buffer):
        top, bottom = pl.ds(0, tile_rows), pl.ds(tile_rows, side)
        return (
            buffer.at[:, top, pl.ds(0, tile_cols)],
            buffer.at[:, top, pl.ds(tile_cols, half)],
            buffer.at[:, top, pl.ds(tile_cols + half, half)],
            buffer.at[:, bottom, pl.ds(0, half)],
            buffer.at[:, bottom, pl.ds(half, half)],
            buffer.at[:, bottom, pl.ds(side, tile_cols - side)],
            buffer.at[:, bottom, pl.ds(tile_cols, half)],
            buffer.at[:, bottom, pl.ds(tile_cols + half, half)],
        )

    odd = meta[slots, 0]
    targets = pieces(region)
    sources = (
        tile_hbm,
        right_a_hbm,
        right_b_hbm,
        lower_a_hbm,
        lower_b_hbm,
        lower_c_hbm,
        corner_a_hbm,
    )
    loads = [
        pltpu.make_async_copy(src, dst, in_sems.at[n])
        for n, (src, dst) in enumerate(zip(sources, targets))
    ]
    for load in loads:
        load.start()
    from_side = pltpu.make_async_copy(corner_side_hbm, targets[7], in_sems.at[7])
    from_below = pltpu.make_async_copy(corner_up_hbm, targets[7], in_sems.at[7])
    pl.when(odd == 1)(from_side.start)
    pl.when(odd != 1)(from_below.start)
    loads.append(from_side)
    late = (
        (pupil_hbm, pupil),
        (mat_hi_hbm, mat_hi),
        (mat_lo_hbm, mat_lo),
        (mat_t_hi_hbm, mat_t_hi),
        (mat_t_lo_hbm, mat_t_lo),
        (amps_hbm, amps),
    )
    late_loads = [
        pltpu.make_async_copy(src, dst, in_sems.at[8 + n]) for n, (src, dst) in enumerate(late)
    ]
    for load in late_loads:
        load.start()

    top, bottom = pl.ds(0, tile_rows), pl.ds(tile_rows, side)
    outs = (
        (corner_a_out, bottom, pl.ds(tile_cols, half)),
        (corner_b_out, bottom, pl.ds(tile_cols + half, half)),
        (lower_c_out, bottom, pl.ds(side, tile_cols - side)),
        (lower_ab_out, bottom, pl.ds(0, side)),
        (right_out, top, pl.ds(tile_cols, side)),
        (own_out, top, pl.ds(0, tile_cols)),
    )
    stores = [
        pltpu.make_async_copy(grads.at[:, rows, cols], dst, out_sems.at[n])
        for n, (dst, rows, cols) in enumerate(outs)
    ]
    dpup_store = pltpu.make_async_copy(dpup, dpup_out, out_sems.at[6])
    lower_stores = stores[:4]
    upper_stores = stores[4:]

    zero_rows = 16

    @pl.loop(0, grads.shape[1] // zero_rows)
    def _(step):
        rows = pl.ds(pl.multiple_of(step * zero_rows, zero_rows), zero_rows)
        grads[:, rows, :] = jnp.zeros((2, zero_rows, grads.shape[2]), jnp.float32)

    @pl.loop(0, side // zero_rows)
    def _(step):
        rows = pl.ds(pl.multiple_of(step * zero_rows, zero_rows), zero_rows)
        dpup[:, rows, :] = jnp.zeros((2, zero_rows, side), jnp.float32)

    for load in loads:
        load.wait()

    count = meta[0, 2]
    for slot in range(1, slots):
        count = count + meta[slot, 2]

    def one_slot(slot):
        row = meta[slot, 0]
        col = meta[slot, 1]
        col_base = pl.multiple_of((col // lanes) * lanes, lanes)
        col_shift = col - col_base
        row_base = pl.multiple_of((row // 8) * 8, 8)
        row_shift = row - row_base

        @pl.loop(0, side // 32, unroll=2)
        def _(step):
            base = pl.multiple_of(step * 32, 32)
            rows = pl.ds(pl.multiple_of(row_base + base, 8), 32)
            for plane in range(2):
                block = region[plane, rows, pl.ds(col_base, wide)]
                win[plane, pl.ds(base, 32), :] = wrap_lanes(block, col_shift)

        first_keep = lax.broadcasted_iota(jnp.int32, (8, side), 0) >= row_shift
        last_rows = pl.ds(pl.multiple_of(row_base + side, 8), 8)
        for plane in range(2):
            block = region[plane, last_rows, pl.ds(col_base, wide)]
            block = wrap_lanes(block, col_shift)
            win[plane, :8, :] = jnp.where(first_keep, win[plane, :8, :], block)

        @pl.when(slot == 0)
        def _():
            for load in late_loads:
                load.wait()

        for start in (0, half):
            for base in range(0, short, 16):
                for col0 in range(start, start + half, short):
                    cols = pl.ds(col0, short)
                    values = []
                    for q in range(RADIX):
                        rows = pl.ds(base + q * short, 16)
                        wr, wi = win[0, rows, cols], win[1, rows, cols]
                        pr, pi = pupil[slot, 0, rows, cols], pupil[slot, 1, rows, cols]
                        values.append((wr * pr - wi * pi, wr * pi + wi * pr))
                    for p, (re, im) in enumerate(butterfly(values, 1)):
                        for offset, value in ((0, re), (short, im)):
                            hi, lo = split(value)
                            rows = pl.ds(base + offset, 16)
                            left_hi[p, rows, cols] = hi
                            left_lo[p, rows, cols] = lo
            cols = pl.ds(start, half)
            for p in range(RADIX):
                rows_f32[p, :, cols] = left_dot(
                    mat_hi[p], mat_lo[p], left_hi[p, :, cols], left_lo[p, :, cols]
                )

        for p in range(RADIX):
            for base in range(0, short, 16):
                values = []
                for q in range(RADIX):
                    cols = pl.ds(q * short, short)
                    values.append(
                        (
                            rows_f32[p, pl.ds(base, 16), cols],
                            rows_f32[p, pl.ds(base + short, 16), cols],
                        )
                    )
                for t, (re, im) in enumerate(butterfly(values, 1)):
                    for offset, value in ((0, re), (short, im)):
                        hi, lo = split(value)
                        rows = pl.ds(base + p * short, 16)
                        right_hi[t, rows, pl.ds(offset, short)] = hi
                        right_lo[t, rows, pl.ds(offset, short)] = lo

        for t in range(RADIX):
            for start in (0, half):
                rows = pl.ds(start, half)
                field = right_dot(
                    right_hi[t, rows, :], right_lo[t, rows, :], mat_t_hi[t], mat_t_lo[t]
                )
                fre, fim = field[:, :short], field[:, short:]
                measured = amps[slot, rows, pl.ds(t * short, short)]
                factor = 1.0 - measured * lax.rsqrt(fre * fre + fim * fim + 1.0)
                residual = jnp.concatenate([factor * fre, factor * fim], axis=1)
                hi, lo = split(residual)
                cols_f32[t, rows, :] = right_dot(hi, lo, mat_hi[t], mat_lo[t])

        for p in range(RADIX):
            for base in range(0, short, 16):
                rows = pl.ds(base + p * short, 16)
                values = [
                    (cols_f32[t, rows, pl.ds(0, short)], cols_f32[t, rows, pl.ds(short, short)])
                    for t in range(RADIX)
                ]
                for q, (re, im) in enumerate(butterfly(values, -1)):
                    cols = pl.ds(q * short, short)
                    for offset, value in ((0, re), (short, im)):
                        hi, lo = split(value)
                        left_hi[p, pl.ds(base + offset, 16), cols] = hi
                        left_lo[p, pl.ds(base + offset, 16), cols] = lo

        for start in (0, half):
            cols = pl.ds(start, half)
            for p in range(RADIX):
                rows_f32[p, :, cols] = left_dot(
                    mat_t_hi[p], mat_t_lo[p], left_hi[p, :, cols], left_lo[p, :, cols]
                )
            for base in range(0, short, 8):
                for col0 in range(start, start + half, short):
                    cols = pl.ds(col0, short)
                    values = [
                        (
                            rows_f32[p, pl.ds(base, 8), cols],
                            rows_f32[p, pl.ds(base + short, 8), cols],
                        )
                        for p in range(RADIX)
                    ]
                    for q, (re, im) in enumerate(butterfly(values, -1)):
                        rows = pl.ds(base + q * short, 8)
                        pr, pi = pupil[slot, 0, rows, cols], pupil[slot, 1, rows, cols]
                        dwin[0, rows, cols] = pr * re + pi * im
                        dwin[1, rows, cols] = pr * im - pi * re
                        wr, wi = win[0, rows, cols], win[1, rows, cols]
                        win[0, rows, cols] = wr * re + wi * im
                        win[1, rows, cols] = wr * im - wi * re

        @pl.loop(0, side // 32, unroll=2)
        def _(step):
            base = pl.multiple_of(step * 32, 32)
            after = pl.multiple_of((base + 32) % side, 8)
            for plane in range(2):
                tiles = [win[plane, pl.ds(base + 8 * i, 8), :] for i in range(4)]
                tiles.append(win[plane, pl.ds(after, 8), :])
                for i, tile in enumerate(shift_back(tiles, row_shift, col_shift)):
                    dpup[plane, pl.ds(base + 8 * i, 8), :] += tile

        last = slot == count - 1
        pl.when(last)(dpup_store.start)

        zero = jnp.zeros((8, side), jnp.float32)
        for plane in range(2):
            block = dwin[plane, :8, :]
            dwin[plane, :8, :] = jnp.where(first_keep, block, zero)
            dwin[plane, pl.ds(side, 8), :] = jnp.where(first_keep, zero, block)

        def place(step):
            base = pl.multiple_of(step * 40, 8)
            rows = pl.ds(pl.multiple_of(row_base + base, 8), 40)
            for plane in range(2):
                block = unwrap_lanes(dwin[plane, pl.ds(base, 40), :], col_shift)
                target = (plane, rows, pl.ds(col_base, wide))
                grads[target] = grads[target] + block

        steps = (side + 8) // 40
        above = (tile_rows - row_base) // 40
        pl.loop(above, steps)(place)

        @pl.when(last)
        def _():
            for store in lower_stores:
                store.start()

        pl.loop(0, above)(place)

    pl.loop(0, count)(one_slot)

    @pl.when(count == 0)
    def _():
        for store in [dpup_store] + lower_stores:
            store.start()
        for load in late_loads:
            load.wait()

    for store in upper_stores:
        store.start()
    for store in [dpup_store] + stores:
        store.wait()


def slots_call(meta, tile, parts, amps, pupils):
    side = pupils.shape[-1]
    short = side // RADIX
    slots = amps.shape[0]
    tile_rows, tile_cols = tile.shape[1:]
    high, low = dft_blocks(side)
    tables = [jnp.asarray(x) for x in (high, low, high.transpose(0, 2, 1), low.transpose(0, 2, 1))]
    anywhere = pl.BlockSpec(memory_space=pl.ANY)
    f32, bf16 = jnp.float32, jnp.bfloat16
    region = (2, tile_rows + side, tile_cols + side)
    _, _, _, _, lower_c, corner_a, corner_b, _ = parts
    right = jax.ShapeDtypeStruct((2, tile_rows, side), f32)
    lower_ab = jax.ShapeDtypeStruct((2, side, side), f32)
    outs = (tile, right, lower_ab, lower_c, corner_a, corner_b, jax.ShapeDtypeStruct(pupils.shape[1:], f32))
    table = pltpu.VMEM(high.shape, bf16)
    return pl.pallas_call(
        slots_kernel,
        out_shape=[jax.ShapeDtypeStruct(x.shape, f32) for x in outs],
        in_specs=[pl.BlockSpec(memory_space=pltpu.SMEM)] + [anywhere] * (len(parts) + 7),
        out_specs=[anywhere] * len(outs),
        scratch_shapes=[
            pltpu.VMEM(region, f32),
            pltpu.VMEM(region, f32),
            pltpu.VMEM((2, side, side), f32),
            pltpu.VMEM((RADIX, 2 * short, side), bf16),
            pltpu.VMEM((RADIX, 2 * short, side), bf16),
            pltpu.VMEM((RADIX, side, 2 * short), bf16),
            pltpu.VMEM((RADIX, side, 2 * short), bf16),
            pltpu.VMEM((RADIX, side, 2 * short), f32),
            pltpu.VMEM((RADIX, 2 * short, side), f32),
            pltpu.VMEM((2, side + 8, side), f32),
            pltpu.VMEM((2, side, side), f32),
            pltpu.VMEM(amps.shape, f32),
            pltpu.VMEM(pupils.shape, f32),
            table,
            table,
            table,
            table,
            pltpu.SemaphoreType.DMA((14,)),
            pltpu.SemaphoreType.DMA((7,)),
        ],
        compiler_params=pltpu.CompilerParams(vmem_limit_bytes=56 * 1024 * 1024),
        cost_estimate=pl.CostEstimate(
            flops=slots * 48 * 2 * 4 * short * short * side,
            bytes_accessed=40 * 1024 * 1024,
            transcendentals=slots * side * side,
        ),
        name="slots",
    )(meta, tile, *parts, amps, pupils, *tables)


def exact_parts(value):
    hi, rest = split(value)
    rest = value - hi.astype(jnp.float32)
    return (hi, *split(rest))


def prepare_kernel(meta, amps, pupil, perm_rows, perm_cols, amps_out, pupil_out):
    value = sum(dot(part, perm_cols[...]) for part in exact_parts(amps[0]))
    amps_out[0] = sum(dot(perm_rows[...], part) for part in exact_parts(value))

    slot = pl.program_id(0)
    row_shift = meta[slot, 0] % 8
    col_shift = meta[slot, 1] % 128
    side = pupil.shape[-1]

    @pl.loop(0, side // 32, unroll=2)
    def _(step):
        base = pl.multiple_of(step * 32, 32)
        before = pl.multiple_of((base + side - 8) % side, 8)
        for plane in range(2):
            tiles = [pupil[plane, pl.ds(before, 8), :]]
            tiles += [pupil[plane, pl.ds(base + 8 * i, 8), :] for i in range(4)]
            for i, tile in enumerate(shift_on(tiles, row_shift, col_shift)):
                pupil_out[0, plane, pl.ds(base + 8 * i, 8), :] = tile


def prepare(meta, amps, pupil):
    slots, side, _ = amps.shape
    index = np.arange(side)
    perm = np.zeros((side, side), ml_dtypes.bfloat16)
    perm[index, (index % RADIX) * (side // RADIX) + index // RADIX] = 1
    block = pl.BlockSpec((1, side, side), lambda s: (s, 0, 0))
    table = pl.BlockSpec((side, side), lambda s: (0, 0))
    return pl.pallas_call(
        prepare_kernel,
        grid=(slots,),
        out_shape=[
            jax.ShapeDtypeStruct(amps.shape, amps.dtype),
            jax.ShapeDtypeStruct((slots, 2, side, side), pupil.dtype),
        ],
        in_specs=[
            pl.BlockSpec(memory_space=pltpu.SMEM),
            block,
            pl.BlockSpec((2, side, side), lambda s: (0, 0, 0)),
            table,
            table,
        ],
        out_specs=[block, pl.BlockSpec((1, 2, side, side), lambda s: (s, 0, 0, 0))],
        compiler_params=pltpu.CompilerParams(vmem_limit_bytes=32 * 1024 * 1024),
        cost_estimate=pl.CostEstimate(
            flops=slots * 12 * side**3, bytes_accessed=24 * slots * side**2, transcendentals=0
        ),
        name="prepare",
    )(meta, amps, pupil, jnp.asarray(perm.T), jnp.asarray(perm))


def along(axis_pairs, members):
    n_ty, n_tx = members
    pairs = []
    for i in range(n_ty):
        for j in range(n_tx):
            target = axis_pairs(i, j)
            if target is not None and 0 <= target[0] < n_ty and 0 <= target[1] < n_tx:
                pairs.append((i * n_tx + j, target[0] * n_tx + target[1]))
    return pairs


def send(array, rule):
    sizes = (lax.axis_size("ty"), lax.axis_size("tx"))
    return lax.ppermute(array, ("ty", "tx"), along(rule, sizes))


def halve(value, bit):
    rows = value.shape[0] // 2
    mine = lax.axis_index("ty") // bit % 2
    kept = lax.dynamic_slice_in_dim(value, mine * rows, rows, 0)
    sent = lax.dynamic_slice_in_dim(value, (1 - mine) * rows, rows, 0)
    received = lax.ppermute(sent, "ty", [(i, i ^ bit) for i in range(lax.axis_size("ty"))])
    return kept + received


def double(value, bit):
    mine = lax.axis_index("ty") // bit % 2
    other = lax.ppermute(value, "ty", [(i, i ^ bit) for i in range(lax.axis_size("ty"))])
    first = jnp.where(mine == 0, value, other)
    second = jnp.where(mine == 0, other, value)
    return jnp.concatenate([first, second], axis=0)


def scatter(value, axis, inner):
    size, own = lax.axis_size(axis), lax.axis_index(axis) // inner
    members = size // inner
    rows = value.shape[0] // members
    total = lax.dynamic_slice_in_dim(value, own * rows, rows, 0)
    for step in range(1, members):
        pairs = [(i, (i + step * inner) % size) for i in range(size)]
        piece = lax.dynamic_slice_in_dim(value, (own + step) % members * rows, rows, 0)
        total = total + lax.ppermute(piece, axis, pairs)
    return total


def after(value, *arrivals):
    return lax.optimization_barrier((value, *arrivals))[0]


def body(spectrum, pupil, amplitudes, offsets, live):
    side = pupil.shape[-1]
    half = side // 2
    tile_rows, tile_cols = spectrum.shape[1:]
    own_ty, own_tx = lax.axis_index("ty"), lax.axis_index("tx")
    rows_local = offsets[:, 0] - own_ty * tile_rows
    cols_local = offsets[:, 1] - own_tx * tile_cols
    meta = jnp.stack([rows_local, cols_local, live], axis=1)
    meta = jnp.concatenate([meta, jnp.full((1, 3), own_ty % 2, jnp.int32)], axis=0)

    def left(i, j):
        return (i, j - 1)

    def up(i, j):
        return (i - 1, j)

    lower_b = send(spectrum[:, :side, half:side], up)
    right_a = send(spectrum[:, :, :half], left)
    right_b = send(after(spectrum[:, :, half:side], lower_b), left)
    lower_a = send(spectrum[:, :side, :half], up)
    lower_c = send(spectrum[:, :side, side:], up)
    amps, pupils = prepare(meta, amplitudes, pupil)
    lower_b, amps = lax.optimization_barrier((lower_b, amps))
    corner_side = send(lower_b, lambda i, j: (i, j - 1) if i % 2 else None)
    corner_a = send(right_a[:, :side], up)
    right_b_again = after(right_b, corner_side)
    corner_up = send(right_b_again[:, :side], lambda i, j: (i - 1, j) if i % 2 else None)

    parts = (right_a, right_b, lower_a, lower_b, lower_c, corner_a, corner_up, corner_side)
    own_g, right_g, lower_ab_g, lower_c_g, corner_a_g, corner_b_g, dpup = slots_call(
        meta, spectrum, parts, amps, pupils
    )

    def down(i, j):
        return (i + 1, j)

    def right(i, j):
        return (i, j + 1)

    back_side = send(corner_b_g, lambda i, j: (i, j + 1) if i % 2 else None)
    back_a = send(corner_a_g, down)
    back_down = send(corner_b_g, lambda i, j: None if i % 2 else (i + 1, j))
    n_ty, n_tx = lax.axis_size("ty"), lax.axis_size("tx")
    over_cores = halve(dpup.reshape(-1, side), 1)
    over_ty = scatter(over_cores, "ty", 2)
    lower_c = send(after(lower_c_g, over_ty), down)
    over_ty = after(over_ty, back_a, back_down, back_side)
    part = scatter(over_ty, "tx", 1) * (1.0 / math.sqrt(n_ty * n_tx))
    right_total = right_g + jnp.concatenate([back_a, back_down], axis=2)
    right_back = send(after(right_total, part), right)
    lower_ab = send(lower_ab_g.at[:, :, half:].add(after(back_side, part)), down)
    groups = [
        [(2 * k + core) * n_tx + j for k in range(n_ty // 2) for j in range(n_tx)]
        for core in range(2)
    ]
    part = lax.all_gather(part, ("ty", "tx"), axis_index_groups=groups, axis=0, tiled=True)
    spec_grad = jnp.concatenate(
        [
            own_g[:, :, :side] + lower_ab + right_back,
            own_g[:, :, side:] + lower_c,
        ],
        axis=2,
    )
    return spec_grad, double(part, 1).reshape(pupil.shape)


def solution(mesh):
    return jax.shard_map(
        body,
        mesh=mesh,
        in_specs=(
            P(None, "ty", "tx"),
            P(),
            P(("ty", "tx"), None, None),
            P(("ty", "tx"), None),
            P(("ty", "tx")),
        ),
        out_specs=(P(None, "ty", "tx"), P()),
        check_vma=False,
    )
```

```python
import math

import jax
import jax.numpy as jnp
import ml_dtypes
import numpy as np
from jax import lax
from jax.experimental import pallas as pl
from jax.experimental.pallas import tpu as pltpu
from jax.sharding import PartitionSpec as P

RADIX = 4


def dft_blocks(length):
    short = length // RADIX
    out_idx = np.arange(short)[:, None]
    in_idx = np.arange(short)[None, :]
    blocks = []
    for p in range(RADIX):
        phase = (p * in_idx + RADIX * out_idx * in_idx) % length
        angle = phase * (2.0 * math.pi / length)
        cos = np.cos(angle) / math.sqrt(length)
        sin = np.sin(angle) / math.sqrt(length)
        blocks.append(np.block([[cos, -sin], [sin, cos]]))
    full = np.stack(blocks).astype(np.float32)
    high = full.astype(ml_dtypes.bfloat16)
    low = (full - high.astype(np.float32)).astype(ml_dtypes.bfloat16)
    return high, low


def split(value):
    high = value.astype(jnp.bfloat16)
    low = (value - high.astype(jnp.float32)).astype(jnp.bfloat16)
    return high, low


def dot(lhs, rhs):
    return jnp.dot(lhs, rhs, preferred_element_type=jnp.float32)


def left_dot(mat_hi, mat_lo, val_hi, val_lo):
    lhs = jnp.concatenate([mat_hi, mat_hi, mat_lo], axis=1)
    return dot(lhs, jnp.concatenate([val_hi, val_lo, val_hi], axis=0))


def right_dot(val_hi, val_lo, mat_hi, mat_lo):
    lhs = jnp.concatenate([val_hi, val_lo, val_hi], axis=1)
    return dot(lhs, jnp.concatenate([mat_hi, mat_hi, mat_lo], axis=0))


def butterfly(parts, sign):
    (r0, i0), (r1, i1), (r2, i2), (r3, i3) = parts
    sr, si, dr, di = r0 + r2, i0 + i2, r0 - r2, i0 - i2
    tr, ti, er, ei = r1 + r3, i1 + i3, r1 - r3, i1 - i3
    if sign < 0:
        er, ei = -er, -ei
    return [(sr + tr, si + ti), (dr - ei, di + er), (sr - tr, si - ti), (dr + ei, di - er)]


def row_index():
    return lax.broadcasted_iota(jnp.int32, (8, 128), 0)


def lane_index():
    return lax.broadcasted_iota(jnp.int32, (8, 128), 1)


def lane_tiles(tile):
    return [tile[:, i : i + 128] for i in range(0, tile.shape[1], 128)]


def rolled(tiles, amount, axis):
    return [[pltpu.roll(part, amount, axis) for part in tile] for tile in tiles]


def shift_on(tiles, row_shift, col_shift):
    keep = lane_index() >= col_shift
    tiles = rolled([lane_tiles(tile) for tile in tiles], col_shift, 1)
    tiles = [[jnp.where(keep, x, y) for x, y in zip(t, t[-1:] + t[:-1])] for t in tiles]
    keep = row_index() >= row_shift
    tiles = rolled(tiles, row_shift, 0)
    return [
        jnp.concatenate([jnp.where(keep, y, x) for x, y in zip(a, b)], axis=1)
        for a, b in zip(tiles, tiles[1:])
    ]


def shift_back(tiles, row_shift, col_shift):
    keep = lane_index() < 128 - col_shift
    tiles = rolled([lane_tiles(tile) for tile in tiles], (128 - col_shift) % 128, 1)
    tiles = [[jnp.where(keep, x, y) for x, y in zip(t, t[1:] + t[:1])] for t in tiles]
    keep = row_index() < 8 - row_shift
    tiles = rolled(tiles, (8 - row_shift) % 8, 0)
    return [
        jnp.concatenate([jnp.where(keep, x, y) for x, y in zip(a, b)], axis=1)
        for a, b in zip(tiles, tiles[1:])
    ]


def wrap_lanes(block, col_shift):
    rows = block.shape[0]
    keep = lax.broadcasted_iota(jnp.int32, (rows, 128), 1) >= col_shift
    first = jnp.where(keep, block[:, :128], block[:, -128:])
    return jnp.concatenate([first, block[:, 128:-128]], axis=1)


def unwrap_lanes(block, col_shift):
    rows = block.shape[0]
    keep = lax.broadcasted_iota(jnp.int32, (rows, 128), 1) >= col_shift
    zero = jnp.zeros((rows, 128), jnp.float32)
    first = jnp.where(keep, block[:, :128], zero)
    last = jnp.where(keep, zero, block[:, :128])
    return jnp.concatenate([first, block[:, 128:], last], axis=1)


def slots_kernel(
    meta,
    tile_hbm,
    right_a_hbm,
    right_b_hbm,
    lower_a_hbm,
    lower_bc_hbm,
    corner_a_hbm,
    corner_up_hbm,
    corner_side_hbm,
    amps_hbm,
    pupil_hbm,
    mat_hi_hbm,
    mat_lo_hbm,
    mat_t_hi_hbm,
    mat_t_lo_hbm,
    own_out,
    right_out,
    lower_ab_out,
    lower_c_out,
    corner_a_out,
    corner_b_out,
    dpup_out,
    region,
    grads,
    win,
    left_hi,
    left_lo,
    right_hi,
    right_lo,
    cols_f32,
    rows_f32,
    dwin,
    dpup,
    amps,
    pupil,
    mat_hi,
    mat_lo,
    mat_t_hi,
    mat_t_lo,
    in_sems,
    slot_sems,
    out_sems,
):
    side = pupil.shape[-1]
    short = side // RADIX
    tile_rows, tile_cols = tile_hbm.shape[1:]
    slots = amps_hbm.shape[0]
    lanes = 128
    wide = side + lanes
    half = side // 2
    cut = corner_a_hbm.shape[-1]

    def pieces(buffer):
        top, bottom = pl.ds(0, tile_rows), pl.ds(tile_rows, side)
        return (
            buffer.at[:, top, pl.ds(0, tile_cols)],
            buffer.at[:, top, pl.ds(tile_cols, cut)],
            buffer.at[:, top, pl.ds(tile_cols + cut, side - cut)],
            buffer.at[:, bottom, pl.ds(0, cut)],
            buffer.at[:, bottom, pl.ds(cut, tile_cols - cut)],
            buffer.at[:, bottom, pl.ds(tile_cols, cut)],
            buffer.at[:, bottom, pl.ds(tile_cols + cut, side - cut)],
        )

    odd = meta[slots, 0]
    targets = pieces(region)
    sources = (
        tile_hbm,
        right_a_hbm,
        right_b_hbm,
        lower_a_hbm,
        lower_bc_hbm,
        corner_a_hbm,
    )
    loads = [
        pltpu.make_async_copy(src, dst, in_sems.at[n])
        for n, (src, dst) in enumerate(zip(sources, targets))
    ]
    for load in loads:
        load.start()
    from_side = pltpu.make_async_copy(corner_side_hbm, targets[6], in_sems.at[6])
    from_below = pltpu.make_async_copy(corner_up_hbm, targets[6], in_sems.at[6])
    pl.when(odd == 1)(from_side.start)
    pl.when(odd != 1)(from_below.start)
    loads.append(from_side)
    late = (
        (mat_hi_hbm, mat_hi),
        (mat_lo_hbm, mat_lo),
        (mat_t_hi_hbm, mat_t_hi),
        (mat_t_lo_hbm, mat_t_lo),
    )
    late_loads = [
        pltpu.make_async_copy(src, dst, in_sems.at[7 + n]) for n, (src, dst) in enumerate(late)
    ]
    for load in late_loads:
        load.start()
    count = meta[0, 2]
    for slot in range(1, slots):
        count = count + meta[slot, 2]

    def slot_loads(slot):
        return (
            pltpu.make_async_copy(pupil_hbm.at[slot], pupil.at[slot], slot_sems.at[0, slot]),
            pltpu.make_async_copy(amps_hbm.at[slot], amps.at[slot], slot_sems.at[1, slot]),
        )

    @pl.loop(0, count)
    def _(slot):
        for load in slot_loads(slot):
            load.start()

    top, bottom = pl.ds(0, tile_rows), pl.ds(tile_rows, side)
    outs = (
        (corner_a_out, bottom, pl.ds(tile_cols, cut)),
        (corner_b_out, bottom, pl.ds(tile_cols + cut, side - cut)),
        (lower_c_out, bottom, pl.ds(side, tile_cols - side)),
        (lower_ab_out, bottom, pl.ds(0, side)),
        (right_out, top, pl.ds(tile_cols, side)),
        (own_out, top, pl.ds(0, tile_cols)),
    )
    stores = [
        pltpu.make_async_copy(grads.at[:, rows, cols], dst, out_sems.at[n])
        for n, (dst, rows, cols) in enumerate(outs)
    ]
    dpup_store = pltpu.make_async_copy(dpup, dpup_out, out_sems.at[6])
    lower_stores = stores[:4]
    upper_stores = stores[4:]

    zero_rows = 16

    @pl.loop(0, grads.shape[1] // zero_rows)
    def _(step):
        rows = pl.ds(pl.multiple_of(step * zero_rows, zero_rows), zero_rows)
        grads[:, rows, :] = jnp.zeros((2, zero_rows, grads.shape[2]), jnp.float32)

    @pl.loop(0, side // zero_rows)
    def _(step):
        rows = pl.ds(pl.multiple_of(step * zero_rows, zero_rows), zero_rows)
        dpup[:, rows, :] = jnp.zeros((2, zero_rows, side), jnp.float32)

    for load in loads:
        load.wait()

    def one_slot(slot):
        row = meta[slot, 0]
        col = meta[slot, 1]
        col_base = pl.multiple_of((col // lanes) * lanes, lanes)
        col_shift = col - col_base
        row_base = pl.multiple_of((row // 8) * 8, 8)
        row_shift = row - row_base

        @pl.loop(0, side // 32, unroll=2)
        def _(step):
            base = pl.multiple_of(step * 32, 32)
            rows = pl.ds(pl.multiple_of(row_base + base, 8), 32)
            for plane in range(2):
                block = region[plane, rows, pl.ds(col_base, wide)]
                win[plane, pl.ds(base, 32), :] = wrap_lanes(block, col_shift)

        first_keep = lax.broadcasted_iota(jnp.int32, (8, side), 0) >= row_shift
        last_rows = pl.ds(pl.multiple_of(row_base + side, 8), 8)
        for plane in range(2):
            block = region[plane, last_rows, pl.ds(col_base, wide)]
            block = wrap_lanes(block, col_shift)
            win[plane, :8, :] = jnp.where(first_keep, win[plane, :8, :], block)

        pupil_load, amps_load = slot_loads(slot)
        pupil_load.wait()

        @pl.when(slot == 0)
        def _():
            for load in late_loads:
                load.wait()

        for start in (0, half):
            for base in range(0, short, 16):
                for col0 in range(start, start + half, short):
                    cols = pl.ds(col0, short)
                    values = []
                    for q in range(RADIX):
                        rows = pl.ds(base + q * short, 16)
                        wr, wi = win[0, rows, cols], win[1, rows, cols]
                        pr, pi = pupil[slot, 0, rows, cols], pupil[slot, 1, rows, cols]
                        values.append((wr * pr - wi * pi, wr * pi + wi * pr))
                    for p, (re, im) in enumerate(butterfly(values, 1)):
                        for offset, value in ((0, re), (short, im)):
                            hi, lo = split(value)
                            rows = pl.ds(base + offset, 16)
                            left_hi[p, rows, cols] = hi
                            left_lo[p, rows, cols] = lo
            cols = pl.ds(start, half)
            for p in range(RADIX):
                rows_f32[p, :, cols] = left_dot(
                    mat_hi[p], mat_lo[p], left_hi[p, :, cols], left_lo[p, :, cols]
                )

        for p in range(RADIX):
            for base in range(0, short, 16):
                values = []
                for q in range(RADIX):
                    cols = pl.ds(q * short, short)
                    values.append(
                        (
                            rows_f32[p, pl.ds(base, 16), cols],
                            rows_f32[p, pl.ds(base + short, 16), cols],
                        )
                    )
                for t, (re, im) in enumerate(butterfly(values, 1)):
                    for offset, value in ((0, re), (short, im)):
                        hi, lo = split(value)
                        rows = pl.ds(base + p * short, 16)
                        right_hi[t, rows, pl.ds(offset, short)] = hi
                        right_lo[t, rows, pl.ds(offset, short)] = lo

        amps_load.wait()

        for t in range(RADIX):
            for start in (0, half):
                rows = pl.ds(start, half)
                field = right_dot(
                    right_hi[t, rows, :], right_lo[t, rows, :], mat_t_hi[t], mat_t_lo[t]
                )
                fre, fim = field[:, :short], field[:, short:]
                measured = amps[slot, rows, pl.ds(t * short, short)]
                factor = 1.0 - measured * lax.rsqrt(fre * fre + fim * fim + 1.0)
                residual = jnp.concatenate([factor * fre, factor * fim], axis=1)
                hi, lo = split(residual)
                cols_f32[t, rows, :] = right_dot(hi, lo, mat_hi[t], mat_lo[t])

        for p in range(RADIX):
            for base in range(0, short, 16):
                rows = pl.ds(base + p * short, 16)
                values = [
                    (cols_f32[t, rows, pl.ds(0, short)], cols_f32[t, rows, pl.ds(short, short)])
                    for t in range(RADIX)
                ]
                for q, (re, im) in enumerate(butterfly(values, -1)):
                    cols = pl.ds(q * short, short)
                    for offset, value in ((0, re), (short, im)):
                        hi, lo = split(value)
                        left_hi[p, pl.ds(base + offset, 16), cols] = hi
                        left_lo[p, pl.ds(base + offset, 16), cols] = lo

        for start in (0, half):
            cols = pl.ds(start, half)
            for p in range(RADIX):
                rows_f32[p, :, cols] = left_dot(
                    mat_t_hi[p], mat_t_lo[p], left_hi[p, :, cols], left_lo[p, :, cols]
                )
            for base in range(0, short, 8):
                for col0 in range(start, start + half, short):
                    cols = pl.ds(col0, short)
                    values = [
                        (
                            rows_f32[p, pl.ds(base, 8), cols],
                            rows_f32[p, pl.ds(base + short, 8), cols],
                        )
                        for p in range(RADIX)
                    ]
                    for q, (re, im) in enumerate(butterfly(values, -1)):
                        rows = pl.ds(base + q * short, 8)
                        pr, pi = pupil[slot, 0, rows, cols], pupil[slot, 1, rows, cols]
                        dwin[0, rows, cols] = pr * re + pi * im
                        dwin[1, rows, cols] = pr * im - pi * re
                        wr, wi = win[0, rows, cols], win[1, rows, cols]
                        win[0, rows, cols] = wr * re + wi * im
                        win[1, rows, cols] = wr * im - wi * re

        @pl.loop(0, side // 32, unroll=2)
        def _(step):
            base = pl.multiple_of(step * 32, 32)
            after = pl.multiple_of((base + 32) % side, 8)
            for plane in range(2):
                tiles = [win[plane, pl.ds(base + 8 * i, 8), :] for i in range(4)]
                tiles.append(win[plane, pl.ds(after, 8), :])
                for i, tile in enumerate(shift_back(tiles, row_shift, col_shift)):
                    dpup[plane, pl.ds(base + 8 * i, 8), :] += tile

        last = slot == count - 1
        pl.when(last)(dpup_store.start)

        zero = jnp.zeros((8, side), jnp.float32)
        for plane in range(2):
            block = dwin[plane, :8, :]
            dwin[plane, :8, :] = jnp.where(first_keep, block, zero)
            dwin[plane, pl.ds(side, 8), :] = jnp.where(first_keep, zero, block)

        def place(step):
            base = pl.multiple_of(step * 40, 8)
            rows = pl.ds(pl.multiple_of(row_base + base, 8), 40)
            for plane in range(2):
                block = unwrap_lanes(dwin[plane, pl.ds(base, 40), :], col_shift)
                target = (plane, rows, pl.ds(col_base, wide))
                grads[target] = grads[target] + block

        steps = (side + 8) // 40
        above = (tile_rows - row_base) // 40
        pl.loop(above, steps)(place)

        @pl.when(last)
        def _():
            for store in lower_stores:
                store.start()

        pl.loop(0, above)(place)

    pl.loop(0, count)(one_slot)

    @pl.when(count == 0)
    def _():
        for store in [dpup_store] + lower_stores:
            store.start()
        for load in late_loads:
            load.wait()

    for store in upper_stores:
        store.start()
    for store in [dpup_store] + stores:
        store.wait()


def slots_call(meta, tile, parts, amps, pupils):
    side = pupils.shape[-1]
    short = side // RADIX
    slots = amps.shape[0]
    tile_rows, tile_cols = tile.shape[1:]
    high, low = dft_blocks(side)
    tables = [jnp.asarray(x) for x in (high, low, high.transpose(0, 2, 1), low.transpose(0, 2, 1))]
    anywhere = pl.BlockSpec(memory_space=pl.ANY)
    f32, bf16 = jnp.float32, jnp.bfloat16
    region = (2, tile_rows + side, tile_cols + side)
    corner_a, corner_b, _ = parts[-3:]
    lower_c = jax.ShapeDtypeStruct((2, side, tile_cols - side), f32)
    right = jax.ShapeDtypeStruct((2, tile_rows, side), f32)
    lower_ab = jax.ShapeDtypeStruct((2, side, side), f32)
    outs = (tile, right, lower_ab, lower_c, corner_a, corner_b, jax.ShapeDtypeStruct(pupils.shape[1:], f32))
    table = pltpu.VMEM(high.shape, bf16)
    return pl.pallas_call(
        slots_kernel,
        out_shape=[jax.ShapeDtypeStruct(x.shape, f32) for x in outs],
        in_specs=[pl.BlockSpec(memory_space=pltpu.SMEM)] + [anywhere] * (len(parts) + 7),
        out_specs=[anywhere] * len(outs),
        scratch_shapes=[
            pltpu.VMEM(region, f32),
            pltpu.VMEM(region, f32),
            pltpu.VMEM((2, side, side), f32),
            pltpu.VMEM((RADIX, 2 * short, side), bf16),
            pltpu.VMEM((RADIX, 2 * short, side), bf16),
            pltpu.VMEM((RADIX, side, 2 * short), bf16),
            pltpu.VMEM((RADIX, side, 2 * short), bf16),
            pltpu.VMEM((RADIX, side, 2 * short), f32),
            pltpu.VMEM((RADIX, 2 * short, side), f32),
            pltpu.VMEM((2, side + 8, side), f32),
            pltpu.VMEM((2, side, side), f32),
            pltpu.VMEM(amps.shape, f32),
            pltpu.VMEM(pupils.shape, f32),
            table,
            table,
            table,
            table,
            pltpu.SemaphoreType.DMA((11,)),
            pltpu.SemaphoreType.DMA((2, slots)),
            pltpu.SemaphoreType.DMA((7,)),
        ],
        compiler_params=pltpu.CompilerParams(vmem_limit_bytes=56 * 1024 * 1024),
        cost_estimate=pl.CostEstimate(
            flops=slots * 48 * 2 * 4 * short * short * side,
            bytes_accessed=40 * 1024 * 1024,
            transcendentals=slots * side * side,
        ),
        name="slots",
    )(meta, tile, *parts, amps, pupils, *tables)


def exact_parts(value):
    hi, rest = split(value)
    rest = value - hi.astype(jnp.float32)
    return (hi, *split(rest))


def prepare_kernel(meta, amps, pupil, perm_rows, perm_cols, amps_out, pupil_out):
    value = sum(dot(part, perm_cols[...]) for part in exact_parts(amps[0]))
    amps_out[0] = sum(dot(perm_rows[...], part) for part in exact_parts(value))

    slot = pl.program_id(0)
    row_shift = meta[slot, 0] % 8
    col_shift = meta[slot, 1] % 128
    side = pupil.shape[-1]

    @pl.loop(0, side // 32, unroll=2)
    def _(step):
        base = pl.multiple_of(step * 32, 32)
        before = pl.multiple_of((base + side - 8) % side, 8)
        for plane in range(2):
            tiles = [pupil[plane, pl.ds(before, 8), :]]
            tiles += [pupil[plane, pl.ds(base + 8 * i, 8), :] for i in range(4)]
            for i, tile in enumerate(shift_on(tiles, row_shift, col_shift)):
                pupil_out[0, plane, pl.ds(base + 8 * i, 8), :] = tile


def prepare(meta, amps, pupil):
    slots, side, _ = amps.shape
    index = np.arange(side)
    perm = np.zeros((side, side), ml_dtypes.bfloat16)
    perm[index, (index % RADIX) * (side // RADIX) + index // RADIX] = 1
    block = pl.BlockSpec((1, side, side), lambda s: (s, 0, 0))
    table = pl.BlockSpec((side, side), lambda s: (0, 0))
    return pl.pallas_call(
        prepare_kernel,
        grid=(slots,),
        out_shape=[
            jax.ShapeDtypeStruct(amps.shape, amps.dtype),
            jax.ShapeDtypeStruct((slots, 2, side, side), pupil.dtype),
        ],
        in_specs=[
            pl.BlockSpec(memory_space=pltpu.SMEM),
            block,
            pl.BlockSpec((2, side, side), lambda s: (0, 0, 0)),
            table,
            table,
        ],
        out_specs=[block, pl.BlockSpec((1, 2, side, side), lambda s: (s, 0, 0, 0))],
        compiler_params=pltpu.CompilerParams(vmem_limit_bytes=32 * 1024 * 1024),
        cost_estimate=pl.CostEstimate(
            flops=slots * 12 * side**3, bytes_accessed=24 * slots * side**2, transcendentals=0
        ),
        name="prepare",
    )(meta, amps, pupil, jnp.asarray(perm.T), jnp.asarray(perm))


def along(axis_pairs, members):
    n_ty, n_tx = members
    pairs = []
    for i in range(n_ty):
        for j in range(n_tx):
            target = axis_pairs(i, j)
            if target is not None and 0 <= target[0] < n_ty and 0 <= target[1] < n_tx:
                pairs.append((i * n_tx + j, target[0] * n_tx + target[1]))
    return pairs


def send(array, rule):
    sizes = (lax.axis_size("ty"), lax.axis_size("tx"))
    return lax.ppermute(array, ("ty", "tx"), along(rule, sizes))


def halve(value, bit):
    rows = value.shape[0] // 2
    mine = lax.axis_index("ty") // bit % 2
    kept = lax.dynamic_slice_in_dim(value, mine * rows, rows, 0)
    sent = lax.dynamic_slice_in_dim(value, (1 - mine) * rows, rows, 0)
    received = lax.ppermute(sent, "ty", [(i, i ^ bit) for i in range(lax.axis_size("ty"))])
    return kept + received


def double(value, bit):
    mine = lax.axis_index("ty") // bit % 2
    other = lax.ppermute(value, "ty", [(i, i ^ bit) for i in range(lax.axis_size("ty"))])
    first = jnp.where(mine == 0, value, other)
    second = jnp.where(mine == 0, other, value)
    return jnp.concatenate([first, second], axis=0)


def scatter(value, axis, inner):
    size, own = lax.axis_size(axis), lax.axis_index(axis) // inner
    members = size // inner
    rows = value.shape[0] // members
    total = lax.dynamic_slice_in_dim(value, own * rows, rows, 0)
    for step in range(1, members):
        pairs = [(i, (i + step * inner) % size) for i in range(size)]
        piece = lax.dynamic_slice_in_dim(value, (own + step) % members * rows, rows, 0)
        total = total + lax.ppermute(piece, axis, pairs)
    return total


def after(value, *arrivals):
    return lax.optimization_barrier((value, *arrivals))[0]


def body(spectrum, pupil, amplitudes, offsets, live):
    side = pupil.shape[-1]
    cut = 3 * side // 4
    tile_rows, tile_cols = spectrum.shape[1:]
    own_ty, own_tx = lax.axis_index("ty"), lax.axis_index("tx")
    rows_local = offsets[:, 0] - own_ty * tile_rows
    cols_local = offsets[:, 1] - own_tx * tile_cols
    meta = jnp.stack([rows_local, cols_local, live], axis=1)
    meta = jnp.concatenate([meta, jnp.full((1, 3), own_ty % 2, jnp.int32)], axis=0)

    def left(i, j):
        return (i, j - 1)

    def up(i, j):
        return (i - 1, j)

    lower_bc = send(spectrum[:, :side, cut:], up)
    right_a = send(spectrum[:, :, :cut], left)
    right_b = send(spectrum[:, :, cut:side], left)
    lower_a = send(spectrum[:, :side, :cut], up)
    amps, pupils = prepare(meta, amplitudes, pupil)
    corner_a = send(right_a[:, :side], up)
    corner_side = send(lower_bc[:, :, : side - cut], lambda i, j: (i, j - 1) if i % 2 else None)
    right_b_again = after(right_b, corner_side)
    corner_up = send(right_b_again[:, :side], lambda i, j: (i - 1, j) if i % 2 else None)

    parts = (right_a, right_b, lower_a, lower_bc, corner_a, corner_up, corner_side)
    own_g, right_g, lower_ab_g, lower_c_g, corner_a_g, corner_b_g, dpup = slots_call(
        meta, spectrum, parts, amps, pupils
    )

    def down(i, j):
        return (i + 1, j)

    def right(i, j):
        return (i, j + 1)

    back_side = send(corner_b_g, lambda i, j: (i, j + 1) if i % 2 else None)
    back_a = send(corner_a_g, down)
    back_down = send(corner_b_g, lambda i, j: None if i % 2 else (i + 1, j))
    n_ty, n_tx = lax.axis_size("ty"), lax.axis_size("tx")
    part = halve(dpup.reshape(-1, side), 1)
    part, lower_c_g, back_a, back_down, back_side = lax.optimization_barrier(
        (part, lower_c_g, back_a, back_down, back_side)
    )
    lower_c = send(lower_c_g, down)
    over_tx = scatter(part, "tx", 1)
    right_total = right_g + jnp.concatenate([back_a, back_down], axis=2)
    right_back = send(after(right_total, over_tx), right)
    part = scatter(after(over_tx, lower_c), "ty", 2)
    part = part * (1.0 / math.sqrt(n_ty * n_tx))
    lower_ab = send(lower_ab_g.at[:, :, cut:].add(after(back_side, part)), down)
    groups = [
        [(2 * k + core) * n_tx + j for j in range(n_tx) for k in range(n_ty // 2)]
        for core in range(2)
    ]
    part = lax.all_gather(part, ("ty", "tx"), axis_index_groups=groups, axis=0, tiled=True)
    spec_grad = own_g.at[:, :, side:].add(lower_c)
    spec_grad = spec_grad.at[:, :, :side].add(lower_ab + right_back)
    return spec_grad, double(part, 1).reshape(pupil.shape)


def solution(mesh):
    return jax.shard_map(
        body,
        mesh=mesh,
        in_specs=(
            P(None, "ty", "tx"),
            P(),
            P(("ty", "tx"), None, None),
            P(("ty", "tx"), None),
            P(("ty", "tx")),
        ),
        out_specs=(P(None, "ty", "tx"), P()),
        check_vma=False,
    )
```

```python
import math

import jax
import jax.numpy as jnp
import ml_dtypes
import numpy as np
from jax import lax
from jax.experimental import pallas as pl
from jax.experimental.pallas import tpu as pltpu
from jax.sharding import PartitionSpec as P

RADIX = 4


def dft_blocks(length):
    short = length // RADIX
    out_idx = np.arange(short)[:, None]
    in_idx = np.arange(short)[None, :]
    blocks = []
    for p in range(RADIX):
        phase = (p * in_idx + RADIX * out_idx * in_idx) % length
        angle = phase * (2.0 * math.pi / length)
        cos = np.cos(angle) / math.sqrt(length)
        sin = np.sin(angle) / math.sqrt(length)
        blocks.append(np.block([[cos, -sin], [sin, cos]]))
    full = np.stack(blocks).astype(np.float32)
    high = full.astype(ml_dtypes.bfloat16)
    low = (full - high.astype(np.float32)).astype(ml_dtypes.bfloat16)
    return high, low


def split(value):
    high = value.astype(jnp.bfloat16)
    low = (value - high.astype(jnp.float32)).astype(jnp.bfloat16)
    return high, low


def dot(lhs, rhs):
    return jnp.dot(lhs, rhs, preferred_element_type=jnp.float32)


def left_dot(mat_hi, mat_lo, val_hi, val_lo):
    lhs = jnp.concatenate([mat_hi, mat_hi, mat_lo], axis=1)
    return dot(lhs, jnp.concatenate([val_hi, val_lo, val_hi], axis=0))


def right_dot(val_hi, val_lo, mat_hi, mat_lo):
    lhs = jnp.concatenate([val_hi, val_lo, val_hi], axis=1)
    return dot(lhs, jnp.concatenate([mat_hi, mat_hi, mat_lo], axis=0))


def butterfly(parts, sign):
    (r0, i0), (r1, i1), (r2, i2), (r3, i3) = parts
    sr, si, dr, di = r0 + r2, i0 + i2, r0 - r2, i0 - i2
    tr, ti, er, ei = r1 + r3, i1 + i3, r1 - r3, i1 - i3
    if sign < 0:
        er, ei = -er, -ei
    return [(sr + tr, si + ti), (dr - ei, di + er), (sr - tr, si - ti), (dr + ei, di - er)]


def row_index():
    return lax.broadcasted_iota(jnp.int32, (8, 128), 0)


def lane_index():
    return lax.broadcasted_iota(jnp.int32, (8, 128), 1)


def lane_tiles(tile):
    return [tile[:, i : i + 128] for i in range(0, tile.shape[1], 128)]


def rolled(tiles, amount, axis):
    return [[pltpu.roll(part, amount, axis) for part in tile] for tile in tiles]


def shift_on(tiles, row_shift, col_shift):
    keep = lane_index() >= col_shift
    tiles = rolled([lane_tiles(tile) for tile in tiles], col_shift, 1)
    tiles = [[jnp.where(keep, x, y) for x, y in zip(t, t[-1:] + t[:-1])] for t in tiles]
    keep = row_index() >= row_shift
    tiles = rolled(tiles, row_shift, 0)
    return [
        jnp.concatenate([jnp.where(keep, y, x) for x, y in zip(a, b)], axis=1)
        for a, b in zip(tiles, tiles[1:])
    ]


def shift_back(tiles, row_shift, col_shift):
    keep = lane_index() < 128 - col_shift
    tiles = rolled([lane_tiles(tile) for tile in tiles], (128 - col_shift) % 128, 1)
    tiles = [[jnp.where(keep, x, y) for x, y in zip(t, t[1:] + t[:1])] for t in tiles]
    keep = row_index() < 8 - row_shift
    tiles = rolled(tiles, (8 - row_shift) % 8, 0)
    return [
        jnp.concatenate([jnp.where(keep, x, y) for x, y in zip(a, b)], axis=1)
        for a, b in zip(tiles, tiles[1:])
    ]


def wrap_lanes(block, col_shift):
    rows = block.shape[0]
    keep = lax.broadcasted_iota(jnp.int32, (rows, 128), 1) >= col_shift
    first = jnp.where(keep, block[:, :128], block[:, -128:])
    return jnp.concatenate([first, block[:, 128:-128]], axis=1)


def unwrap_lanes(block, col_shift):
    rows = block.shape[0]
    keep = lax.broadcasted_iota(jnp.int32, (rows, 128), 1) >= col_shift
    zero = jnp.zeros((rows, 128), jnp.float32)
    first = jnp.where(keep, block[:, :128], zero)
    last = jnp.where(keep, zero, block[:, :128])
    return jnp.concatenate([first, block[:, 128:], last], axis=1)


def slots_kernel(
    meta,
    tile_hbm,
    right_a_hbm,
    right_b_hbm,
    lower_a_hbm,
    lower_b_hbm,
    lower_c_hbm,
    corner_a_hbm,
    corner_up_a_hbm,
    corner_up_b_hbm,
    corner_side_hbm,
    amps_hbm,
    pupil_hbm,
    mat_hi_hbm,
    mat_lo_hbm,
    mat_t_hi_hbm,
    mat_t_lo_hbm,
    own_out,
    right_out,
    lower_a_out,
    lower_b_out,
    lower_c_out,
    corner_a_out,
    corner_b_out,
    dpup_out,
    region,
    grads,
    win,
    left_hi,
    left_lo,
    right_hi,
    right_lo,
    cols_f32,
    rows_f32,
    dwin,
    dpup,
    amps,
    pupil,
    mat_hi,
    mat_lo,
    mat_t_hi,
    mat_t_lo,
    in_sems,
    slot_sems,
    out_sems,
):
    side = pupil.shape[-1]
    short = side // RADIX
    tile_rows, tile_cols = tile_hbm.shape[1:]
    slots = amps_hbm.shape[0]
    lanes = 128
    wide = side + lanes
    half = side // 2
    top, bottom = pl.ds(0, tile_rows), pl.ds(tile_rows, side)

    def copy_in(src, row_range, start, sem):
        dst = region.at[:, row_range, pl.ds(start, src.shape[-1])]
        return pltpu.make_async_copy(src, dst, in_sems.at[sem])

    loads = [
        copy_in(tile_hbm, top, 0, 0),
        copy_in(right_a_hbm, top, tile_cols, 1),
        copy_in(right_b_hbm, top, tile_cols + half, 2),
        copy_in(lower_a_hbm, bottom, 0, 3),
        copy_in(lower_b_hbm, bottom, half, 4),
        copy_in(lower_c_hbm, bottom, side, 5),
        copy_in(corner_a_hbm, bottom, tile_cols, 6),
    ]
    for load in loads:
        load.start()
    from_side = copy_in(corner_side_hbm, bottom, tile_cols + half, 7)
    from_below_a = copy_in(corner_up_a_hbm, bottom, tile_cols + half, 7)
    from_below_b = copy_in(corner_up_b_hbm, bottom, tile_cols + half + half // 2, 7)
    odd = meta[slots, 0]
    pl.when(odd == 1)(from_side.start)

    @pl.when(odd != 1)
    def _():
        from_below_a.start()
        from_below_b.start()

    loads.append(from_side)
    late = (
        (mat_hi_hbm, mat_hi),
        (mat_lo_hbm, mat_lo),
        (mat_t_hi_hbm, mat_t_hi),
        (mat_t_lo_hbm, mat_t_lo),
    )
    late_loads = [
        pltpu.make_async_copy(src, dst, in_sems.at[8 + n]) for n, (src, dst) in enumerate(late)
    ]
    for load in late_loads:
        load.start()
    count = meta[0, 2]
    for slot in range(1, slots):
        count = count + meta[slot, 2]

    def slot_loads(slot):
        return (
            pltpu.make_async_copy(pupil_hbm.at[slot], pupil.at[slot], slot_sems.at[0, slot]),
            pltpu.make_async_copy(amps_hbm.at[slot], amps.at[slot], slot_sems.at[1, slot]),
        )

    @pl.loop(0, count)
    def _(slot):
        for load in slot_loads(slot):
            load.start()

    outs = (
        (corner_a_out, bottom, tile_cols),
        (corner_b_out, bottom, tile_cols + half),
        (lower_a_out, bottom, 0),
        (lower_b_out, bottom, half),
        (lower_c_out, bottom, side),
        (right_out, top, tile_cols),
        (own_out, top, 0),
    )
    stores = [
        pltpu.make_async_copy(
            grads.at[:, rows, pl.ds(start, dst.shape[-1])], dst, out_sems.at[n]
        )
        for n, (dst, rows, start) in enumerate(outs)
    ]
    dpup_store = pltpu.make_async_copy(dpup, dpup_out, out_sems.at[7])
    lower_stores = stores[:5]
    upper_stores = stores[5:]

    zero_rows = 16

    @pl.loop(0, grads.shape[1] // zero_rows)
    def _(step):
        rows = pl.ds(pl.multiple_of(step * zero_rows, zero_rows), zero_rows)
        grads[:, rows, :] = jnp.zeros((2, zero_rows, grads.shape[2]), jnp.float32)

    @pl.loop(0, side // zero_rows)
    def _(step):
        rows = pl.ds(pl.multiple_of(step * zero_rows, zero_rows), zero_rows)
        dpup[:, rows, :] = jnp.zeros((2, zero_rows, side), jnp.float32)

    for load in loads:
        load.wait()

    def one_slot(slot):
        row = meta[slot, 0]
        col = meta[slot, 1]
        col_base = pl.multiple_of((col // lanes) * lanes, lanes)
        col_shift = col - col_base
        row_base = pl.multiple_of((row // 8) * 8, 8)
        row_shift = row - row_base

        @pl.loop(0, side // 32, unroll=2)
        def _(step):
            base = pl.multiple_of(step * 32, 32)
            rows = pl.ds(pl.multiple_of(row_base + base, 8), 32)
            for plane in range(2):
                block = region[plane, rows, pl.ds(col_base, wide)]
                win[plane, pl.ds(base, 32), :] = wrap_lanes(block, col_shift)

        first_keep = lax.broadcasted_iota(jnp.int32, (8, side), 0) >= row_shift
        last_rows = pl.ds(pl.multiple_of(row_base + side, 8), 8)
        for plane in range(2):
            block = region[plane, last_rows, pl.ds(col_base, wide)]
            block = wrap_lanes(block, col_shift)
            win[plane, :8, :] = jnp.where(first_keep, win[plane, :8, :], block)

        pupil_load, amps_load = slot_loads(slot)
        pupil_load.wait()

        @pl.when(slot == 0)
        def _():
            for load in late_loads:
                load.wait()

        for start in (0, half):
            for base in range(0, short, 16):
                for col0 in range(start, start + half, short):
                    cols = pl.ds(col0, short)
                    values = []
                    for q in range(RADIX):
                        rows = pl.ds(base + q * short, 16)
                        wr, wi = win[0, rows, cols], win[1, rows, cols]
                        pr, pi = pupil[slot, 0, rows, cols], pupil[slot, 1, rows, cols]
                        values.append((wr * pr - wi * pi, wr * pi + wi * pr))
                    for p, (re, im) in enumerate(butterfly(values, 1)):
                        for offset, value in ((0, re), (short, im)):
                            hi, lo = split(value)
                            rows = pl.ds(base + offset, 16)
                            left_hi[p, rows, cols] = hi
                            left_lo[p, rows, cols] = lo
            cols = pl.ds(start, half)
            for p in range(RADIX):
                rows_f32[p, :, cols] = left_dot(
                    mat_hi[p], mat_lo[p], left_hi[p, :, cols], left_lo[p, :, cols]
                )

        for p in range(RADIX):
            for base in range(0, short, 16):
                values = []
                for q in range(RADIX):
                    cols = pl.ds(q * short, short)
                    values.append(
                        (
                            rows_f32[p, pl.ds(base, 16), cols],
                            rows_f32[p, pl.ds(base + short, 16), cols],
                        )
                    )
                for t, (re, im) in enumerate(butterfly(values, 1)):
                    for offset, value in ((0, re), (short, im)):
                        hi, lo = split(value)
                        rows = pl.ds(base + p * short, 16)
                        right_hi[t, rows, pl.ds(offset, short)] = hi
                        right_lo[t, rows, pl.ds(offset, short)] = lo

        amps_load.wait()

        for t in range(RADIX):
            for start in (0, half):
                rows = pl.ds(start, half)
                field = right_dot(
                    right_hi[t, rows, :], right_lo[t, rows, :], mat_t_hi[t], mat_t_lo[t]
                )
                fre, fim = field[:, :short], field[:, short:]
                measured = amps[slot, rows, pl.ds(t * short, short)]
                factor = 1.0 - measured * lax.rsqrt(fre * fre + fim * fim + 1.0)
                residual = jnp.concatenate([factor * fre, factor * fim], axis=1)
                hi, lo = split(residual)
                cols_f32[t, rows, :] = right_dot(hi, lo, mat_hi[t], mat_lo[t])

        for p in range(RADIX):
            for base in range(0, short, 16):
                rows = pl.ds(base + p * short, 16)
                values = [
                    (cols_f32[t, rows, pl.ds(0, short)], cols_f32[t, rows, pl.ds(short, short)])
                    for t in range(RADIX)
                ]
                for q, (re, im) in enumerate(butterfly(values, -1)):
                    cols = pl.ds(q * short, short)
                    for offset, value in ((0, re), (short, im)):
                        hi, lo = split(value)
                        left_hi[p, pl.ds(base + offset, 16), cols] = hi
                        left_lo[p, pl.ds(base + offset, 16), cols] = lo

        for start in (0, half):
            cols = pl.ds(start, half)
            for p in range(RADIX):
                rows_f32[p, :, cols] = left_dot(
                    mat_t_hi[p], mat_t_lo[p], left_hi[p, :, cols], left_lo[p, :, cols]
                )
            for base in range(0, short, 8):
                for col0 in range(start, start + half, short):
                    cols = pl.ds(col0, short)
                    values = [
                        (
                            rows_f32[p, pl.ds(base, 8), cols],
                            rows_f32[p, pl.ds(base + short, 8), cols],
                        )
                        for p in range(RADIX)
                    ]
                    for q, (re, im) in enumerate(butterfly(values, -1)):
                        rows = pl.ds(base + q * short, 8)
                        pr, pi = pupil[slot, 0, rows, cols], pupil[slot, 1, rows, cols]
                        dwin[0, rows, cols] = pr * re + pi * im
                        dwin[1, rows, cols] = pr * im - pi * re
                        wr, wi = win[0, rows, cols], win[1, rows, cols]
                        win[0, rows, cols] = wr * re + wi * im
                        win[1, rows, cols] = wr * im - wi * re

        @pl.loop(0, side // 32, unroll=2)
        def _(step):
            base = pl.multiple_of(step * 32, 32)
            after = pl.multiple_of((base + 32) % side, 8)
            for plane in range(2):
                tiles = [win[plane, pl.ds(base + 8 * i, 8), :] for i in range(4)]
                tiles.append(win[plane, pl.ds(after, 8), :])
                for i, tile in enumerate(shift_back(tiles, row_shift, col_shift)):
                    dpup[plane, pl.ds(base + 8 * i, 8), :] += tile

        last = slot == count - 1
        pl.when(last)(dpup_store.start)

        zero = jnp.zeros((8, side), jnp.float32)
        for plane in range(2):
            block = dwin[plane, :8, :]
            dwin[plane, :8, :] = jnp.where(first_keep, block, zero)
            dwin[plane, pl.ds(side, 8), :] = jnp.where(first_keep, zero, block)

        def place(step):
            base = pl.multiple_of(step * 40, 8)
            rows = pl.ds(pl.multiple_of(row_base + base, 8), 40)
            for plane in range(2):
                block = unwrap_lanes(dwin[plane, pl.ds(base, 40), :], col_shift)
                target = (plane, rows, pl.ds(col_base, wide))
                grads[target] = grads[target] + block

        steps = (side + 8) // 40
        above = (tile_rows - row_base) // 40
        pl.loop(above, steps)(place)

        @pl.when(last)
        def _():
            for store in lower_stores:
                store.start()

        pl.loop(0, above)(place)

    pl.loop(0, count)(one_slot)

    @pl.when(count == 0)
    def _():
        for store in [dpup_store] + lower_stores:
            store.start()
        for load in late_loads:
            load.wait()

    for store in upper_stores:
        store.start()
    for store in [dpup_store] + stores:
        store.wait()


def slots_call(meta, tile, parts, amps, pupils):
    side = pupils.shape[-1]
    short = side // RADIX
    slots = amps.shape[0]
    tile_rows, tile_cols = tile.shape[1:]
    high, low = dft_blocks(side)
    tables = [jnp.asarray(x) for x in (high, low, high.transpose(0, 2, 1), low.transpose(0, 2, 1))]
    anywhere = pl.BlockSpec(memory_space=pl.ANY)
    f32, bf16 = jnp.float32, jnp.bfloat16
    region = (2, tile_rows + side, tile_cols + side)
    lower_a, lower_b, lower_c, corner_a = parts[2:6]
    right = jax.ShapeDtypeStruct((2, tile_rows, side), f32)
    dpup = jax.ShapeDtypeStruct(pupils.shape[1:], f32)
    outs = (tile, right, lower_a, lower_b, lower_c, corner_a, corner_a, dpup)
    table = pltpu.VMEM(high.shape, bf16)
    return pl.pallas_call(
        slots_kernel,
        out_shape=[jax.ShapeDtypeStruct(x.shape, f32) for x in outs],
        in_specs=[pl.BlockSpec(memory_space=pltpu.SMEM)] + [anywhere] * (len(parts) + 7),
        out_specs=[anywhere] * len(outs),
        scratch_shapes=[
            pltpu.VMEM(region, f32),
            pltpu.VMEM(region, f32),
            pltpu.VMEM((2, side, side), f32),
            pltpu.VMEM((RADIX, 2 * short, side), bf16),
            pltpu.VMEM((RADIX, 2 * short, side), bf16),
            pltpu.VMEM((RADIX, side, 2 * short), bf16),
            pltpu.VMEM((RADIX, side, 2 * short), bf16),
            pltpu.VMEM((RADIX, side, 2 * short), f32),
            pltpu.VMEM((RADIX, 2 * short, side), f32),
            pltpu.VMEM((2, side + 8, side), f32),
            pltpu.VMEM((2, side, side), f32),
            pltpu.VMEM(amps.shape, f32),
            pltpu.VMEM(pupils.shape, f32),
            table,
            table,
            table,
            table,
            pltpu.SemaphoreType.DMA((12,)),
            pltpu.SemaphoreType.DMA((2, slots)),
            pltpu.SemaphoreType.DMA((8,)),
        ],
        compiler_params=pltpu.CompilerParams(vmem_limit_bytes=56 * 1024 * 1024),
        cost_estimate=pl.CostEstimate(
            flops=slots * 48 * 2 * 4 * short * short * side,
            bytes_accessed=40 * 1024 * 1024,
            transcendentals=slots * side * side,
        ),
        name="slots",
    )(meta, tile, *parts, amps, pupils, *tables)


def exact_parts(value):
    hi, rest = split(value)
    rest = value - hi.astype(jnp.float32)
    return (hi, *split(rest))


def prepare_kernel(meta, amps, pupil, perm_rows, perm_cols, amps_out, pupil_out):
    value = sum(dot(part, perm_cols[...]) for part in exact_parts(amps[0]))
    amps_out[0] = sum(dot(perm_rows[...], part) for part in exact_parts(value))

    slot = pl.program_id(0)
    row_shift = meta[slot, 0] % 8
    col_shift = meta[slot, 1] % 128
    side = pupil.shape[-1]

    @pl.loop(0, side // 32, unroll=2)
    def _(step):
        base = pl.multiple_of(step * 32, 32)
        before = pl.multiple_of((base + side - 8) % side, 8)
        for plane in range(2):
            tiles = [pupil[plane, pl.ds(before, 8), :]]
            tiles += [pupil[plane, pl.ds(base + 8 * i, 8), :] for i in range(4)]
            for i, tile in enumerate(shift_on(tiles, row_shift, col_shift)):
                pupil_out[0, plane, pl.ds(base + 8 * i, 8), :] = tile


def prepare(meta, amps, pupil):
    slots, side, _ = amps.shape
    index = np.arange(side)
    perm = np.zeros((side, side), ml_dtypes.bfloat16)
    perm[index, (index % RADIX) * (side // RADIX) + index // RADIX] = 1
    block = pl.BlockSpec((1, side, side), lambda s: (s, 0, 0))
    table = pl.BlockSpec((side, side), lambda s: (0, 0))
    return pl.pallas_call(
        prepare_kernel,
        grid=(slots,),
        out_shape=[
            jax.ShapeDtypeStruct(amps.shape, amps.dtype),
            jax.ShapeDtypeStruct((slots, 2, side, side), pupil.dtype),
        ],
        in_specs=[
            pl.BlockSpec(memory_space=pltpu.SMEM),
            block,
            pl.BlockSpec((2, side, side), lambda s: (0, 0, 0)),
            table,
            table,
        ],
        out_specs=[block, pl.BlockSpec((1, 2, side, side), lambda s: (s, 0, 0, 0))],
        compiler_params=pltpu.CompilerParams(vmem_limit_bytes=32 * 1024 * 1024),
        cost_estimate=pl.CostEstimate(
            flops=slots * 12 * side**3, bytes_accessed=24 * slots * side**2, transcendentals=0
        ),
        name="prepare",
    )(meta, amps, pupil, jnp.asarray(perm.T), jnp.asarray(perm))


def along(axis_pairs, members):
    n_ty, n_tx = members
    pairs = []
    for i in range(n_ty):
        for j in range(n_tx):
            target = axis_pairs(i, j)
            if target is not None and 0 <= target[0] < n_ty and 0 <= target[1] < n_tx:
                pairs.append((i * n_tx + j, target[0] * n_tx + target[1]))
    return pairs


def send(array, rule):
    sizes = (lax.axis_size("ty"), lax.axis_size("tx"))
    return lax.ppermute(array, ("ty", "tx"), along(rule, sizes))


def halve(value, bit):
    rows = value.shape[0] // 2
    mine = lax.axis_index("ty") // bit % 2
    kept = lax.dynamic_slice_in_dim(value, mine * rows, rows, 0)
    sent = lax.dynamic_slice_in_dim(value, (1 - mine) * rows, rows, 0)
    received = lax.ppermute(sent, "ty", [(i, i ^ bit) for i in range(lax.axis_size("ty"))])
    return kept + received


def double(value, bit):
    mine = lax.axis_index("ty") // bit % 2
    other = lax.ppermute(value, "ty", [(i, i ^ bit) for i in range(lax.axis_size("ty"))])
    first = jnp.where(mine == 0, value, other)
    second = jnp.where(mine == 0, other, value)
    return jnp.concatenate([first, second], axis=0)


def stepped(value, axis, inner, step):
    size = lax.axis_size(axis)
    return lax.ppermute(value, axis, [(i, (i + step * inner) % size) for i in range(size)])


def scatter(value, axis, inner):
    members, own = lax.axis_size(axis) // inner, lax.axis_index(axis) // inner
    rows = value.shape[0] // members
    total = lax.dynamic_slice_in_dim(value, own * rows, rows, 0)
    for step in range(1, members):
        piece = lax.dynamic_slice_in_dim(value, (own + step) % members * rows, rows, 0)
        total = total + stepped(piece, axis, inner, step)
    return total


def gather(value, axis, inner):
    members, own = lax.axis_size(axis) // inner, lax.axis_index(axis) // inner
    rows = value.shape[0]
    parts = [value] + [stepped(value, axis, inner, step) for step in range(1, members)]
    out = jnp.zeros((members * rows,) + value.shape[1:], value.dtype)
    for step, part in enumerate(parts):
        out = lax.dynamic_update_slice_in_dim(out, part, (own - step) % members * rows, 0)
    return out


def sum_all(value, axis):
    parts = [value] + [stepped(value, axis, 1, step) for step in range(1, lax.axis_size(axis))]
    while len(parts) > 1:
        middle = len(parts) // 2
        parts = [a + b for a, b in zip(parts[:middle], parts[middle:])]
    return parts[0]


def after(value, *arrivals):
    return lax.optimization_barrier((value, *arrivals))[0]


def body(spectrum, pupil, amplitudes, offsets, live):
    side = pupil.shape[-1]
    half = side // 2
    tile_rows, tile_cols = spectrum.shape[1:]
    n_ty, n_tx = lax.axis_size("ty"), lax.axis_size("tx")
    own_ty, own_tx = lax.axis_index("ty"), lax.axis_index("tx")
    rows_local = offsets[:, 0] - own_ty * tile_rows
    cols_local = offsets[:, 1] - own_tx * tile_cols
    meta = jnp.stack([rows_local, cols_local, live], axis=1)
    meta = jnp.concatenate([meta, jnp.full((1, 3), own_ty % 2, jnp.int32)], axis=0)

    def left(i, j):
        return (i, j - 1)

    def up(i, j):
        return (i - 1, j)

    def up_odd(i, j):
        return (i - 1, j) if i % 2 else None

    lower_b = send(spectrum[:, :side, half:side], up)
    right_a = send(spectrum[:, :, :half], left)
    right_b = send(spectrum[:, :, half:side], left)
    lower_a = send(spectrum[:, :side, :half], up)
    lower_c = send(spectrum[:, :side, side:], up)
    amps, pupils = prepare(meta, amplitudes, pupil)
    lower_b, amps = lax.optimization_barrier((lower_b, amps))
    corner_side = send(lower_b, lambda i, j: (i, j - 1) if i % 2 else None)
    corner_a = send(right_a[:, :side], up)
    corner_up_a = send(right_b[:, :side, : half // 2], up_odd)
    corner_up_b = send(right_b[:, :side, half // 2 :], up_odd)

    parts = (
        right_a,
        right_b,
        lower_a,
        lower_b,
        lower_c,
        corner_a,
        corner_up_a,
        corner_up_b,
        corner_side,
    )
    own_g, right_g, lower_a_g, lower_b_g, lower_c_g, corner_a_g, corner_b_g, dpup = (
        slots_call(meta, spectrum, parts, amps, pupils)
    )

    def down(i, j):
        return (i + 1, j)

    def right(i, j):
        return (i, j + 1)

    part = halve(dpup.reshape(-1, side), 1)
    back_a = send(corner_a_g, down)
    back_side = send(corner_b_g, lambda i, j: (i, j + 1) if i % 2 else None)
    back_down = send(corner_b_g, lambda i, j: None if i % 2 else (i + 1, j))
    part, back_a, back_side, back_down = lax.optimization_barrier(
        (part, back_a, back_side, back_down)
    )
    part = scatter(part, "ty", 2)
    lower_a = send(after(lower_a_g, part), down)
    lower_c = send(after(lower_c_g, part), down)
    part = sum_all(part, "tx") * (1.0 / math.sqrt(n_ty * n_tx))
    right_g = right_g + jnp.concatenate([back_a, back_down], axis=2)
    right_back = send(after(right_g, part), right)
    part = gather(after(part, lower_a, lower_c), "ty", 2)
    lower_b = send(after(lower_b_g + back_side, part), down)
    spec_grad = own_g.at[:, :, side:].add(lower_c)
    spec_grad = spec_grad.at[:, :, :half].add(lower_a)
    part, spec_grad = lax.optimization_barrier((part, spec_grad))
    spec_grad = spec_grad.at[:, :, :side].add(right_back.at[:, :, half:].add(lower_b))
    return spec_grad, double(part, 1).reshape(pupil.shape)


def solution(mesh):
    return jax.shard_map(
        body,
        mesh=mesh,
        in_specs=(
            P(None, "ty", "tx"),
            P(),
            P(("ty", "tx"), None, None),
            P(("ty", "tx"), None),
            P(("ty", "tx")),
        ),
        out_specs=(P(None, "ty", "tx"), P()),
        check_vma=False,
    )
```

```python
import math

import jax
import jax.numpy as jnp
import ml_dtypes
import numpy as np
from jax import lax
from jax.experimental import pallas as pl
from jax.experimental.pallas import tpu as pltpu
from jax.sharding import PartitionSpec as P

RADIX = 4


def dft_blocks(length):
    short = length // RADIX
    out_idx = np.arange(short)[:, None]
    in_idx = np.arange(short)[None, :]
    blocks = []
    for p in range(RADIX):
        phase = (p * in_idx + RADIX * out_idx * in_idx) % length
        angle = phase * (2.0 * math.pi / length)
        cos = np.cos(angle) / math.sqrt(length)
        sin = np.sin(angle) / math.sqrt(length)
        blocks.append(np.block([[cos, -sin], [sin, cos]]))
    full = np.stack(blocks).astype(np.float32)
    high = full.astype(ml_dtypes.bfloat16)
    low = (full - high.astype(np.float32)).astype(ml_dtypes.bfloat16)
    return high, low


def split(value):
    high = value.astype(jnp.bfloat16)
    low = (value - high.astype(jnp.float32)).astype(jnp.bfloat16)
    return high, low


def dot(lhs, rhs):
    return jnp.dot(lhs, rhs, preferred_element_type=jnp.float32)


def left_dot(mat_hi, mat_lo, val_hi, val_lo):
    lhs = jnp.concatenate([mat_hi, mat_hi, mat_lo], axis=1)
    return dot(lhs, jnp.concatenate([val_hi, val_lo, val_hi], axis=0))


def right_dot(val_hi, val_lo, mat_hi, mat_lo):
    lhs = jnp.concatenate([val_hi, val_lo, val_hi], axis=1)
    return dot(lhs, jnp.concatenate([mat_hi, mat_hi, mat_lo], axis=0))


def butterfly(parts, sign):
    (r0, i0), (r1, i1), (r2, i2), (r3, i3) = parts
    sr, si, dr, di = r0 + r2, i0 + i2, r0 - r2, i0 - i2
    tr, ti, er, ei = r1 + r3, i1 + i3, r1 - r3, i1 - i3
    if sign < 0:
        er, ei = -er, -ei
    return [(sr + tr, si + ti), (dr - ei, di + er), (sr - tr, si - ti), (dr + ei, di - er)]


def row_index():
    return lax.broadcasted_iota(jnp.int32, (8, 128), 0)


def lane_index():
    return lax.broadcasted_iota(jnp.int32, (8, 128), 1)


def lane_tiles(tile):
    return [tile[:, i : i + 128] for i in range(0, tile.shape[1], 128)]


def rolled(tiles, amount, axis):
    return [[pltpu.roll(part, amount, axis) for part in tile] for tile in tiles]


def shift_on(tiles, row_shift, col_shift):
    keep = lane_index() >= col_shift
    tiles = rolled([lane_tiles(tile) for tile in tiles], col_shift, 1)
    tiles = [[jnp.where(keep, x, y) for x, y in zip(t, t[-1:] + t[:-1])] for t in tiles]
    keep = row_index() >= row_shift
    tiles = rolled(tiles, row_shift, 0)
    return [
        jnp.concatenate([jnp.where(keep, y, x) for x, y in zip(a, b)], axis=1)
        for a, b in zip(tiles, tiles[1:])
    ]


def shift_back(tiles, row_shift, col_shift):
    keep = lane_index() < 128 - col_shift
    tiles = rolled([lane_tiles(tile) for tile in tiles], (128 - col_shift) % 128, 1)
    tiles = [[jnp.where(keep, x, y) for x, y in zip(t, t[1:] + t[:1])] for t in tiles]
    keep = row_index() < 8 - row_shift
    tiles = rolled(tiles, (8 - row_shift) % 8, 0)
    return [
        jnp.concatenate([jnp.where(keep, x, y) for x, y in zip(a, b)], axis=1)
        for a, b in zip(tiles, tiles[1:])
    ]


def wrap_lanes(block, col_shift):
    rows = block.shape[0]
    keep = lax.broadcasted_iota(jnp.int32, (rows, 128), 1) >= col_shift
    first = jnp.where(keep, block[:, :128], block[:, -128:])
    return jnp.concatenate([first, block[:, 128:-128]], axis=1)


def unwrap_lanes(block, col_shift):
    rows = block.shape[0]
    keep = lax.broadcasted_iota(jnp.int32, (rows, 128), 1) >= col_shift
    zero = jnp.zeros((rows, 128), jnp.float32)
    first = jnp.where(keep, block[:, :128], zero)
    last = jnp.where(keep, zero, block[:, :128])
    return jnp.concatenate([first, block[:, 128:], last], axis=1)


def slots_kernel(
    meta,
    tile_hbm,
    right_a_hbm,
    right_b_hbm,
    lower_a_hbm,
    lower_b_hbm,
    lower_c_hbm,
    corner_a_hbm,
    corner_up_a_hbm,
    corner_up_b_hbm,
    corner_side_hbm,
    amps_hbm,
    pupil_hbm,
    mat_hi_hbm,
    mat_lo_hbm,
    mat_t_hi_hbm,
    mat_t_lo_hbm,
    own_out,
    right_a_out,
    right_b_out,
    lower_a_out,
    lower_b_out,
    lower_c_out,
    corner_a_out,
    corner_b_out,
    dpup_out,
    region,
    grads,
    win,
    left_hi,
    left_lo,
    right_hi,
    right_lo,
    cols_f32,
    rows_f32,
    dwin,
    dpup,
    amps,
    pupil,
    mat_hi,
    mat_lo,
    mat_t_hi,
    mat_t_lo,
    in_sems,
    slot_sems,
    out_sems,
):
    side = pupil.shape[-1]
    short = side // RADIX
    tile_rows, tile_cols = tile_hbm.shape[1:]
    slots = amps_hbm.shape[0]
    lanes = 128
    wide = side + lanes
    half = side // 2
    top, bottom = pl.ds(0, tile_rows), pl.ds(tile_rows, side)

    def copy_in(src, row_range, start, sem):
        dst = region.at[:, row_range, pl.ds(start, src.shape[-1])]
        return pltpu.make_async_copy(src, dst, in_sems.at[sem])

    loads = [
        copy_in(tile_hbm, top, 0, 0),
        copy_in(right_a_hbm, top, tile_cols, 1),
        copy_in(right_b_hbm, top, tile_cols + half, 2),
        copy_in(lower_a_hbm, bottom, 0, 3),
        copy_in(lower_b_hbm, bottom, half, 4),
        copy_in(lower_c_hbm, bottom, side, 5),
        copy_in(corner_a_hbm, bottom, tile_cols, 6),
    ]
    for load in loads:
        load.start()
    from_side = copy_in(corner_side_hbm, bottom, tile_cols + half, 7)
    from_below_a = copy_in(corner_up_a_hbm, bottom, tile_cols + half, 7)
    from_below_b = copy_in(corner_up_b_hbm, bottom, tile_cols + half + half // 2, 7)
    odd = meta[slots, 0]
    pl.when(odd == 1)(from_side.start)

    @pl.when(odd != 1)
    def _():
        from_below_a.start()
        from_below_b.start()

    loads.append(from_side)
    late = (
        (mat_hi_hbm, mat_hi),
        (mat_lo_hbm, mat_lo),
        (mat_t_hi_hbm, mat_t_hi),
        (mat_t_lo_hbm, mat_t_lo),
    )
    late_loads = [
        pltpu.make_async_copy(src, dst, in_sems.at[8 + n]) for n, (src, dst) in enumerate(late)
    ]
    for load in late_loads:
        load.start()
    count = meta[0, 2]
    for slot in range(1, slots):
        count = count + meta[slot, 2]

    def slot_loads(slot):
        return (
            pltpu.make_async_copy(pupil_hbm.at[slot], pupil.at[slot], slot_sems.at[0, slot]),
            pltpu.make_async_copy(amps_hbm.at[slot], amps.at[slot], slot_sems.at[1, slot]),
        )

    @pl.loop(0, count)
    def _(slot):
        for load in slot_loads(slot):
            load.start()

    outs = (
        (corner_a_out, bottom, tile_cols),
        (corner_b_out, bottom, tile_cols + half),
        (lower_a_out, bottom, 0),
        (lower_b_out, bottom, half),
        (lower_c_out, bottom, side),
        (right_a_out, top, tile_cols),
        (right_b_out, top, tile_cols + half),
        (own_out, top, 0),
    )
    stores = [
        pltpu.make_async_copy(
            grads.at[:, rows, pl.ds(start, dst.shape[-1])], dst, out_sems.at[n]
        )
        for n, (dst, rows, start) in enumerate(outs)
    ]
    dpup_store = pltpu.make_async_copy(dpup, dpup_out, out_sems.at[8])
    lower_stores = stores[:5]
    upper_stores = stores[5:]

    zero_rows = 16

    @pl.loop(0, grads.shape[1] // zero_rows)
    def _(step):
        rows = pl.ds(pl.multiple_of(step * zero_rows, zero_rows), zero_rows)
        grads[:, rows, :] = jnp.zeros((2, zero_rows, grads.shape[2]), jnp.float32)

    @pl.loop(0, side // zero_rows)
    def _(step):
        rows = pl.ds(pl.multiple_of(step * zero_rows, zero_rows), zero_rows)
        dpup[:, rows, :] = jnp.zeros((2, zero_rows, side), jnp.float32)

    def one_slot(slot):
        row = meta[slot, 0]
        col = meta[slot, 1]
        col_base = pl.multiple_of((col // lanes) * lanes, lanes)
        col_shift = col - col_base
        row_base = pl.multiple_of((row // 8) * 8, 8)
        row_shift = row - row_base

        def cut(step):
            base = pl.multiple_of(step * 32, 32)
            rows = pl.ds(pl.multiple_of(row_base + base, 8), 32)
            for plane in range(2):
                block = region[plane, rows, pl.ds(col_base, wide)]
                win[plane, pl.ds(base, 32), :] = wrap_lanes(block, col_shift)

        above = (tile_rows - row_base) // 32

        @pl.when(slot == 0)
        def _():
            for load in loads[:3]:
                load.wait()

        pl.loop(0, above)(cut)

        @pl.when(slot == 0)
        def _():
            for load in loads[3:]:
                load.wait()

        pl.loop(above, side // 32)(cut)

        first_keep = lax.broadcasted_iota(jnp.int32, (8, side), 0) >= row_shift
        last_rows = pl.ds(pl.multiple_of(row_base + side, 8), 8)
        for plane in range(2):
            block = region[plane, last_rows, pl.ds(col_base, wide)]
            block = wrap_lanes(block, col_shift)
            win[plane, :8, :] = jnp.where(first_keep, win[plane, :8, :], block)

        pupil_load, amps_load = slot_loads(slot)
        pupil_load.wait()

        @pl.when(slot == 0)
        def _():
            for load in late_loads:
                load.wait()

        for start in (0, half):
            for base in range(0, short, 16):
                for col0 in range(start, start + half, short):
                    cols = pl.ds(col0, short)
                    values = []
                    for q in range(RADIX):
                        rows = pl.ds(base + q * short, 16)
                        wr, wi = win[0, rows, cols], win[1, rows, cols]
                        pr, pi = pupil[slot, 0, rows, cols], pupil[slot, 1, rows, cols]
                        values.append((wr * pr - wi * pi, wr * pi + wi * pr))
                    for p, (re, im) in enumerate(butterfly(values, 1)):
                        for offset, value in ((0, re), (short, im)):
                            hi, lo = split(value)
                            rows = pl.ds(base + offset, 16)
                            left_hi[p, rows, cols] = hi
                            left_lo[p, rows, cols] = lo
            cols = pl.ds(start, half)
            for p in range(RADIX):
                rows_f32[p, :, cols] = left_dot(
                    mat_hi[p], mat_lo[p], left_hi[p, :, cols], left_lo[p, :, cols]
                )

        for p in range(RADIX):
            for base in range(0, short, 16):
                values = []
                for q in range(RADIX):
                    cols = pl.ds(q * short, short)
                    values.append(
                        (
                            rows_f32[p, pl.ds(base, 16), cols],
                            rows_f32[p, pl.ds(base + short, 16), cols],
                        )
                    )
                for t, (re, im) in enumerate(butterfly(values, 1)):
                    for offset, value in ((0, re), (short, im)):
                        hi, lo = split(value)
                        rows = pl.ds(base + p * short, 16)
                        right_hi[t, rows, pl.ds(offset, short)] = hi
                        right_lo[t, rows, pl.ds(offset, short)] = lo

        amps_load.wait()

        for t in range(RADIX):
            for start in (0, half):
                rows = pl.ds(start, half)
                field = right_dot(
                    right_hi[t, rows, :], right_lo[t, rows, :], mat_t_hi[t], mat_t_lo[t]
                )
                fre, fim = field[:, :short], field[:, short:]
                measured = amps[slot, rows, pl.ds(t * short, short)]
                factor = 1.0 - measured * lax.rsqrt(fre * fre + fim * fim + 1.0)
                residual = jnp.concatenate([factor * fre, factor * fim], axis=1)
                hi, lo = split(residual)
                cols_f32[t, rows, :] = right_dot(hi, lo, mat_hi[t], mat_lo[t])

        for p in range(RADIX):
            for base in range(0, short, 16):
                rows = pl.ds(base + p * short, 16)
                values = [
                    (cols_f32[t, rows, pl.ds(0, short)], cols_f32[t, rows, pl.ds(short, short)])
                    for t in range(RADIX)
                ]
                for q, (re, im) in enumerate(butterfly(values, -1)):
                    cols = pl.ds(q * short, short)
                    for offset, value in ((0, re), (short, im)):
                        hi, lo = split(value)
                        left_hi[p, pl.ds(base + offset, 16), cols] = hi
                        left_lo[p, pl.ds(base + offset, 16), cols] = lo

        for start in (0, half):
            cols = pl.ds(start, half)
            for p in range(RADIX):
                rows_f32[p, :, cols] = left_dot(
                    mat_t_hi[p], mat_t_lo[p], left_hi[p, :, cols], left_lo[p, :, cols]
                )
            for base in range(0, short, 8):
                for col0 in range(start, start + half, short):
                    cols = pl.ds(col0, short)
                    values = [
                        (
                            rows_f32[p, pl.ds(base, 8), cols],
                            rows_f32[p, pl.ds(base + short, 8), cols],
                        )
                        for p in range(RADIX)
                    ]
                    for q, (re, im) in enumerate(butterfly(values, -1)):
                        rows = pl.ds(base + q * short, 8)
                        pr, pi = pupil[slot, 0, rows, cols], pupil[slot, 1, rows, cols]
                        dwin[0, rows, cols] = pr * re + pi * im
                        dwin[1, rows, cols] = pr * im - pi * re
                        wr, wi = win[0, rows, cols], win[1, rows, cols]
                        win[0, rows, cols] = wr * re + wi * im
                        win[1, rows, cols] = wr * im - wi * re

        @pl.loop(0, side // 32, unroll=2)
        def _(step):
            base = pl.multiple_of(step * 32, 32)
            after = pl.multiple_of((base + 32) % side, 8)
            for plane in range(2):
                tiles = [win[plane, pl.ds(base + 8 * i, 8), :] for i in range(4)]
                tiles.append(win[plane, pl.ds(after, 8), :])
                for i, tile in enumerate(shift_back(tiles, row_shift, col_shift)):
                    dpup[plane, pl.ds(base + 8 * i, 8), :] += tile

        last = slot == count - 1
        pl.when(last)(dpup_store.start)

        zero = jnp.zeros((8, side), jnp.float32)
        for plane in range(2):
            block = dwin[plane, :8, :]
            dwin[plane, :8, :] = jnp.where(first_keep, block, zero)
            dwin[plane, pl.ds(side, 8), :] = jnp.where(first_keep, zero, block)

        def place(step):
            base = pl.multiple_of(step * 40, 8)
            rows = pl.ds(pl.multiple_of(row_base + base, 8), 40)
            for plane in range(2):
                block = unwrap_lanes(dwin[plane, pl.ds(base, 40), :], col_shift)
                target = (plane, rows, pl.ds(col_base, wide))
                grads[target] = grads[target] + block

        steps = (side + 8) // 40
        above = (tile_rows - row_base) // 40
        pl.loop(above, steps)(place)

        @pl.when(last)
        def _():
            for store in lower_stores:
                store.start()

        pl.loop(0, above)(place)

    pl.loop(0, count)(one_slot)

    @pl.when(count == 0)
    def _():
        for store in [dpup_store] + lower_stores:
            store.start()
        for load in loads + late_loads:
            load.wait()

    for store in upper_stores:
        store.start()
    for store in [dpup_store] + stores:
        store.wait()


def slots_call(meta, tile, parts, amps, pupils):
    side = pupils.shape[-1]
    short = side // RADIX
    slots = amps.shape[0]
    tile_rows, tile_cols = tile.shape[1:]
    high, low = dft_blocks(side)
    tables = [jnp.asarray(x) for x in (high, low, high.transpose(0, 2, 1), low.transpose(0, 2, 1))]
    anywhere = pl.BlockSpec(memory_space=pl.ANY)
    f32, bf16 = jnp.float32, jnp.bfloat16
    region = (2, tile_rows + side, tile_cols + side)
    right_a, right_b, lower_a, lower_b, lower_c, corner_a = parts[:6]
    dpup = jax.ShapeDtypeStruct(pupils.shape[1:], f32)
    outs = (tile, right_a, right_b, lower_a, lower_b, lower_c, corner_a, corner_a, dpup)
    table = pltpu.VMEM(high.shape, bf16)
    return pl.pallas_call(
        slots_kernel,
        out_shape=[jax.ShapeDtypeStruct(x.shape, f32) for x in outs],
        in_specs=[pl.BlockSpec(memory_space=pltpu.SMEM)] + [anywhere] * (len(parts) + 7),
        out_specs=[anywhere] * len(outs),
        scratch_shapes=[
            pltpu.VMEM(region, f32),
            pltpu.VMEM(region, f32),
            pltpu.VMEM((2, side, side), f32),
            pltpu.VMEM((RADIX, 2 * short, side), bf16),
            pltpu.VMEM((RADIX, 2 * short, side), bf16),
            pltpu.VMEM((RADIX, side, 2 * short), bf16),
            pltpu.VMEM((RADIX, side, 2 * short), bf16),
            pltpu.VMEM((RADIX, side, 2 * short), f32),
            pltpu.VMEM((RADIX, 2 * short, side), f32),
            pltpu.VMEM((2, side + 8, side), f32),
            pltpu.VMEM((2, side, side), f32),
            pltpu.VMEM(amps.shape, f32),
            pltpu.VMEM(pupils.shape, f32),
            table,
            table,
            table,
            table,
            pltpu.SemaphoreType.DMA((12,)),
            pltpu.SemaphoreType.DMA((2, slots)),
            pltpu.SemaphoreType.DMA((9,)),
        ],
        compiler_params=pltpu.CompilerParams(vmem_limit_bytes=56 * 1024 * 1024),
        cost_estimate=pl.CostEstimate(
            flops=slots * 48 * 2 * 4 * short * short * side,
            bytes_accessed=40 * 1024 * 1024,
            transcendentals=slots * side * side,
        ),
        name="slots",
    )(meta, tile, *parts, amps, pupils, *tables)


def exact_parts(value):
    hi, rest = split(value)
    rest = value - hi.astype(jnp.float32)
    return (hi, *split(rest))


def prepare_kernel(meta, amps, pupil, perm_rows, perm_cols, amps_out, pupil_out):
    value = sum(dot(part, perm_cols[...]) for part in exact_parts(amps[0]))
    amps_out[0] = sum(dot(perm_rows[...], part) for part in exact_parts(value))

    slot = pl.program_id(0)
    row_shift = meta[slot, 0] % 8
    col_shift = meta[slot, 1] % 128
    side = pupil.shape[-1]

    @pl.loop(0, side // 32, unroll=2)
    def _(step):
        base = pl.multiple_of(step * 32, 32)
        before = pl.multiple_of((base + side - 8) % side, 8)
        for plane in range(2):
            tiles = [pupil[plane, pl.ds(before, 8), :]]
            tiles += [pupil[plane, pl.ds(base + 8 * i, 8), :] for i in range(4)]
            for i, tile in enumerate(shift_on(tiles, row_shift, col_shift)):
                pupil_out[0, plane, pl.ds(base + 8 * i, 8), :] = tile


def prepare(meta, amps, pupil):
    slots, side, _ = amps.shape
    index = np.arange(side)
    perm = np.zeros((side, side), ml_dtypes.bfloat16)
    perm[index, (index % RADIX) * (side // RADIX) + index // RADIX] = 1
    block = pl.BlockSpec((1, side, side), lambda s: (s, 0, 0))
    table = pl.BlockSpec((side, side), lambda s: (0, 0))
    return pl.pallas_call(
        prepare_kernel,
        grid=(slots,),
        out_shape=[
            jax.ShapeDtypeStruct(amps.shape, amps.dtype),
            jax.ShapeDtypeStruct((slots, 2, side, side), pupil.dtype),
        ],
        in_specs=[
            pl.BlockSpec(memory_space=pltpu.SMEM),
            block,
            pl.BlockSpec((2, side, side), lambda s: (0, 0, 0)),
            table,
            table,
        ],
        out_specs=[block, pl.BlockSpec((1, 2, side, side), lambda s: (s, 0, 0, 0))],
        compiler_params=pltpu.CompilerParams(vmem_limit_bytes=32 * 1024 * 1024),
        cost_estimate=pl.CostEstimate(
            flops=slots * 12 * side**3, bytes_accessed=24 * slots * side**2, transcendentals=0
        ),
        name="prepare",
    )(meta, amps, pupil, jnp.asarray(perm.T), jnp.asarray(perm))


def along(axis_pairs, members):
    n_ty, n_tx = members
    pairs = []
    for i in range(n_ty):
        for j in range(n_tx):
            target = axis_pairs(i, j)
            if target is not None and 0 <= target[0] < n_ty and 0 <= target[1] < n_tx:
                pairs.append((i * n_tx + j, target[0] * n_tx + target[1]))
    return pairs


def send(array, rule):
    sizes = (lax.axis_size("ty"), lax.axis_size("tx"))
    return lax.ppermute(array, ("ty", "tx"), along(rule, sizes))


def halve(value, bit):
    rows = value.shape[0] // 2
    mine = lax.axis_index("ty") // bit % 2
    kept = lax.dynamic_slice_in_dim(value, mine * rows, rows, 0)
    sent = lax.dynamic_slice_in_dim(value, (1 - mine) * rows, rows, 0)
    received = lax.ppermute(sent, "ty", [(i, i ^ bit) for i in range(lax.axis_size("ty"))])
    return kept + received


def double(value, bit):
    mine = lax.axis_index("ty") // bit % 2
    other = lax.ppermute(value, "ty", [(i, i ^ bit) for i in range(lax.axis_size("ty"))])
    first = jnp.where(mine == 0, value, other)
    second = jnp.where(mine == 0, other, value)
    return jnp.concatenate([first, second], axis=0)


def stepped(value, axis, inner, step):
    size = lax.axis_size(axis)
    return lax.ppermute(value, axis, [(i, (i + step * inner) % size) for i in range(size)])


def scatter(value, axis, inner):
    members, own = lax.axis_size(axis) // inner, lax.axis_index(axis) // inner
    rows = value.shape[0] // members
    total = lax.dynamic_slice_in_dim(value, own * rows, rows, 0)
    for step in range(1, members):
        piece = lax.dynamic_slice_in_dim(value, (own + step) % members * rows, rows, 0)
        total = total + stepped(piece, axis, inner, step)
    return total


def gather(value, axis, inner):
    members, own = lax.axis_size(axis) // inner, lax.axis_index(axis) // inner
    rows = value.shape[0]
    parts = [value] + [stepped(value, axis, inner, step) for step in range(1, members)]
    out = jnp.zeros((members * rows,) + value.shape[1:], value.dtype)
    for step, part in enumerate(parts):
        out = lax.dynamic_update_slice_in_dim(out, part, (own - step) % members * rows, 0)
    return out


def sum_all(value, axis):
    parts = [value] + [stepped(value, axis, 1, step) for step in range(1, lax.axis_size(axis))]
    while len(parts) > 1:
        middle = len(parts) // 2
        parts = [a + b for a, b in zip(parts[:middle], parts[middle:])]
    return parts[0]


def after(value, *arrivals):
    return lax.optimization_barrier((value, *arrivals))[0]


def body(spectrum, pupil, amplitudes, offsets, live):
    side = pupil.shape[-1]
    half = side // 2
    tile_rows, tile_cols = spectrum.shape[1:]
    n_ty, n_tx = lax.axis_size("ty"), lax.axis_size("tx")
    own_ty, own_tx = lax.axis_index("ty"), lax.axis_index("tx")
    rows_local = offsets[:, 0] - own_ty * tile_rows
    cols_local = offsets[:, 1] - own_tx * tile_cols
    meta = jnp.stack([rows_local, cols_local, live], axis=1)
    meta = jnp.concatenate([meta, jnp.full((1, 3), own_ty % 2, jnp.int32)], axis=0)

    def left(i, j):
        return (i, j - 1)

    def up(i, j):
        return (i - 1, j)

    def up_odd(i, j):
        return (i - 1, j) if i % 2 else None

    lower_b = send(spectrum[:, :side, half:side], up)
    right_a = send(spectrum[:, :, :half], left)
    right_b = send(spectrum[:, :, half:side], left)
    lower_a = send(spectrum[:, :side, :half], up)
    lower_c = send(spectrum[:, :side, side:], up)
    amps, pupils = prepare(meta, amplitudes, pupil)
    lower_b, amps = lax.optimization_barrier((lower_b, amps))
    corner_side = send(lower_b, lambda i, j: (i, j - 1) if i % 2 else None)
    corner_a = send(right_a[:, :side], up)
    corner_up_a = send(right_b[:, :side, : half // 2], up_odd)
    corner_up_b = send(right_b[:, :side, half // 2 :], up_odd)

    parts = (
        right_a,
        right_b,
        lower_a,
        lower_b,
        lower_c,
        corner_a,
        corner_up_a,
        corner_up_b,
        corner_side,
    )
    own_g, right_a_g, right_b_g, lower_a_g, lower_b_g, lower_c_g, corner_a_g, corner_b_g, dpup = (
        slots_call(meta, spectrum, parts, amps, pupils)
    )

    def down(i, j):
        return (i + 1, j)

    def right(i, j):
        return (i, j + 1)

    part = halve(dpup.reshape(-1, side), 1)
    back_a = send(corner_a_g, down)
    back_side = send(corner_b_g, lambda i, j: (i, j + 1) if i % 2 else None)
    back_down = send(corner_b_g, lambda i, j: None if i % 2 else (i + 1, j))
    part = scatter(part, "ty", 2)
    lower_a = send(after(lower_a_g, part), down)
    lower_c = send(after(lower_c_g, part), down)
    part, back_a, back_side, back_down = lax.optimization_barrier(
        (part, back_a, back_side, back_down)
    )
    part = sum_all(part, "tx") * (1.0 / math.sqrt(n_ty * n_tx))
    right_a = send(after(right_a_g + back_a, part), right)
    right_b = send(after(right_b_g + back_down, part), right)
    part = gather(after(part, lower_a, lower_c), "ty", 2)
    lower_b = send(after(lower_b_g + back_side, part), down)
    spec_grad = own_g.at[:, :, side:].add(lower_c)
    spec_grad = spec_grad.at[:, :, :half].add(lower_a + right_a)
    part, spec_grad = lax.optimization_barrier((part, spec_grad))
    spec_grad = spec_grad.at[:, :, half:side].add(lower_b + right_b)
    return spec_grad, double(part, 1).reshape(pupil.shape)


def solution(mesh):
    return jax.shard_map(
        body,
        mesh=mesh,
        in_specs=(
            P(None, "ty", "tx"),
            P(),
            P(("ty", "tx"), None, None),
            P(("ty", "tx"), None),
            P(("ty", "tx")),
        ),
        out_specs=(P(None, "ty", "tx"), P()),
        check_vma=False,
    )
```

```python
import math

import jax
import jax.numpy as jnp
import ml_dtypes
import numpy as np
from jax import lax
from jax.experimental import pallas as pl
from jax.experimental.pallas import tpu as pltpu
from jax.sharding import PartitionSpec as P

RADIX = 4


def dft_blocks(length):
    short = length // RADIX
    out_idx = np.arange(short)[:, None]
    in_idx = np.arange(short)[None, :]
    blocks = []
    for p in range(RADIX):
        phase = (p * in_idx + RADIX * out_idx * in_idx) % length
        angle = phase * (2.0 * math.pi / length)
        cos = np.cos(angle) / math.sqrt(length)
        sin = np.sin(angle) / math.sqrt(length)
        blocks.append(np.block([[cos, -sin], [sin, cos]]))
    full = np.stack(blocks).astype(np.float32)
    high = full.astype(ml_dtypes.bfloat16)
    low = (full - high.astype(np.float32)).astype(ml_dtypes.bfloat16)
    return high, low


def split(value):
    high = value.astype(jnp.bfloat16)
    low = (value - high.astype(jnp.float32)).astype(jnp.bfloat16)
    return high, low


def dot(lhs, rhs):
    return jnp.dot(lhs, rhs, preferred_element_type=jnp.float32)


def left_dot(mat_hi, mat_lo, val_hi, val_lo):
    lhs = jnp.concatenate([mat_hi, mat_hi, mat_lo], axis=1)
    return dot(lhs, jnp.concatenate([val_hi, val_lo, val_hi], axis=0))


def right_dot(val_hi, val_lo, mat_hi, mat_lo):
    lhs = jnp.concatenate([val_hi, val_lo, val_hi], axis=1)
    return dot(lhs, jnp.concatenate([mat_hi, mat_hi, mat_lo], axis=0))


def butterfly(parts, sign):
    (r0, i0), (r1, i1), (r2, i2), (r3, i3) = parts
    sr, si, dr, di = r0 + r2, i0 + i2, r0 - r2, i0 - i2
    tr, ti, er, ei = r1 + r3, i1 + i3, r1 - r3, i1 - i3
    if sign < 0:
        er, ei = -er, -ei
    return [(sr + tr, si + ti), (dr - ei, di + er), (sr - tr, si - ti), (dr + ei, di - er)]


def row_index():
    return lax.broadcasted_iota(jnp.int32, (8, 128), 0)


def lane_index():
    return lax.broadcasted_iota(jnp.int32, (8, 128), 1)


def lane_tiles(tile):
    return [tile[:, i : i + 128] for i in range(0, tile.shape[1], 128)]


def rolled(tiles, amount, axis):
    return [[pltpu.roll(part, amount, axis) for part in tile] for tile in tiles]


def shift_on(tiles, row_shift, col_shift):
    keep = lane_index() >= col_shift
    tiles = rolled([lane_tiles(tile) for tile in tiles], col_shift, 1)
    tiles = [[jnp.where(keep, x, y) for x, y in zip(t, t[-1:] + t[:-1])] for t in tiles]
    keep = row_index() >= row_shift
    tiles = rolled(tiles, row_shift, 0)
    return [
        jnp.concatenate([jnp.where(keep, y, x) for x, y in zip(a, b)], axis=1)
        for a, b in zip(tiles, tiles[1:])
    ]


def shift_back(tiles, row_shift, col_shift):
    keep = lane_index() < 128 - col_shift
    tiles = rolled([lane_tiles(tile) for tile in tiles], (128 - col_shift) % 128, 1)
    tiles = [[jnp.where(keep, x, y) for x, y in zip(t, t[1:] + t[:1])] for t in tiles]
    keep = row_index() < 8 - row_shift
    tiles = rolled(tiles, (8 - row_shift) % 8, 0)
    return [
        jnp.concatenate([jnp.where(keep, x, y) for x, y in zip(a, b)], axis=1)
        for a, b in zip(tiles, tiles[1:])
    ]


def wrap_lanes(block, col_shift):
    rows = block.shape[0]
    keep = lax.broadcasted_iota(jnp.int32, (rows, 128), 1) >= col_shift
    first = jnp.where(keep, block[:, :128], block[:, -128:])
    return jnp.concatenate([first, block[:, 128:-128]], axis=1)


def unwrap_lanes(block, col_shift):
    rows = block.shape[0]
    keep = lax.broadcasted_iota(jnp.int32, (rows, 128), 1) >= col_shift
    zero = jnp.zeros((rows, 128), jnp.float32)
    first = jnp.where(keep, block[:, :128], zero)
    last = jnp.where(keep, zero, block[:, :128])
    return jnp.concatenate([first, block[:, 128:], last], axis=1)


def slots_kernel(
    meta,
    tile_hbm,
    right_a_hbm,
    right_b_hbm,
    lower_a_hbm,
    lower_b_hbm,
    lower_c_hbm,
    corner_a_hbm,
    corner_up_a_hbm,
    corner_up_b_hbm,
    corner_side_hbm,
    amps_hbm,
    pupil_hbm,
    mat_hi_hbm,
    mat_lo_hbm,
    mat_t_hi_hbm,
    mat_t_lo_hbm,
    own_out,
    right_out,
    lower_ca_out,
    lower_b_out,
    corner_a_out,
    corner_b_out,
    dpup_out,
    region,
    grads,
    win,
    left_hi,
    left_lo,
    right_hi,
    right_lo,
    cols_f32,
    rows_f32,
    dwin,
    dpup,
    amps,
    pupil,
    mat_hi,
    mat_lo,
    mat_t_hi,
    mat_t_lo,
    in_sems,
    slot_sems,
    out_sems,
):
    side = pupil.shape[-1]
    short = side // RADIX
    tile_rows, tile_cols = tile_hbm.shape[1:]
    slots = amps_hbm.shape[0]
    lanes = 128
    wide = side + lanes
    half = side // 2
    top, bottom = pl.ds(0, tile_rows), pl.ds(tile_rows, side)

    def copy_in(src, row_range, start, sem):
        dst = region.at[:, row_range, pl.ds(start, src.shape[-1])]
        return pltpu.make_async_copy(src, dst, in_sems.at[sem])

    loads = [
        copy_in(tile_hbm, top, 0, 0),
        copy_in(right_a_hbm, top, tile_cols, 1),
        copy_in(right_b_hbm, top, tile_cols + half, 2),
        copy_in(lower_a_hbm, bottom, 0, 3),
        copy_in(lower_b_hbm, bottom, half, 4),
        copy_in(lower_c_hbm, bottom, side, 5),
        copy_in(corner_a_hbm, bottom, tile_cols, 6),
    ]
    for load in loads:
        load.start()
    from_side = copy_in(corner_side_hbm, bottom, tile_cols + half, 7)
    from_below_a = copy_in(corner_up_a_hbm, bottom, tile_cols + half, 7)
    from_below_b = copy_in(corner_up_b_hbm, bottom, tile_cols + half + half // 2, 7)
    odd = meta[slots, 0]
    pl.when(odd == 1)(from_side.start)

    @pl.when(odd != 1)
    def _():
        from_below_a.start()
        from_below_b.start()

    loads.append(from_side)
    late = (
        (mat_hi_hbm, mat_hi),
        (mat_lo_hbm, mat_lo),
        (mat_t_hi_hbm, mat_t_hi),
        (mat_t_lo_hbm, mat_t_lo),
    )
    late_loads = [
        pltpu.make_async_copy(src, dst, in_sems.at[8 + n]) for n, (src, dst) in enumerate(late)
    ]
    for load in late_loads:
        load.start()
    count = meta[0, 2]
    for slot in range(1, slots):
        count = count + meta[slot, 2]

    def slot_loads(slot):
        return (
            pltpu.make_async_copy(pupil_hbm.at[slot], pupil.at[slot], slot_sems.at[0, slot]),
            pltpu.make_async_copy(amps_hbm.at[slot], amps.at[slot], slot_sems.at[1, slot]),
        )

    @pl.loop(0, count)
    def _(slot):
        for load in slot_loads(slot):
            load.start()

    lower_c_out = lower_ca_out.at[:, :, pl.ds(0, tile_cols - side)]
    lower_a_out = lower_ca_out.at[:, :, pl.ds(tile_cols - side, half)]
    outs = (
        (corner_a_out, bottom, tile_cols),
        (corner_b_out, bottom, tile_cols + half),
        (lower_c_out, bottom, side),
        (lower_a_out, bottom, 0),
        (lower_b_out, bottom, half),
        (right_out, top, tile_cols),
        (own_out, top, 0),
    )
    stores = [
        pltpu.make_async_copy(
            grads.at[:, rows, pl.ds(start, dst.shape[-1])], dst, out_sems.at[n]
        )
        for n, (dst, rows, start) in enumerate(outs)
    ]
    dpup_store = pltpu.make_async_copy(dpup, dpup_out, out_sems.at[7])
    lower_stores = stores[:5]
    upper_stores = stores[5:]

    zero_rows = 16

    @pl.loop(0, grads.shape[1] // zero_rows)
    def _(step):
        rows = pl.ds(pl.multiple_of(step * zero_rows, zero_rows), zero_rows)
        grads[:, rows, :] = jnp.zeros((2, zero_rows, grads.shape[2]), jnp.float32)

    @pl.loop(0, side // zero_rows)
    def _(step):
        rows = pl.ds(pl.multiple_of(step * zero_rows, zero_rows), zero_rows)
        dpup[:, rows, :] = jnp.zeros((2, zero_rows, side), jnp.float32)

    def one_slot(slot):
        row = meta[slot, 0]
        col = meta[slot, 1]
        col_base = pl.multiple_of((col // lanes) * lanes, lanes)
        col_shift = col - col_base
        row_base = pl.multiple_of((row // 8) * 8, 8)
        row_shift = row - row_base

        def cut(step):
            base = pl.multiple_of(step * 32, 32)
            rows = pl.ds(pl.multiple_of(row_base + base, 8), 32)
            for plane in range(2):
                block = region[plane, rows, pl.ds(col_base, wide)]
                win[plane, pl.ds(base, 32), :] = wrap_lanes(block, col_shift)

        above = (tile_rows - row_base) // 32

        @pl.when(slot == 0)
        def _():
            for load in loads[:3]:
                load.wait()

        pl.loop(0, above)(cut)

        @pl.when(slot == 0)
        def _():
            for load in loads[3:]:
                load.wait()

        pl.loop(above, side // 32)(cut)

        first_keep = lax.broadcasted_iota(jnp.int32, (8, side), 0) >= row_shift
        last_rows = pl.ds(pl.multiple_of(row_base + side, 8), 8)
        for plane in range(2):
            block = region[plane, last_rows, pl.ds(col_base, wide)]
            block = wrap_lanes(block, col_shift)
            win[plane, :8, :] = jnp.where(first_keep, win[plane, :8, :], block)

        pupil_load, amps_load = slot_loads(slot)
        pupil_load.wait()

        @pl.when(slot == 0)
        def _():
            for load in late_loads:
                load.wait()

        for start in (0, half):
            for base in range(0, short, 16):
                for col0 in range(start, start + half, short):
                    cols = pl.ds(col0, short)
                    values = []
                    for q in range(RADIX):
                        rows = pl.ds(base + q * short, 16)
                        wr, wi = win[0, rows, cols], win[1, rows, cols]
                        pr, pi = pupil[slot, 0, rows, cols], pupil[slot, 1, rows, cols]
                        values.append((wr * pr - wi * pi, wr * pi + wi * pr))
                    for p, (re, im) in enumerate(butterfly(values, 1)):
                        for offset, value in ((0, re), (short, im)):
                            hi, lo = split(value)
                            rows = pl.ds(base + offset, 16)
                            left_hi[p, rows, cols] = hi
                            left_lo[p, rows, cols] = lo
            cols = pl.ds(start, half)
            for p in range(RADIX):
                rows_f32[p, :, cols] = left_dot(
                    mat_hi[p], mat_lo[p], left_hi[p, :, cols], left_lo[p, :, cols]
                )

        for p in range(RADIX):
            for base in range(0, short, 16):
                values = []
                for q in range(RADIX):
                    cols = pl.ds(q * short, short)
                    values.append(
                        (
                            rows_f32[p, pl.ds(base, 16), cols],
                            rows_f32[p, pl.ds(base + short, 16), cols],
                        )
                    )
                for t, (re, im) in enumerate(butterfly(values, 1)):
                    for offset, value in ((0, re), (short, im)):
                        hi, lo = split(value)
                        rows = pl.ds(base + p * short, 16)
                        right_hi[t, rows, pl.ds(offset, short)] = hi
                        right_lo[t, rows, pl.ds(offset, short)] = lo

        amps_load.wait()

        for t in range(RADIX):
            for start in (0, half):
                rows = pl.ds(start, half)
                field = right_dot(
                    right_hi[t, rows, :], right_lo[t, rows, :], mat_t_hi[t], mat_t_lo[t]
                )
                fre, fim = field[:, :short], field[:, short:]
                measured = amps[slot, rows, pl.ds(t * short, short)]
                factor = 1.0 - measured * lax.rsqrt(fre * fre + fim * fim + 1.0)
                residual = jnp.concatenate([factor * fre, factor * fim], axis=1)
                hi, lo = split(residual)
                cols_f32[t, rows, :] = right_dot(hi, lo, mat_hi[t], mat_lo[t])

        for p in range(RADIX):
            for base in range(0, short, 16):
                rows = pl.ds(base + p * short, 16)
                values = [
                    (cols_f32[t, rows, pl.ds(0, short)], cols_f32[t, rows, pl.ds(short, short)])
                    for t in range(RADIX)
                ]
                for q, (re, im) in enumerate(butterfly(values, -1)):
                    cols = pl.ds(q * short, short)
                    for offset, value in ((0, re), (short, im)):
                        hi, lo = split(value)
                        left_hi[p, pl.ds(base + offset, 16), cols] = hi
                        left_lo[p, pl.ds(base + offset, 16), cols] = lo

        for start in (0, half):
            cols = pl.ds(start, half)
            for p in range(RADIX):
                rows_f32[p, :, cols] = left_dot(
                    mat_t_hi[p], mat_t_lo[p], left_hi[p, :, cols], left_lo[p, :, cols]
                )
            for base in range(0, short, 8):
                for col0 in range(start, start + half, short):
                    cols = pl.ds(col0, short)
                    values = [
                        (
                            rows_f32[p, pl.ds(base, 8), cols],
                            rows_f32[p, pl.ds(base + short, 8), cols],
                        )
                        for p in range(RADIX)
                    ]
                    for q, (re, im) in enumerate(butterfly(values, -1)):
                        rows = pl.ds(base + q * short, 8)
                        pr, pi = pupil[slot, 0, rows, cols], pupil[slot, 1, rows, cols]
                        dwin[0, rows, cols] = pr * re + pi * im
                        dwin[1, rows, cols] = pr * im - pi * re
                        wr, wi = win[0, rows, cols], win[1, rows, cols]
                        win[0, rows, cols] = wr * re + wi * im
                        win[1, rows, cols] = wr * im - wi * re

        @pl.loop(0, side // 32, unroll=2)
        def _(step):
            base = pl.multiple_of(step * 32, 32)
            after = pl.multiple_of((base + 32) % side, 8)
            for plane in range(2):
                tiles = [win[plane, pl.ds(base + 8 * i, 8), :] for i in range(4)]
                tiles.append(win[plane, pl.ds(after, 8), :])
                for i, tile in enumerate(shift_back(tiles, row_shift, col_shift)):
                    dpup[plane, pl.ds(base + 8 * i, 8), :] += tile

        last = slot == count - 1
        pl.when(last)(dpup_store.start)

        zero = jnp.zeros((8, side), jnp.float32)
        for plane in range(2):
            block = dwin[plane, :8, :]
            dwin[plane, :8, :] = jnp.where(first_keep, block, zero)
            dwin[plane, pl.ds(side, 8), :] = jnp.where(first_keep, zero, block)

        def place(step):
            base = pl.multiple_of(step * 40, 8)
            rows = pl.ds(pl.multiple_of(row_base + base, 8), 40)
            for plane in range(2):
                block = unwrap_lanes(dwin[plane, pl.ds(base, 40), :], col_shift)
                target = (plane, rows, pl.ds(col_base, wide))
                grads[target] = grads[target] + block

        steps = (side + 8) // 40
        above = (tile_rows - row_base) // 40
        pl.loop(above, steps)(place)

        @pl.when(last)
        def _():
            for store in lower_stores:
                store.start()

        pl.loop(0, above)(place)

    pl.loop(0, count)(one_slot)

    @pl.when(count == 0)
    def _():
        for store in [dpup_store] + lower_stores:
            store.start()
        for load in loads + late_loads:
            load.wait()

    for store in upper_stores:
        store.start()
    for store in [dpup_store] + stores:
        store.wait()


def slots_call(meta, tile, parts, amps, pupils):
    side = pupils.shape[-1]
    short = side // RADIX
    slots = amps.shape[0]
    tile_rows, tile_cols = tile.shape[1:]
    high, low = dft_blocks(side)
    tables = [jnp.asarray(x) for x in (high, low, high.transpose(0, 2, 1), low.transpose(0, 2, 1))]
    anywhere = pl.BlockSpec(memory_space=pl.ANY)
    f32, bf16 = jnp.float32, jnp.bfloat16
    region = (2, tile_rows + side, tile_cols + side)
    corner = parts[5]
    right = jax.ShapeDtypeStruct((2, tile_rows, side), f32)
    lower_ca = jax.ShapeDtypeStruct((2, side, tile_cols - side // 2), f32)
    dpup = jax.ShapeDtypeStruct(pupils.shape[1:], f32)
    outs = (tile, right, lower_ca, corner, corner, corner, dpup)
    table = pltpu.VMEM(high.shape, bf16)
    return pl.pallas_call(
        slots_kernel,
        out_shape=[jax.ShapeDtypeStruct(x.shape, f32) for x in outs],
        in_specs=[pl.BlockSpec(memory_space=pltpu.SMEM)] + [anywhere] * (len(parts) + 7),
        out_specs=[anywhere] * len(outs),
        scratch_shapes=[
            pltpu.VMEM(region, f32),
            pltpu.VMEM(region, f32),
            pltpu.VMEM((2, side, side), f32),
            pltpu.VMEM((RADIX, 2 * short, side), bf16),
            pltpu.VMEM((RADIX, 2 * short, side), bf16),
            pltpu.VMEM((RADIX, side, 2 * short), bf16),
            pltpu.VMEM((RADIX, side, 2 * short), bf16),
            pltpu.VMEM((RADIX, side, 2 * short), f32),
            pltpu.VMEM((RADIX, 2 * short, side), f32),
            pltpu.VMEM((2, side + 8, side), f32),
            pltpu.VMEM((2, side, side), f32),
            pltpu.VMEM(amps.shape, f32),
            pltpu.VMEM(pupils.shape, f32),
            table,
            table,
            table,
            table,
            pltpu.SemaphoreType.DMA((12,)),
            pltpu.SemaphoreType.DMA((2, slots)),
            pltpu.SemaphoreType.DMA((8,)),
        ],
        compiler_params=pltpu.CompilerParams(vmem_limit_bytes=56 * 1024 * 1024),
        cost_estimate=pl.CostEstimate(
            flops=slots * 48 * 2 * 4 * short * short * side,
            bytes_accessed=40 * 1024 * 1024,
            transcendentals=slots * side * side,
        ),
        name="slots",
    )(meta, tile, *parts, amps, pupils, *tables)


def exact_parts(value):
    hi, rest = split(value)
    rest = value - hi.astype(jnp.float32)
    return (hi, *split(rest))


def prepare_kernel(meta, amps, pupil, perm_rows, perm_cols, amps_out, pupil_out):
    value = sum(dot(part, perm_cols[...]) for part in exact_parts(amps[0]))
    amps_out[0] = sum(dot(perm_rows[...], part) for part in exact_parts(value))

    slot = pl.program_id(0)
    row_shift = meta[slot, 0] % 8
    col_shift = meta[slot, 1] % 128
    side = pupil.shape[-1]

    @pl.loop(0, side // 32, unroll=2)
    def _(step):
        base = pl.multiple_of(step * 32, 32)
        before = pl.multiple_of((base + side - 8) % side, 8)
        for plane in range(2):
            tiles = [pupil[plane, pl.ds(before, 8), :]]
            tiles += [pupil[plane, pl.ds(base + 8 * i, 8), :] for i in range(4)]
            for i, tile in enumerate(shift_on(tiles, row_shift, col_shift)):
                pupil_out[0, plane, pl.ds(base + 8 * i, 8), :] = tile


def prepare(meta, amps, pupil):
    slots, side, _ = amps.shape
    index = np.arange(side)
    perm = np.zeros((side, side), ml_dtypes.bfloat16)
    perm[index, (index % RADIX) * (side // RADIX) + index // RADIX] = 1
    block = pl.BlockSpec((1, side, side), lambda s: (s, 0, 0))
    table = pl.BlockSpec((side, side), lambda s: (0, 0))
    return pl.pallas_call(
        prepare_kernel,
        grid=(slots,),
        out_shape=[
            jax.ShapeDtypeStruct(amps.shape, amps.dtype),
            jax.ShapeDtypeStruct((slots, 2, side, side), pupil.dtype),
        ],
        in_specs=[
            pl.BlockSpec(memory_space=pltpu.SMEM),
            block,
            pl.BlockSpec((2, side, side), lambda s: (0, 0, 0)),
            table,
            table,
        ],
        out_specs=[block, pl.BlockSpec((1, 2, side, side), lambda s: (s, 0, 0, 0))],
        compiler_params=pltpu.CompilerParams(vmem_limit_bytes=32 * 1024 * 1024),
        cost_estimate=pl.CostEstimate(
            flops=slots * 12 * side**3, bytes_accessed=24 * slots * side**2, transcendentals=0
        ),
        name="prepare",
    )(meta, amps, pupil, jnp.asarray(perm.T), jnp.asarray(perm))


def along(axis_pairs, members):
    n_ty, n_tx = members
    pairs = []
    for i in range(n_ty):
        for j in range(n_tx):
            target = axis_pairs(i, j)
            if target is not None and 0 <= target[0] < n_ty and 0 <= target[1] < n_tx:
                pairs.append((i * n_tx + j, target[0] * n_tx + target[1]))
    return pairs


def send(array, rule):
    sizes = (lax.axis_size("ty"), lax.axis_size("tx"))
    return lax.ppermute(array, ("ty", "tx"), along(rule, sizes))


def halve(value, bit):
    rows = value.shape[0] // 2
    mine = lax.axis_index("ty") // bit % 2
    kept = lax.dynamic_slice_in_dim(value, mine * rows, rows, 0)
    sent = lax.dynamic_slice_in_dim(value, (1 - mine) * rows, rows, 0)
    received = lax.ppermute(sent, "ty", [(i, i ^ bit) for i in range(lax.axis_size("ty"))])
    return kept + received


def double(value, bit):
    mine = lax.axis_index("ty") // bit % 2
    other = lax.ppermute(value, "ty", [(i, i ^ bit) for i in range(lax.axis_size("ty"))])
    first = jnp.where(mine == 0, value, other)
    second = jnp.where(mine == 0, other, value)
    return jnp.concatenate([first, second], axis=0)


def stepped(value, axis, inner, step):
    size = lax.axis_size(axis)
    return lax.ppermute(value, axis, [(i, (i + step * inner) % size) for i in range(size)])


def scatter(value, axis, inner):
    members, own = lax.axis_size(axis) // inner, lax.axis_index(axis) // inner
    rows = value.shape[0] // members
    total = lax.dynamic_slice_in_dim(value, own * rows, rows, 0)
    for step in range(1, members):
        piece = lax.dynamic_slice_in_dim(value, (own + step) % members * rows, rows, 0)
        total = total + stepped(piece, axis, inner, step)
    return total


def gather(value, axis, inner):
    members, own = lax.axis_size(axis) // inner, lax.axis_index(axis) // inner
    rows = value.shape[0]
    parts = [value] + [stepped(value, axis, inner, step) for step in range(1, members)]
    out = jnp.zeros((members * rows,) + value.shape[1:], value.dtype)
    for step, part in enumerate(parts):
        out = lax.dynamic_update_slice_in_dim(out, part, (own - step) % members * rows, 0)
    return out


def sum_all(value, axis):
    parts = [value] + [stepped(value, axis, 1, step) for step in range(1, lax.axis_size(axis))]
    while len(parts) > 1:
        middle = len(parts) // 2
        parts = [a + b for a, b in zip(parts[:middle], parts[middle:])]
    return parts[0]


def after(value, *arrivals):
    return lax.optimization_barrier((value, *arrivals))[0]


def body(spectrum, pupil, amplitudes, offsets, live):
    side = pupil.shape[-1]
    half = side // 2
    tile_rows, tile_cols = spectrum.shape[1:]
    n_ty, n_tx = lax.axis_size("ty"), lax.axis_size("tx")
    own_ty, own_tx = lax.axis_index("ty"), lax.axis_index("tx")
    rows_local = offsets[:, 0] - own_ty * tile_rows
    cols_local = offsets[:, 1] - own_tx * tile_cols
    meta = jnp.stack([rows_local, cols_local, live], axis=1)
    meta = jnp.concatenate([meta, jnp.full((1, 3), own_ty % 2, jnp.int32)], axis=0)

    def left(i, j):
        return (i, j - 1)

    def up(i, j):
        return (i - 1, j)

    def up_odd(i, j):
        return (i - 1, j) if i % 2 else None

    lower_b = send(spectrum[:, :side, half:side], up)
    right_a = send(spectrum[:, :, :half], left)
    right_b = send(spectrum[:, :, half:side], left)
    lower_a = send(spectrum[:, :side, :half], up)
    lower_c = send(spectrum[:, :side, side:], up)
    amps, pupils = prepare(meta, amplitudes, pupil)
    lower_b, amps = lax.optimization_barrier((lower_b, amps))
    corner_side = send(lower_b, lambda i, j: (i, j - 1) if i % 2 else None)
    corner_a = send(right_a[:, :side], up)
    corner_up_a = send(right_b[:, :side, : half // 2], up_odd)
    corner_up_b = send(right_b[:, :side, half // 2 :], up_odd)

    parts = (
        right_a,
        right_b,
        lower_a,
        lower_b,
        lower_c,
        corner_a,
        corner_up_a,
        corner_up_b,
        corner_side,
    )
    own_g, right_g, lower_ca_g, lower_b_g, corner_a_g, corner_b_g, dpup = slots_call(
        meta, spectrum, parts, amps, pupils
    )

    def down(i, j):
        return (i + 1, j)

    def right(i, j):
        return (i, j + 1)

    part = halve(dpup.reshape(-1, side), 1)
    back_a = send(corner_a_g, down)
    back_side = send(corner_b_g, lambda i, j: (i, j + 1) if i % 2 else None)
    back_down = send(corner_b_g, lambda i, j: None if i % 2 else (i + 1, j))
    part, back_down = lax.optimization_barrier((part, back_down))
    part = scatter(part, "ty", 2)
    part, lower_ca_g, back_a, back_side = lax.optimization_barrier(
        (part, lower_ca_g, back_a, back_side)
    )
    lower_ca = send(lower_ca_g, down)
    part = sum_all(part, "tx") * (1.0 / math.sqrt(n_ty * n_tx))
    right_g = right_g + jnp.concatenate([back_a, back_down], axis=2)
    right_back = send(after(right_g, part), right)
    part = gather(after(part, lower_ca), "ty", 2)
    lower_b = send(after(lower_b_g + back_side, part), down)
    split_at = tile_cols - side
    spec_grad = own_g.at[:, :, side:].add(lower_ca[:, :, :split_at])
    spec_grad = spec_grad.at[:, :, :half].add(lower_ca[:, :, split_at:])
    part, spec_grad = lax.optimization_barrier((part, spec_grad))
    spec_grad = spec_grad.at[:, :, :side].add(right_back.at[:, :, half:].add(lower_b))
    return spec_grad, double(part, 1).reshape(pupil.shape)


def solution(mesh):
    return jax.shard_map(
        body,
        mesh=mesh,
        in_specs=(
            P(None, "ty", "tx"),
            P(),
            P(("ty", "tx"), None, None),
            P(("ty", "tx"), None),
            P(("ty", "tx")),
        ),
        out_specs=(P(None, "ty", "tx"), P()),
        check_vma=False,
    )
```

```python
import math

import jax
import jax.numpy as jnp
import ml_dtypes
import numpy as np
from jax import lax
from jax.experimental import pallas as pl
from jax.experimental.pallas import tpu as pltpu
from jax.sharding import PartitionSpec as P

RADIX = 4


def dft_blocks(length):
    short = length // RADIX
    out_idx = np.arange(short)[:, None]
    in_idx = np.arange(short)[None, :]
    blocks = []
    for p in range(RADIX):
        phase = (p * in_idx + RADIX * out_idx * in_idx) % length
        angle = phase * (2.0 * math.pi / length)
        cos = np.cos(angle) / math.sqrt(length)
        sin = np.sin(angle) / math.sqrt(length)
        blocks.append(np.block([[cos, -sin], [sin, cos]]))
    full = np.stack(blocks).astype(np.float32)
    high = full.astype(ml_dtypes.bfloat16)
    low = (full - high.astype(np.float32)).astype(ml_dtypes.bfloat16)
    return high, low


def split(value):
    high = value.astype(jnp.bfloat16)
    low = (value - high.astype(jnp.float32)).astype(jnp.bfloat16)
    return high, low


def dot(lhs, rhs):
    return jnp.dot(lhs, rhs, preferred_element_type=jnp.float32)


def left_dot(mat_hi, mat_lo, val_hi, val_lo):
    lhs = jnp.concatenate([mat_hi, mat_hi, mat_lo], axis=1)
    return dot(lhs, jnp.concatenate([val_hi, val_lo, val_hi], axis=0))


def right_dot(val_hi, val_lo, mat_hi, mat_lo):
    lhs = jnp.concatenate([val_hi, val_lo, val_hi], axis=1)
    return dot(lhs, jnp.concatenate([mat_hi, mat_hi, mat_lo], axis=0))


def butterfly(parts, sign):
    (r0, i0), (r1, i1), (r2, i2), (r3, i3) = parts
    sr, si, dr, di = r0 + r2, i0 + i2, r0 - r2, i0 - i2
    tr, ti, er, ei = r1 + r3, i1 + i3, r1 - r3, i1 - i3
    if sign < 0:
        er, ei = -er, -ei
    return [(sr + tr, si + ti), (dr - ei, di + er), (sr - tr, si - ti), (dr + ei, di - er)]


def row_index():
    return lax.broadcasted_iota(jnp.int32, (8, 128), 0)


def lane_index():
    return lax.broadcasted_iota(jnp.int32, (8, 128), 1)


def lane_tiles(tile):
    return [tile[:, i : i + 128] for i in range(0, tile.shape[1], 128)]


def rolled(tiles, amount, axis):
    return [[pltpu.roll(part, amount, axis) for part in tile] for tile in tiles]


def shift_on(tiles, row_shift, col_shift):
    keep = lane_index() >= col_shift
    tiles = rolled([lane_tiles(tile) for tile in tiles], col_shift, 1)
    tiles = [[jnp.where(keep, x, y) for x, y in zip(t, t[-1:] + t[:-1])] for t in tiles]
    keep = row_index() >= row_shift
    tiles = rolled(tiles, row_shift, 0)
    return [
        jnp.concatenate([jnp.where(keep, y, x) for x, y in zip(a, b)], axis=1)
        for a, b in zip(tiles, tiles[1:])
    ]


def shift_back(tiles, row_shift, col_shift):
    keep = lane_index() < 128 - col_shift
    tiles = rolled([lane_tiles(tile) for tile in tiles], (128 - col_shift) % 128, 1)
    tiles = [[jnp.where(keep, x, y) for x, y in zip(t, t[1:] + t[:1])] for t in tiles]
    keep = row_index() < 8 - row_shift
    tiles = rolled(tiles, (8 - row_shift) % 8, 0)
    return [
        jnp.concatenate([jnp.where(keep, x, y) for x, y in zip(a, b)], axis=1)
        for a, b in zip(tiles, tiles[1:])
    ]


def wrap_lanes(block, col_shift):
    rows = block.shape[0]
    keep = lax.broadcasted_iota(jnp.int32, (rows, 128), 1) >= col_shift
    first = jnp.where(keep, block[:, :128], block[:, -128:])
    return jnp.concatenate([first, block[:, 128:-128]], axis=1)


def unwrap_lanes(block, col_shift):
    rows = block.shape[0]
    keep = lax.broadcasted_iota(jnp.int32, (rows, 128), 1) >= col_shift
    zero = jnp.zeros((rows, 128), jnp.float32)
    first = jnp.where(keep, block[:, :128], zero)
    last = jnp.where(keep, zero, block[:, :128])
    return jnp.concatenate([first, block[:, 128:], last], axis=1)


def slots_kernel(
    meta,
    tile_hbm,
    right_a_hbm,
    right_b_hbm,
    lower_a_hbm,
    lower_b_hbm,
    lower_c_hbm,
    corner_a_hbm,
    corner_up_a_hbm,
    corner_up_b_hbm,
    corner_side_hbm,
    amps_hbm,
    pupil_hbm,
    mat_hi_hbm,
    mat_lo_hbm,
    mat_t_hi_hbm,
    mat_t_lo_hbm,
    own_out,
    right_out,
    side_out,
    lower_ca_out,
    lower_b_out,
    corner_out,
    dpup_out,
    region,
    grads,
    win,
    left_hi,
    left_lo,
    right_hi,
    right_lo,
    cols_f32,
    rows_f32,
    dwin,
    dpup,
    amps,
    pupil,
    mat_hi,
    mat_lo,
    mat_t_hi,
    mat_t_lo,
    in_sems,
    slot_sems,
    out_sems,
):
    side = pupil.shape[-1]
    short = side // RADIX
    tile_rows, tile_cols = tile_hbm.shape[1:]
    slots = amps_hbm.shape[0]
    lanes = 128
    wide = side + lanes
    half = side // 2
    top, bottom = pl.ds(0, tile_rows), pl.ds(tile_rows, side)

    def copy_in(src, row_range, start, sem):
        dst = region.at[:, row_range, pl.ds(start, src.shape[-1])]
        return pltpu.make_async_copy(src, dst, in_sems.at[sem])

    loads = [
        copy_in(tile_hbm, top, 0, 0),
        copy_in(right_a_hbm, top, tile_cols, 1),
        copy_in(right_b_hbm, top, tile_cols + half, 2),
        copy_in(lower_a_hbm, bottom, 0, 3),
        copy_in(lower_b_hbm, bottom, half, 4),
        copy_in(lower_c_hbm, bottom, side, 5),
        copy_in(corner_a_hbm, bottom, tile_cols, 6),
    ]
    for load in loads:
        load.start()
    from_side = copy_in(corner_side_hbm, bottom, tile_cols + half, 7)
    from_below_a = copy_in(corner_up_a_hbm, bottom, tile_cols + half, 7)
    from_below_b = copy_in(corner_up_b_hbm, bottom, tile_cols + half + half // 2, 7)
    odd = meta[slots, 0]
    pl.when(odd == 1)(from_side.start)

    @pl.when(odd != 1)
    def _():
        from_below_a.start()
        from_below_b.start()

    loads.append(from_side)
    late = (
        (mat_hi_hbm, mat_hi),
        (mat_lo_hbm, mat_lo),
        (mat_t_hi_hbm, mat_t_hi),
        (mat_t_lo_hbm, mat_t_lo),
    )
    late_loads = [
        pltpu.make_async_copy(src, dst, in_sems.at[8 + n]) for n, (src, dst) in enumerate(late)
    ]
    for load in late_loads:
        load.start()
    count = meta[0, 2]
    for slot in range(1, slots):
        count = count + meta[slot, 2]

    def slot_loads(slot):
        return (
            pltpu.make_async_copy(pupil_hbm.at[slot], pupil.at[slot], slot_sems.at[0, slot]),
            pltpu.make_async_copy(amps_hbm.at[slot], amps.at[slot], slot_sems.at[1, slot]),
        )

    @pl.loop(0, count)
    def _(slot):
        for load in slot_loads(slot):
            load.start()

    cut = corner_out.shape[-1]
    lower_c_out = lower_ca_out.at[:, :, pl.ds(0, tile_cols - side)]
    lower_a_out = lower_ca_out.at[:, :, pl.ds(tile_cols - side, cut)]
    outs = (
        (corner_out, bottom, tile_cols),
        (lower_c_out, bottom, side),
        (lower_a_out, bottom, 0),
        (lower_b_out, bottom, cut),
        (side_out, pl.ds(0, tile_rows + side), tile_cols + cut),
        (right_out, top, tile_cols),
        (own_out, top, 0),
    )
    stores = [
        pltpu.make_async_copy(
            grads.at[:, rows, pl.ds(start, dst.shape[-1])], dst, out_sems.at[n]
        )
        for n, (dst, rows, start) in enumerate(outs)
    ]
    dpup_store = pltpu.make_async_copy(dpup, dpup_out, out_sems.at[7])
    lower_stores = stores[:4]
    upper_stores = stores[4:]

    zero_rows = 16

    @pl.loop(0, grads.shape[1] // zero_rows)
    def _(step):
        rows = pl.ds(pl.multiple_of(step * zero_rows, zero_rows), zero_rows)
        grads[:, rows, :] = jnp.zeros((2, zero_rows, grads.shape[2]), jnp.float32)

    @pl.loop(0, side // zero_rows)
    def _(step):
        rows = pl.ds(pl.multiple_of(step * zero_rows, zero_rows), zero_rows)
        dpup[:, rows, :] = jnp.zeros((2, zero_rows, side), jnp.float32)

    def one_slot(slot):
        row = meta[slot, 0]
        col = meta[slot, 1]
        col_base = pl.multiple_of((col // lanes) * lanes, lanes)
        col_shift = col - col_base
        row_base = pl.multiple_of((row // 8) * 8, 8)
        row_shift = row - row_base

        def cut(step):
            base = pl.multiple_of(step * 32, 32)
            rows = pl.ds(pl.multiple_of(row_base + base, 8), 32)
            for plane in range(2):
                block = region[plane, rows, pl.ds(col_base, wide)]
                win[plane, pl.ds(base, 32), :] = wrap_lanes(block, col_shift)

        above = (tile_rows - row_base) // 32

        @pl.when(slot == 0)
        def _():
            for load in loads[:3]:
                load.wait()

        pl.loop(0, above)(cut)

        @pl.when(slot == 0)
        def _():
            for load in loads[3:]:
                load.wait()

        pl.loop(above, side // 32)(cut)

        first_keep = lax.broadcasted_iota(jnp.int32, (8, side), 0) >= row_shift
        last_rows = pl.ds(pl.multiple_of(row_base + side, 8), 8)
        for plane in range(2):
            block = region[plane, last_rows, pl.ds(col_base, wide)]
            block = wrap_lanes(block, col_shift)
            win[plane, :8, :] = jnp.where(first_keep, win[plane, :8, :], block)

        pupil_load, amps_load = slot_loads(slot)
        pupil_load.wait()

        @pl.when(slot == 0)
        def _():
            for load in late_loads:
                load.wait()

        for start in (0, half):
            for base in range(0, short, 16):
                for col0 in range(start, start + half, short):
                    cols = pl.ds(col0, short)
                    values = []
                    for q in range(RADIX):
                        rows = pl.ds(base + q * short, 16)
                        wr, wi = win[0, rows, cols], win[1, rows, cols]
                        pr, pi = pupil[slot, 0, rows, cols], pupil[slot, 1, rows, cols]
                        values.append((wr * pr - wi * pi, wr * pi + wi * pr))
                    for p, (re, im) in enumerate(butterfly(values, 1)):
                        for offset, value in ((0, re), (short, im)):
                            hi, lo = split(value)
                            rows = pl.ds(base + offset, 16)
                            left_hi[p, rows, cols] = hi
                            left_lo[p, rows, cols] = lo
            cols = pl.ds(start, half)
            for p in range(RADIX):
                rows_f32[p, :, cols] = left_dot(
                    mat_hi[p], mat_lo[p], left_hi[p, :, cols], left_lo[p, :, cols]
                )

        for p in range(RADIX):
            for base in range(0, short, 16):
                values = []
                for q in range(RADIX):
                    cols = pl.ds(q * short, short)
                    values.append(
                        (
                            rows_f32[p, pl.ds(base, 16), cols],
                            rows_f32[p, pl.ds(base + short, 16), cols],
                        )
                    )
                for t, (re, im) in enumerate(butterfly(values, 1)):
                    for offset, value in ((0, re), (short, im)):
                        hi, lo = split(value)
                        rows = pl.ds(base + p * short, 16)
                        right_hi[t, rows, pl.ds(offset, short)] = hi
                        right_lo[t, rows, pl.ds(offset, short)] = lo

        amps_load.wait()

        for t in range(RADIX):
            for start in (0, half):
                rows = pl.ds(start, half)
                field = right_dot(
                    right_hi[t, rows, :], right_lo[t, rows, :], mat_t_hi[t], mat_t_lo[t]
                )
                fre, fim = field[:, :short], field[:, short:]
                measured = amps[slot, rows, pl.ds(t * short, short)]
                factor = 1.0 - measured * lax.rsqrt(fre * fre + fim * fim + 1.0)
                residual = jnp.concatenate([factor * fre, factor * fim], axis=1)
                hi, lo = split(residual)
                cols_f32[t, rows, :] = right_dot(hi, lo, mat_hi[t], mat_lo[t])

        for p in range(RADIX):
            for base in range(0, short, 16):
                rows = pl.ds(base + p * short, 16)
                values = [
                    (cols_f32[t, rows, pl.ds(0, short)], cols_f32[t, rows, pl.ds(short, short)])
                    for t in range(RADIX)
                ]
                for q, (re, im) in enumerate(butterfly(values, -1)):
                    cols = pl.ds(q * short, short)
                    for offset, value in ((0, re), (short, im)):
                        hi, lo = split(value)
                        left_hi[p, pl.ds(base + offset, 16), cols] = hi
                        left_lo[p, pl.ds(base + offset, 16), cols] = lo

        for start in (0, half):
            cols = pl.ds(start, half)
            for p in range(RADIX):
                rows_f32[p, :, cols] = left_dot(
                    mat_t_hi[p], mat_t_lo[p], left_hi[p, :, cols], left_lo[p, :, cols]
                )
            for base in range(0, short, 8):
                for col0 in range(start, start + half, short):
                    cols = pl.ds(col0, short)
                    values = [
                        (
                            rows_f32[p, pl.ds(base, 8), cols],
                            rows_f32[p, pl.ds(base + short, 8), cols],
                        )
                        for p in range(RADIX)
                    ]
                    for q, (re, im) in enumerate(butterfly(values, -1)):
                        rows = pl.ds(base + q * short, 8)
                        pr, pi = pupil[slot, 0, rows, cols], pupil[slot, 1, rows, cols]
                        dwin[0, rows, cols] = pr * re + pi * im
                        dwin[1, rows, cols] = pr * im - pi * re
                        wr, wi = win[0, rows, cols], win[1, rows, cols]
                        win[0, rows, cols] = wr * re + wi * im
                        win[1, rows, cols] = wr * im - wi * re

        @pl.loop(0, side // 32, unroll=2)
        def _(step):
            base = pl.multiple_of(step * 32, 32)
            after = pl.multiple_of((base + 32) % side, 8)
            for plane in range(2):
                tiles = [win[plane, pl.ds(base + 8 * i, 8), :] for i in range(4)]
                tiles.append(win[plane, pl.ds(after, 8), :])
                for i, tile in enumerate(shift_back(tiles, row_shift, col_shift)):
                    dpup[plane, pl.ds(base + 8 * i, 8), :] += tile

        last = slot == count - 1
        pl.when(last)(dpup_store.start)

        zero = jnp.zeros((8, side), jnp.float32)
        for plane in range(2):
            block = dwin[plane, :8, :]
            dwin[plane, :8, :] = jnp.where(first_keep, block, zero)
            dwin[plane, pl.ds(side, 8), :] = jnp.where(first_keep, zero, block)

        def place(step):
            base = pl.multiple_of(step * 40, 8)
            rows = pl.ds(pl.multiple_of(row_base + base, 8), 40)
            for plane in range(2):
                block = unwrap_lanes(dwin[plane, pl.ds(base, 40), :], col_shift)
                target = (plane, rows, pl.ds(col_base, wide))
                grads[target] = grads[target] + block

        steps = (side + 8) // 40
        above = (tile_rows - row_base) // 40
        pl.loop(above, steps)(place)

        @pl.when(last)
        def _():
            for store in lower_stores:
                store.start()

        pl.loop(0, above)(place)

    pl.loop(0, count)(one_slot)

    @pl.when(count == 0)
    def _():
        for store in [dpup_store] + lower_stores:
            store.start()
        for load in loads + late_loads:
            load.wait()

    for store in upper_stores:
        store.start()
    for store in [dpup_store] + stores:
        store.wait()


def back_cut(side):
    return 3 * side // 4


def slots_call(meta, tile, parts, amps, pupils):
    side = pupils.shape[-1]
    short = side // RADIX
    slots = amps.shape[0]
    tile_rows, tile_cols = tile.shape[1:]
    high, low = dft_blocks(side)
    tables = [jnp.asarray(x) for x in (high, low, high.transpose(0, 2, 1), low.transpose(0, 2, 1))]
    anywhere = pl.BlockSpec(memory_space=pl.ANY)
    f32, bf16 = jnp.float32, jnp.bfloat16
    region = (2, tile_rows + side, tile_cols + side)
    cut = back_cut(side)
    dpup = jax.ShapeDtypeStruct(pupils.shape[1:], f32)
    shapes = (
        (tile_rows, cut),
        (tile_rows + side, side - cut),
        (side, tile_cols - side + cut),
        (side, side - cut),
        (side, cut),
    )
    outs = (tile, *(jax.ShapeDtypeStruct((2, *shape), f32) for shape in shapes), dpup)
    table = pltpu.VMEM(high.shape, bf16)
    return pl.pallas_call(
        slots_kernel,
        out_shape=[jax.ShapeDtypeStruct(x.shape, f32) for x in outs],
        in_specs=[pl.BlockSpec(memory_space=pltpu.SMEM)] + [anywhere] * (len(parts) + 7),
        out_specs=[anywhere] * len(outs),
        scratch_shapes=[
            pltpu.VMEM(region, f32),
            pltpu.VMEM(region, f32),
            pltpu.VMEM((2, side, side), f32),
            pltpu.VMEM((RADIX, 2 * short, side), bf16),
            pltpu.VMEM((RADIX, 2 * short, side), bf16),
            pltpu.VMEM((RADIX, side, 2 * short), bf16),
            pltpu.VMEM((RADIX, side, 2 * short), bf16),
            pltpu.VMEM((RADIX, side, 2 * short), f32),
            pltpu.VMEM((RADIX, 2 * short, side), f32),
            pltpu.VMEM((2, side + 8, side), f32),
            pltpu.VMEM((2, side, side), f32),
            pltpu.VMEM(amps.shape, f32),
            pltpu.VMEM(pupils.shape, f32),
            table,
            table,
            table,
            table,
            pltpu.SemaphoreType.DMA((12,)),
            pltpu.SemaphoreType.DMA((2, slots)),
            pltpu.SemaphoreType.DMA((8,)),
        ],
        compiler_params=pltpu.CompilerParams(vmem_limit_bytes=56 * 1024 * 1024),
        cost_estimate=pl.CostEstimate(
            flops=slots * 48 * 2 * 4 * short * short * side,
            bytes_accessed=40 * 1024 * 1024,
            transcendentals=slots * side * side,
        ),
        name="slots",
    )(meta, tile, *parts, amps, pupils, *tables)


def exact_parts(value):
    hi, rest = split(value)
    rest = value - hi.astype(jnp.float32)
    return (hi, *split(rest))


def prepare_kernel(meta, amps, pupil, perm_rows, perm_cols, amps_out, pupil_out):
    value = sum(dot(part, perm_cols[...]) for part in exact_parts(amps[0]))
    amps_out[0] = sum(dot(perm_rows[...], part) for part in exact_parts(value))

    slot = pl.program_id(0)
    row_shift = meta[slot, 0] % 8
    col_shift = meta[slot, 1] % 128
    side = pupil.shape[-1]

    @pl.loop(0, side // 32, unroll=2)
    def _(step):
        base = pl.multiple_of(step * 32, 32)
        before = pl.multiple_of((base + side - 8) % side, 8)
        for plane in range(2):
            tiles = [pupil[plane, pl.ds(before, 8), :]]
            tiles += [pupil[plane, pl.ds(base + 8 * i, 8), :] for i in range(4)]
            for i, tile in enumerate(shift_on(tiles, row_shift, col_shift)):
                pupil_out[0, plane, pl.ds(base + 8 * i, 8), :] = tile


def prepare(meta, amps, pupil):
    slots, side, _ = amps.shape
    index = np.arange(side)
    perm = np.zeros((side, side), ml_dtypes.bfloat16)
    perm[index, (index % RADIX) * (side // RADIX) + index // RADIX] = 1
    block = pl.BlockSpec((1, side, side), lambda s: (s, 0, 0))
    table = pl.BlockSpec((side, side), lambda s: (0, 0))
    return pl.pallas_call(
        prepare_kernel,
        grid=(slots,),
        out_shape=[
            jax.ShapeDtypeStruct(amps.shape, amps.dtype),
            jax.ShapeDtypeStruct((slots, 2, side, side), pupil.dtype),
        ],
        in_specs=[
            pl.BlockSpec(memory_space=pltpu.SMEM),
            block,
            pl.BlockSpec((2, side, side), lambda s: (0, 0, 0)),
            table,
            table,
        ],
        out_specs=[block, pl.BlockSpec((1, 2, side, side), lambda s: (s, 0, 0, 0))],
        compiler_params=pltpu.CompilerParams(vmem_limit_bytes=32 * 1024 * 1024),
        cost_estimate=pl.CostEstimate(
            flops=slots * 12 * side**3, bytes_accessed=24 * slots * side**2, transcendentals=0
        ),
        name="prepare",
    )(meta, amps, pupil, jnp.asarray(perm.T), jnp.asarray(perm))


def along(axis_pairs, members):
    n_ty, n_tx = members
    pairs = []
    for i in range(n_ty):
        for j in range(n_tx):
            target = axis_pairs(i, j)
            if target is not None and 0 <= target[0] < n_ty and 0 <= target[1] < n_tx:
                pairs.append((i * n_tx + j, target[0] * n_tx + target[1]))
    return pairs


def send(array, rule):
    sizes = (lax.axis_size("ty"), lax.axis_size("tx"))
    return lax.ppermute(array, ("ty", "tx"), along(rule, sizes))


def halve(value, bit):
    rows = value.shape[0] // 2
    mine = lax.axis_index("ty") // bit % 2
    kept = lax.dynamic_slice_in_dim(value, mine * rows, rows, 0)
    sent = lax.dynamic_slice_in_dim(value, (1 - mine) * rows, rows, 0)
    received = lax.ppermute(sent, "ty", [(i, i ^ bit) for i in range(lax.axis_size("ty"))])
    return kept + received


def double(value, bit):
    mine = lax.axis_index("ty") // bit % 2
    other = lax.ppermute(value, "ty", [(i, i ^ bit) for i in range(lax.axis_size("ty"))])
    first = jnp.where(mine == 0, value, other)
    second = jnp.where(mine == 0, other, value)
    return jnp.concatenate([first, second], axis=0)


def stepped(value, axis, inner, step):
    size = lax.axis_size(axis)
    return lax.ppermute(value, axis, [(i, (i + step * inner) % size) for i in range(size)])


def scatter(value, axis, inner):
    members, own = lax.axis_size(axis) // inner, lax.axis_index(axis) // inner
    rows = value.shape[0] // members
    total = lax.dynamic_slice_in_dim(value, own * rows, rows, 0)
    for step in range(1, members):
        piece = lax.dynamic_slice_in_dim(value, (own + step) % members * rows, rows, 0)
        total = total + stepped(piece, axis, inner, step)
    return total


def gather(value, axis, inner):
    members, own = lax.axis_size(axis) // inner, lax.axis_index(axis) // inner
    rows = value.shape[0]
    parts = [value] + [stepped(value, axis, inner, step) for step in range(1, members)]
    out = jnp.zeros((members * rows,) + value.shape[1:], value.dtype)
    for step, part in enumerate(parts):
        out = lax.dynamic_update_slice_in_dim(out, part, (own - step) % members * rows, 0)
    return out


def sum_all(value, axis):
    parts = [value] + [stepped(value, axis, 1, step) for step in range(1, lax.axis_size(axis))]
    while len(parts) > 1:
        middle = len(parts) // 2
        parts = [a + b for a, b in zip(parts[:middle], parts[middle:])]
    return parts[0]


def after(value, *arrivals):
    return lax.optimization_barrier((value, *arrivals))[0]


def body(spectrum, pupil, amplitudes, offsets, live):
    side = pupil.shape[-1]
    half = side // 2
    tile_rows, tile_cols = spectrum.shape[1:]
    n_ty, n_tx = lax.axis_size("ty"), lax.axis_size("tx")
    own_ty, own_tx = lax.axis_index("ty"), lax.axis_index("tx")
    rows_local = offsets[:, 0] - own_ty * tile_rows
    cols_local = offsets[:, 1] - own_tx * tile_cols
    meta = jnp.stack([rows_local, cols_local, live], axis=1)
    meta = jnp.concatenate([meta, jnp.full((1, 3), own_ty % 2, jnp.int32)], axis=0)

    def left(i, j):
        return (i, j - 1)

    def up(i, j):
        return (i - 1, j)

    def up_odd(i, j):
        return (i - 1, j) if i % 2 else None

    lower_b = send(spectrum[:, :side, half:side], up)
    right_a = send(spectrum[:, :, :half], left)
    right_b = send(spectrum[:, :, half:side], left)
    lower_a = send(spectrum[:, :side, :half], up)
    lower_c = send(spectrum[:, :side, side:], up)
    amps, pupils = prepare(meta, amplitudes, pupil)
    lower_b, amps = lax.optimization_barrier((lower_b, amps))
    corner_side = send(lower_b, lambda i, j: (i, j - 1) if i % 2 else None)
    corner_a = send(right_a[:, :side], up)
    corner_up_a = send(right_b[:, :side, : half // 2], up_odd)
    corner_up_b = send(right_b[:, :side, half // 2 :], up_odd)

    parts = (
        right_a,
        right_b,
        lower_a,
        lower_b,
        lower_c,
        corner_a,
        corner_up_a,
        corner_up_b,
        corner_side,
    )
    own_g, right_g, side_g, lower_ca_g, lower_b_g, corner_g, dpup = slots_call(
        meta, spectrum, parts, amps, pupils
    )

    def down(i, j):
        return (i + 1, j)

    def right(i, j):
        return (i, j + 1)

    cut = back_cut(side)
    split_at = tile_cols - side
    part = halve(dpup.reshape(-1, side), 1)
    corner = send(corner_g, down)
    beside = send(side_g, right)
    part = scatter(part, "ty", 2)
    part, lower_ca_g, corner, beside = lax.optimization_barrier((part, lower_ca_g, corner, beside))
    lower_ca = send(lower_ca_g, down)
    part = sum_all(part, "tx") * (1.0 / math.sqrt(n_ty * n_tx))
    right_back = send(after(right_g + corner, part), right)
    part = gather(after(part, lower_ca), "ty", 2)
    lower_b = send(after(lower_b_g + beside[:, tile_rows:], part), down)
    spec_grad = own_g.at[:, :, side:].add(lower_ca[:, :, :split_at])
    spec_grad = spec_grad.at[:, :, :cut].add(lower_ca[:, :, split_at:])
    spec_grad = spec_grad.at[:, :, cut:side].add(beside[:, :tile_rows])
    part, spec_grad = lax.optimization_barrier((part, spec_grad))
    spec_grad = spec_grad.at[:, :, cut:side].add(lower_b)
    spec_grad = spec_grad.at[:, :, :cut].add(right_back)
    return spec_grad, double(part, 1).reshape(pupil.shape)


def solution(mesh):
    return jax.shard_map(
        body,
        mesh=mesh,
        in_specs=(
            P(None, "ty", "tx"),
            P(),
            P(("ty", "tx"), None, None),
            P(("ty", "tx"), None),
            P(("ty", "tx")),
        ),
        out_specs=(P(None, "ty", "tx"), P()),
        check_vma=False,
    )
```

```python
import math

import jax
import jax.numpy as jnp
import ml_dtypes
import numpy as np
from jax import lax
from jax.experimental import pallas as pl
from jax.experimental.pallas import tpu as pltpu
from jax.sharding import PartitionSpec as P

RADIX = 4


def dft_blocks(length):
    short = length // RADIX
    out_idx = np.arange(short)[:, None]
    in_idx = np.arange(short)[None, :]
    blocks = []
    for p in range(RADIX):
        phase = (p * in_idx + RADIX * out_idx * in_idx) % length
        angle = phase * (2.0 * math.pi / length)
        cos = np.cos(angle) / math.sqrt(length)
        sin = np.sin(angle) / math.sqrt(length)
        blocks.append(np.block([[cos, -sin], [sin, cos]]))
    full = np.stack(blocks).astype(np.float32)
    high = full.astype(ml_dtypes.bfloat16)
    low = (full - high.astype(np.float32)).astype(ml_dtypes.bfloat16)
    return high, low


def split(value):
    high = value.astype(jnp.bfloat16)
    low = (value - high.astype(jnp.float32)).astype(jnp.bfloat16)
    return high, low


def dot(lhs, rhs):
    return jnp.dot(lhs, rhs, preferred_element_type=jnp.float32)


def left_dot(mat_hi, mat_lo, val_hi, val_lo):
    lhs = jnp.concatenate([mat_hi, mat_hi, mat_lo], axis=1)
    return dot(lhs, jnp.concatenate([val_hi, val_lo, val_hi], axis=0))


def right_dot(val_hi, val_lo, mat_hi, mat_lo):
    lhs = jnp.concatenate([val_hi, val_lo, val_hi], axis=1)
    return dot(lhs, jnp.concatenate([mat_hi, mat_hi, mat_lo], axis=0))


def butterfly(parts, sign):
    (r0, i0), (r1, i1), (r2, i2), (r3, i3) = parts
    sr, si, dr, di = r0 + r2, i0 + i2, r0 - r2, i0 - i2
    tr, ti, er, ei = r1 + r3, i1 + i3, r1 - r3, i1 - i3
    if sign < 0:
        er, ei = -er, -ei
    return [(sr + tr, si + ti), (dr - ei, di + er), (sr - tr, si - ti), (dr + ei, di - er)]


def row_index():
    return lax.broadcasted_iota(jnp.int32, (8, 128), 0)


def lane_index():
    return lax.broadcasted_iota(jnp.int32, (8, 128), 1)


def lane_tiles(tile):
    return [tile[:, i : i + 128] for i in range(0, tile.shape[1], 128)]


def rolled(tiles, amount, axis):
    return [[pltpu.roll(part, amount, axis) for part in tile] for tile in tiles]


def shift_on(tiles, row_shift, col_shift):
    keep = lane_index() >= col_shift
    tiles = rolled([lane_tiles(tile) for tile in tiles], col_shift, 1)
    tiles = [[jnp.where(keep, x, y) for x, y in zip(t, t[-1:] + t[:-1])] for t in tiles]
    keep = row_index() >= row_shift
    tiles = rolled(tiles, row_shift, 0)
    return [
        jnp.concatenate([jnp.where(keep, y, x) for x, y in zip(a, b)], axis=1)
        for a, b in zip(tiles, tiles[1:])
    ]


def shift_back(tiles, row_shift, col_shift):
    keep = lane_index() < 128 - col_shift
    tiles = rolled([lane_tiles(tile) for tile in tiles], (128 - col_shift) % 128, 1)
    tiles = [[jnp.where(keep, x, y) for x, y in zip(t, t[1:] + t[:1])] for t in tiles]
    keep = row_index() < 8 - row_shift
    tiles = rolled(tiles, (8 - row_shift) % 8, 0)
    return [
        jnp.concatenate([jnp.where(keep, x, y) for x, y in zip(a, b)], axis=1)
        for a, b in zip(tiles, tiles[1:])
    ]


def wrap_lanes(block, col_shift):
    rows = block.shape[0]
    keep = lax.broadcasted_iota(jnp.int32, (rows, 128), 1) >= col_shift
    first = jnp.where(keep, block[:, :128], block[:, -128:])
    return jnp.concatenate([first, block[:, 128:-128]], axis=1)


def unwrap_lanes(block, col_shift):
    rows = block.shape[0]
    keep = lax.broadcasted_iota(jnp.int32, (rows, 128), 1) >= col_shift
    zero = jnp.zeros((rows, 128), jnp.float32)
    first = jnp.where(keep, block[:, :128], zero)
    last = jnp.where(keep, zero, block[:, :128])
    return jnp.concatenate([first, block[:, 128:], last], axis=1)


def slots_kernel(
    meta,
    tile_hbm,
    right_a_hbm,
    right_b_hbm,
    lower_a_hbm,
    lower_b_hbm,
    lower_c_hbm,
    corner_a_hbm,
    corner_up_a_hbm,
    corner_up_b_hbm,
    corner_side_hbm,
    amps_hbm,
    pupil_hbm,
    mat_hi_hbm,
    mat_lo_hbm,
    mat_t_hi_hbm,
    mat_t_lo_hbm,
    own_out,
    right_out,
    side_out,
    lower_ca_out,
    lower_b_out,
    corner_out,
    keep_out,
    give_out,
    region,
    grads,
    win,
    left_hi,
    left_lo,
    right_hi,
    right_lo,
    cols_f32,
    rows_f32,
    dwin,
    dpup,
    amps,
    pupil,
    mat_hi,
    mat_lo,
    mat_t_hi,
    mat_t_lo,
    in_sems,
    slot_sems,
    out_sems,
):
    side = pupil.shape[-1]
    short = side // RADIX
    tile_rows, tile_cols = tile_hbm.shape[1:]
    slots = amps_hbm.shape[0]
    lanes = 128
    wide = side + lanes
    half = side // 2
    top, bottom = pl.ds(0, tile_rows), pl.ds(tile_rows, side)

    def copy_in(src, row_range, start, sem):
        dst = region.at[:, row_range, pl.ds(start, src.shape[-1])]
        return pltpu.make_async_copy(src, dst, in_sems.at[sem])

    loads = [
        copy_in(tile_hbm, top, 0, 0),
        copy_in(right_a_hbm, top, tile_cols, 1),
        copy_in(right_b_hbm, top, tile_cols + half, 2),
        copy_in(lower_a_hbm, bottom, 0, 3),
        copy_in(lower_b_hbm, bottom, half, 4),
        copy_in(lower_c_hbm, bottom, side, 5),
        copy_in(corner_a_hbm, bottom, tile_cols, 6),
    ]
    for load in loads:
        load.start()
    from_side = copy_in(corner_side_hbm, bottom, tile_cols + half, 7)
    from_below_a = copy_in(corner_up_a_hbm, bottom, tile_cols + half, 7)
    from_below_b = copy_in(corner_up_b_hbm, bottom, tile_cols + half + half // 2, 7)
    odd = meta[slots, 0]
    pl.when(odd == 1)(from_side.start)

    @pl.when(odd != 1)
    def _():
        from_below_a.start()
        from_below_b.start()

    loads.append(from_side)
    late = (
        (mat_hi_hbm, mat_hi),
        (mat_lo_hbm, mat_lo),
        (mat_t_hi_hbm, mat_t_hi),
        (mat_t_lo_hbm, mat_t_lo),
    )
    late_loads = [
        pltpu.make_async_copy(src, dst, in_sems.at[8 + n]) for n, (src, dst) in enumerate(late)
    ]
    for load in late_loads:
        load.start()
    count = meta[0, 2]
    for slot in range(1, slots):
        count = count + meta[slot, 2]

    def slot_loads(slot):
        return (
            pltpu.make_async_copy(pupil_hbm.at[slot], pupil.at[slot], slot_sems.at[0, slot]),
            pltpu.make_async_copy(amps_hbm.at[slot], amps.at[slot], slot_sems.at[1, slot]),
        )

    @pl.loop(0, count)
    def _(slot):
        for load in slot_loads(slot):
            load.start()

    cut = corner_out.shape[-1]
    lower_c_out = lower_ca_out.at[:, :, pl.ds(0, tile_cols - side)]
    lower_a_out = lower_ca_out.at[:, :, pl.ds(tile_cols - side, cut)]
    outs = (
        (corner_out, bottom, tile_cols),
        (lower_c_out, bottom, side),
        (lower_a_out, bottom, 0),
        (lower_b_out, bottom, cut),
        (side_out, pl.ds(0, tile_rows + side), tile_cols + cut),
        (right_out, top, tile_cols),
        (own_out, top, 0),
    )
    stores = [
        pltpu.make_async_copy(
            grads.at[:, rows, pl.ds(start, dst.shape[-1])], dst, out_sems.at[n]
        )
        for n, (dst, rows, start) in enumerate(outs)
    ]
    dpup_stores = [
        [
            pltpu.make_async_copy(dpup.at[plane], keep_out, out_sems.at[7]),
            pltpu.make_async_copy(dpup.at[1 - plane], give_out, out_sems.at[8]),
        ]
        for plane in range(2)
    ]

    def store_dpup():
        for plane, copies in enumerate(dpup_stores):
            for copy in copies:
                pl.when(odd == plane)(copy.start)

    lower_stores = stores[:4]
    upper_stores = stores[4:]

    zero_rows = 16

    @pl.loop(0, grads.shape[1] // zero_rows)
    def _(step):
        rows = pl.ds(pl.multiple_of(step * zero_rows, zero_rows), zero_rows)
        grads[:, rows, :] = jnp.zeros((2, zero_rows, grads.shape[2]), jnp.float32)

    @pl.loop(0, side // zero_rows)
    def _(step):
        rows = pl.ds(pl.multiple_of(step * zero_rows, zero_rows), zero_rows)
        dpup[:, rows, :] = jnp.zeros((2, zero_rows, side), jnp.float32)

    def one_slot(slot):
        row = meta[slot, 0]
        col = meta[slot, 1]
        col_base = pl.multiple_of((col // lanes) * lanes, lanes)
        col_shift = col - col_base
        row_base = pl.multiple_of((row // 8) * 8, 8)
        row_shift = row - row_base

        def cut(step):
            base = pl.multiple_of(step * 32, 32)
            rows = pl.ds(pl.multiple_of(row_base + base, 8), 32)
            for plane in range(2):
                block = region[plane, rows, pl.ds(col_base, wide)]
                win[plane, pl.ds(base, 32), :] = wrap_lanes(block, col_shift)

        above = (tile_rows - row_base) // 32

        @pl.when(slot == 0)
        def _():
            for load in loads[:3]:
                load.wait()

        pl.loop(0, above)(cut)

        @pl.when(slot == 0)
        def _():
            for load in loads[3:]:
                load.wait()

        pl.loop(above, side // 32)(cut)

        first_keep = lax.broadcasted_iota(jnp.int32, (8, side), 0) >= row_shift
        last_rows = pl.ds(pl.multiple_of(row_base + side, 8), 8)
        for plane in range(2):
            block = region[plane, last_rows, pl.ds(col_base, wide)]
            block = wrap_lanes(block, col_shift)
            win[plane, :8, :] = jnp.where(first_keep, win[plane, :8, :], block)

        pupil_load, amps_load = slot_loads(slot)
        pupil_load.wait()

        @pl.when(slot == 0)
        def _():
            for load in late_loads:
                load.wait()

        for start in (0, half):
            for base in range(0, short, 16):
                for col0 in range(start, start + half, short):
                    cols = pl.ds(col0, short)
                    values = []
                    for q in range(RADIX):
                        rows = pl.ds(base + q * short, 16)
                        wr, wi = win[0, rows, cols], win[1, rows, cols]
                        pr, pi = pupil[slot, 0, rows, cols], pupil[slot, 1, rows, cols]
                        values.append((wr * pr - wi * pi, wr * pi + wi * pr))
                    for p, (re, im) in enumerate(butterfly(values, 1)):
                        for offset, value in ((0, re), (short, im)):
                            hi, lo = split(value)
                            rows = pl.ds(base + offset, 16)
                            left_hi[p, rows, cols] = hi
                            left_lo[p, rows, cols] = lo
            cols = pl.ds(start, half)
            for p in range(RADIX):
                rows_f32[p, :, cols] = left_dot(
                    mat_hi[p], mat_lo[p], left_hi[p, :, cols], left_lo[p, :, cols]
                )

        for p in range(RADIX):
            for base in range(0, short, 16):
                values = []
                for q in range(RADIX):
                    cols = pl.ds(q * short, short)
                    values.append(
                        (
                            rows_f32[p, pl.ds(base, 16), cols],
                            rows_f32[p, pl.ds(base + short, 16), cols],
                        )
                    )
                for t, (re, im) in enumerate(butterfly(values, 1)):
                    for offset, value in ((0, re), (short, im)):
                        hi, lo = split(value)
                        rows = pl.ds(base + p * short, 16)
                        right_hi[t, rows, pl.ds(offset, short)] = hi
                        right_lo[t, rows, pl.ds(offset, short)] = lo

        amps_load.wait()

        for t in range(RADIX):
            for start in (0, half):
                rows = pl.ds(start, half)
                field = right_dot(
                    right_hi[t, rows, :], right_lo[t, rows, :], mat_t_hi[t], mat_t_lo[t]
                )
                fre, fim = field[:, :short], field[:, short:]
                measured = amps[slot, rows, pl.ds(t * short, short)]
                factor = 1.0 - measured * lax.rsqrt(fre * fre + fim * fim + 1.0)
                residual = jnp.concatenate([factor * fre, factor * fim], axis=1)
                hi, lo = split(residual)
                cols_f32[t, rows, :] = right_dot(hi, lo, mat_hi[t], mat_lo[t])

        for p in range(RADIX):
            for base in range(0, short, 16):
                rows = pl.ds(base + p * short, 16)
                values = [
                    (cols_f32[t, rows, pl.ds(0, short)], cols_f32[t, rows, pl.ds(short, short)])
                    for t in range(RADIX)
                ]
                for q, (re, im) in enumerate(butterfly(values, -1)):
                    cols = pl.ds(q * short, short)
                    for offset, value in ((0, re), (short, im)):
                        hi, lo = split(value)
                        left_hi[p, pl.ds(base + offset, 16), cols] = hi
                        left_lo[p, pl.ds(base + offset, 16), cols] = lo

        for start in (0, half):
            cols = pl.ds(start, half)
            for p in range(RADIX):
                rows_f32[p, :, cols] = left_dot(
                    mat_t_hi[p], mat_t_lo[p], left_hi[p, :, cols], left_lo[p, :, cols]
                )
            for base in range(0, short, 8):
                for col0 in range(start, start + half, short):
                    cols = pl.ds(col0, short)
                    values = [
                        (
                            rows_f32[p, pl.ds(base, 8), cols],
                            rows_f32[p, pl.ds(base + short, 8), cols],
                        )
                        for p in range(RADIX)
                    ]
                    for q, (re, im) in enumerate(butterfly(values, -1)):
                        rows = pl.ds(base + q * short, 8)
                        pr, pi = pupil[slot, 0, rows, cols], pupil[slot, 1, rows, cols]
                        dwin[0, rows, cols] = pr * re + pi * im
                        dwin[1, rows, cols] = pr * im - pi * re
                        wr, wi = win[0, rows, cols], win[1, rows, cols]
                        win[0, rows, cols] = wr * re + wi * im
                        win[1, rows, cols] = wr * im - wi * re

        @pl.loop(0, side // 32, unroll=2)
        def _(step):
            base = pl.multiple_of(step * 32, 32)
            after = pl.multiple_of((base + 32) % side, 8)
            for plane in range(2):
                tiles = [win[plane, pl.ds(base + 8 * i, 8), :] for i in range(4)]
                tiles.append(win[plane, pl.ds(after, 8), :])
                for i, tile in enumerate(shift_back(tiles, row_shift, col_shift)):
                    dpup[plane, pl.ds(base + 8 * i, 8), :] += tile

        last = slot == count - 1
        pl.when(last)(store_dpup)

        zero = jnp.zeros((8, side), jnp.float32)
        for plane in range(2):
            block = dwin[plane, :8, :]
            dwin[plane, :8, :] = jnp.where(first_keep, block, zero)
            dwin[plane, pl.ds(side, 8), :] = jnp.where(first_keep, zero, block)

        def place(step):
            base = pl.multiple_of(step * 40, 8)
            rows = pl.ds(pl.multiple_of(row_base + base, 8), 40)
            for plane in range(2):
                block = unwrap_lanes(dwin[plane, pl.ds(base, 40), :], col_shift)
                target = (plane, rows, pl.ds(col_base, wide))
                grads[target] = grads[target] + block

        steps = (side + 8) // 40
        above = (tile_rows - row_base) // 40
        pl.loop(above, steps)(place)

        @pl.when(last)
        def _():
            for store in lower_stores:
                store.start()

        pl.loop(0, above)(place)

    pl.loop(0, count)(one_slot)

    @pl.when(count == 0)
    def _():
        store_dpup()
        for store in lower_stores:
            store.start()
        for load in loads + late_loads:
            load.wait()

    for store in upper_stores:
        store.start()
    for store in dpup_stores[0] + stores:
        store.wait()


def back_cut(side):
    return 3 * side // 4


def slots_call(meta, tile, parts, amps, pupils):
    side = pupils.shape[-1]
    short = side // RADIX
    slots = amps.shape[0]
    tile_rows, tile_cols = tile.shape[1:]
    high, low = dft_blocks(side)
    tables = [jnp.asarray(x) for x in (high, low, high.transpose(0, 2, 1), low.transpose(0, 2, 1))]
    anywhere = pl.BlockSpec(memory_space=pl.ANY)
    f32, bf16 = jnp.float32, jnp.bfloat16
    region = (2, tile_rows + side, tile_cols + side)
    cut = back_cut(side)
    plane = jax.ShapeDtypeStruct((side, side), f32)
    shapes = (
        (tile_rows, cut),
        (tile_rows + side, side - cut),
        (side, tile_cols - side + cut),
        (side, side - cut),
        (side, cut),
    )
    outs = (tile, *(jax.ShapeDtypeStruct((2, *shape), f32) for shape in shapes), plane, plane)
    table = pltpu.VMEM(high.shape, bf16)
    return pl.pallas_call(
        slots_kernel,
        out_shape=[jax.ShapeDtypeStruct(x.shape, f32) for x in outs],
        in_specs=[pl.BlockSpec(memory_space=pltpu.SMEM)] + [anywhere] * (len(parts) + 7),
        out_specs=[anywhere] * len(outs),
        scratch_shapes=[
            pltpu.VMEM(region, f32),
            pltpu.VMEM(region, f32),
            pltpu.VMEM((2, side, side), f32),
            pltpu.VMEM((RADIX, 2 * short, side), bf16),
            pltpu.VMEM((RADIX, 2 * short, side), bf16),
            pltpu.VMEM((RADIX, side, 2 * short), bf16),
            pltpu.VMEM((RADIX, side, 2 * short), bf16),
            pltpu.VMEM((RADIX, side, 2 * short), f32),
            pltpu.VMEM((RADIX, 2 * short, side), f32),
            pltpu.VMEM((2, side + 8, side), f32),
            pltpu.VMEM((2, side, side), f32),
            pltpu.VMEM(amps.shape, f32),
            pltpu.VMEM(pupils.shape, f32),
            table,
            table,
            table,
            table,
            pltpu.SemaphoreType.DMA((12,)),
            pltpu.SemaphoreType.DMA((2, slots)),
            pltpu.SemaphoreType.DMA((9,)),
        ],
        compiler_params=pltpu.CompilerParams(vmem_limit_bytes=56 * 1024 * 1024),
        cost_estimate=pl.CostEstimate(
            flops=slots * 48 * 2 * 4 * short * short * side,
            bytes_accessed=40 * 1024 * 1024,
            transcendentals=slots * side * side,
        ),
        name="slots",
    )(meta, tile, *parts, amps, pupils, *tables)


def exact_parts(value):
    hi, rest = split(value)
    rest = value - hi.astype(jnp.float32)
    return (hi, *split(rest))


def prepare_kernel(meta, amps, pupil, perm_rows, perm_cols, amps_out, pupil_out):
    value = sum(dot(part, perm_cols[...]) for part in exact_parts(amps[0]))
    amps_out[0] = sum(dot(perm_rows[...], part) for part in exact_parts(value))

    slot = pl.program_id(0)
    row_shift = meta[slot, 0] % 8
    col_shift = meta[slot, 1] % 128
    side = pupil.shape[-1]

    @pl.loop(0, side // 32, unroll=2)
    def _(step):
        base = pl.multiple_of(step * 32, 32)
        before = pl.multiple_of((base + side - 8) % side, 8)
        for plane in range(2):
            tiles = [pupil[plane, pl.ds(before, 8), :]]
            tiles += [pupil[plane, pl.ds(base + 8 * i, 8), :] for i in range(4)]
            for i, tile in enumerate(shift_on(tiles, row_shift, col_shift)):
                pupil_out[0, plane, pl.ds(base + 8 * i, 8), :] = tile


def prepare(meta, amps, pupil):
    slots, side, _ = amps.shape
    index = np.arange(side)
    perm = np.zeros((side, side), ml_dtypes.bfloat16)
    perm[index, (index % RADIX) * (side // RADIX) + index // RADIX] = 1
    block = pl.BlockSpec((1, side, side), lambda s: (s, 0, 0))
    table = pl.BlockSpec((side, side), lambda s: (0, 0))
    return pl.pallas_call(
        prepare_kernel,
        grid=(slots,),
        out_shape=[
            jax.ShapeDtypeStruct(amps.shape, amps.dtype),
            jax.ShapeDtypeStruct((slots, 2, side, side), pupil.dtype),
        ],
        in_specs=[
            pl.BlockSpec(memory_space=pltpu.SMEM),
            block,
            pl.BlockSpec((2, side, side), lambda s: (0, 0, 0)),
            table,
            table,
        ],
        out_specs=[block, pl.BlockSpec((1, 2, side, side), lambda s: (s, 0, 0, 0))],
        compiler_params=pltpu.CompilerParams(vmem_limit_bytes=32 * 1024 * 1024),
        cost_estimate=pl.CostEstimate(
            flops=slots * 12 * side**3, bytes_accessed=24 * slots * side**2, transcendentals=0
        ),
        name="prepare",
    )(meta, amps, pupil, jnp.asarray(perm.T), jnp.asarray(perm))


def along(axis_pairs, members):
    n_ty, n_tx = members
    pairs = []
    for i in range(n_ty):
        for j in range(n_tx):
            target = axis_pairs(i, j)
            if target is not None and 0 <= target[0] < n_ty and 0 <= target[1] < n_tx:
                pairs.append((i * n_tx + j, target[0] * n_tx + target[1]))
    return pairs


def send(array, rule):
    sizes = (lax.axis_size("ty"), lax.axis_size("tx"))
    return lax.ppermute(array, ("ty", "tx"), along(rule, sizes))


def double(value, bit):
    mine = lax.axis_index("ty") // bit % 2
    other = lax.ppermute(value, "ty", [(i, i ^ bit) for i in range(lax.axis_size("ty"))])
    first = jnp.where(mine == 0, value, other)
    second = jnp.where(mine == 0, other, value)
    return jnp.concatenate([first, second], axis=0)


def stepped(value, axis, inner, step):
    size = lax.axis_size(axis)
    return lax.ppermute(value, axis, [(i, (i + step * inner) % size) for i in range(size)])


def scatter(value, axis, inner):
    members, own = lax.axis_size(axis) // inner, lax.axis_index(axis) // inner
    rows = value.shape[0] // members
    total = lax.dynamic_slice_in_dim(value, own * rows, rows, 0)
    for step in range(1, members):
        piece = lax.dynamic_slice_in_dim(value, (own + step) % members * rows, rows, 0)
        total = total + stepped(piece, axis, inner, step)
    return total


def gather(value, axis, inner):
    members, own = lax.axis_size(axis) // inner, lax.axis_index(axis) // inner
    rows = value.shape[0]
    parts = [value] + [stepped(value, axis, inner, step) for step in range(1, members)]
    out = jnp.zeros((members * rows,) + value.shape[1:], value.dtype)
    for step, part in enumerate(parts):
        out = lax.dynamic_update_slice_in_dim(out, part, (own - step) % members * rows, 0)
    return out


def sum_all(value, axis):
    parts = [value] + [stepped(value, axis, 1, step) for step in range(1, lax.axis_size(axis))]
    while len(parts) > 1:
        middle = len(parts) // 2
        parts = [a + b for a, b in zip(parts[:middle], parts[middle:])]
    return parts[0]


def after(value, *arrivals):
    return lax.optimization_barrier((value, *arrivals))[0]


def body(spectrum, pupil, amplitudes, offsets, live):
    side = pupil.shape[-1]
    half = side // 2
    tile_rows, tile_cols = spectrum.shape[1:]
    n_ty, n_tx = lax.axis_size("ty"), lax.axis_size("tx")
    own_ty, own_tx = lax.axis_index("ty"), lax.axis_index("tx")
    rows_local = offsets[:, 0] - own_ty * tile_rows
    cols_local = offsets[:, 1] - own_tx * tile_cols
    meta = jnp.stack([rows_local, cols_local, live], axis=1)
    meta = jnp.concatenate([meta, jnp.full((1, 3), own_ty % 2, jnp.int32)], axis=0)

    def left(i, j):
        return (i, j - 1)

    def up(i, j):
        return (i - 1, j)

    def up_odd(i, j):
        return (i - 1, j) if i % 2 else None

    lower_b = send(spectrum[:, :side, half:side], up)
    right_a = send(spectrum[:, :, :half], left)
    right_b = send(spectrum[:, :, half:side], left)
    lower_a = send(spectrum[:, :side, :half], up)
    lower_c = send(spectrum[:, :side, side:], up)
    amps, pupils = prepare(meta, amplitudes, pupil)
    lower_b, amps = lax.optimization_barrier((lower_b, amps))
    corner_side = send(lower_b, lambda i, j: (i, j - 1) if i % 2 else None)
    corner_a = send(right_a[:, :side], up)
    corner_up_a = send(right_b[:, :side, : half // 2], up_odd)
    corner_up_b = send(right_b[:, :side, half // 2 :], up_odd)

    parts = (
        right_a,
        right_b,
        lower_a,
        lower_b,
        lower_c,
        corner_a,
        corner_up_a,
        corner_up_b,
        corner_side,
    )
    own_g, right_g, side_g, lower_ca_g, lower_b_g, corner_g, keep, give = slots_call(
        meta, spectrum, parts, amps, pupils
    )

    def down(i, j):
        return (i + 1, j)

    def right(i, j):
        return (i, j + 1)

    cut = back_cut(side)
    split_at = tile_cols - side
    part = keep + lax.ppermute(give, "ty", [(i, i ^ 1) for i in range(n_ty)])
    corner = send(corner_g, down)
    beside = send(side_g, right)
    part = scatter(part, "ty", 2)
    part, lower_ca_g, corner, beside = lax.optimization_barrier((part, lower_ca_g, corner, beside))
    lower_ca = send(lower_ca_g, down)
    part = sum_all(part, "tx") * (1.0 / math.sqrt(n_ty * n_tx))
    spec_grad = own_g.at[:, :, cut:side].add(beside[:, :tile_rows])
    part, spec_grad = lax.optimization_barrier((part, spec_grad))
    right_back = send(after(right_g + corner, part), right)
    part = gather(after(part, lower_ca), "ty", 2)
    spec_grad = spec_grad.at[:, :, side:].add(lower_ca[:, :, :split_at])
    spec_grad = spec_grad.at[:, :, :cut].add(lower_ca[:, :, split_at:])
    part, spec_grad = lax.optimization_barrier((part, spec_grad))
    lower_b = send(after(lower_b_g + beside[:, tile_rows:], part), down)
    pupil_grad = double(part, 1)
    spec_grad = spec_grad.at[:, :, :cut].add(right_back)
    spec_grad, pupil_grad = lax.optimization_barrier((spec_grad, pupil_grad))
    spec_grad = spec_grad.at[:, :, cut:side].add(lower_b)
    return spec_grad, pupil_grad.reshape(pupil.shape)


def solution(mesh):
    return jax.shard_map(
        body,
        mesh=mesh,
        in_specs=(
            P(None, "ty", "tx"),
            P(),
            P(("ty", "tx"), None, None),
            P(("ty", "tx"), None),
            P(("ty", "tx")),
        ),
        out_specs=(P(None, "ty", "tx"), P()),
        check_vma=False,
    )
```

```python
import math

import jax
import jax.numpy as jnp
import ml_dtypes
import numpy as np
from jax import lax
from jax.experimental import pallas as pl
from jax.experimental.pallas import tpu as pltpu
from jax.sharding import PartitionSpec as P

RADIX = 4


def dft_blocks(length):
    short = length // RADIX
    out_idx = np.arange(short)[:, None]
    in_idx = np.arange(short)[None, :]
    blocks = []
    for p in range(RADIX):
        phase = (p * in_idx + RADIX * out_idx * in_idx) % length
        angle = phase * (2.0 * math.pi / length)
        cos = np.cos(angle) / math.sqrt(length)
        sin = np.sin(angle) / math.sqrt(length)
        blocks.append(np.block([[cos, -sin], [sin, cos]]))
    full = np.stack(blocks).astype(np.float32)
    high = full.astype(ml_dtypes.bfloat16)
    low = (full - high.astype(np.float32)).astype(ml_dtypes.bfloat16)
    return high, low


def split(value):
    high = value.astype(jnp.bfloat16)
    low = (value - high.astype(jnp.float32)).astype(jnp.bfloat16)
    return high, low


def dot(lhs, rhs):
    return jnp.dot(lhs, rhs, preferred_element_type=jnp.float32)


def left_dot(mat_hi, mat_lo, val_hi, val_lo):
    lhs = jnp.concatenate([mat_hi, mat_hi, mat_lo], axis=1)
    return dot(lhs, jnp.concatenate([val_hi, val_lo, val_hi], axis=0))


def right_dot(val_hi, val_lo, mat_hi, mat_lo):
    lhs = jnp.concatenate([val_hi, val_lo, val_hi], axis=1)
    return dot(lhs, jnp.concatenate([mat_hi, mat_hi, mat_lo], axis=0))


def butterfly(parts, sign):
    (r0, i0), (r1, i1), (r2, i2), (r3, i3) = parts
    sr, si, dr, di = r0 + r2, i0 + i2, r0 - r2, i0 - i2
    tr, ti, er, ei = r1 + r3, i1 + i3, r1 - r3, i1 - i3
    if sign < 0:
        er, ei = -er, -ei
    return [(sr + tr, si + ti), (dr - ei, di + er), (sr - tr, si - ti), (dr + ei, di - er)]


def row_index():
    return lax.broadcasted_iota(jnp.int32, (8, 128), 0)


def lane_index():
    return lax.broadcasted_iota(jnp.int32, (8, 128), 1)


def lane_tiles(tile):
    return [tile[:, i : i + 128] for i in range(0, tile.shape[1], 128)]


def rolled(tiles, amount, axis):
    return [[pltpu.roll(part, amount, axis) for part in tile] for tile in tiles]


def shift_on(tiles, row_shift, col_shift):
    keep = lane_index() >= col_shift
    tiles = rolled([lane_tiles(tile) for tile in tiles], col_shift, 1)
    tiles = [[jnp.where(keep, x, y) for x, y in zip(t, t[-1:] + t[:-1])] for t in tiles]
    keep = row_index() >= row_shift
    tiles = rolled(tiles, row_shift, 0)
    return [
        jnp.concatenate([jnp.where(keep, y, x) for x, y in zip(a, b)], axis=1)
        for a, b in zip(tiles, tiles[1:])
    ]


def shift_back(tiles, row_shift, col_shift):
    keep = lane_index() < 128 - col_shift
    tiles = rolled([lane_tiles(tile) for tile in tiles], (128 - col_shift) % 128, 1)
    tiles = [[jnp.where(keep, x, y) for x, y in zip(t, t[1:] + t[:1])] for t in tiles]
    keep = row_index() < 8 - row_shift
    tiles = rolled(tiles, (8 - row_shift) % 8, 0)
    return [
        jnp.concatenate([jnp.where(keep, x, y) for x, y in zip(a, b)], axis=1)
        for a, b in zip(tiles, tiles[1:])
    ]


def wrap_lanes(block, col_shift):
    rows = block.shape[0]
    keep = lax.broadcasted_iota(jnp.int32, (rows, 128), 1) >= col_shift
    first = jnp.where(keep, block[:, :128], block[:, -128:])
    return jnp.concatenate([first, block[:, 128:-128]], axis=1)


def unwrap_lanes(block, col_shift):
    rows = block.shape[0]
    keep = lax.broadcasted_iota(jnp.int32, (rows, 128), 1) >= col_shift
    zero = jnp.zeros((rows, 128), jnp.float32)
    first = jnp.where(keep, block[:, :128], zero)
    last = jnp.where(keep, zero, block[:, :128])
    return jnp.concatenate([first, block[:, 128:], last], axis=1)


def slots_kernel(
    meta,
    tile_hbm,
    right_a_hbm,
    right_b_hbm,
    lower_a_hbm,
    lower_b_hbm,
    lower_c_hbm,
    corner_a_hbm,
    corner_up_a_hbm,
    corner_up_b_hbm,
    corner_side_hbm,
    amps_hbm,
    pupil_hbm,
    mat_hi_hbm,
    mat_lo_hbm,
    mat_t_hi_hbm,
    mat_t_lo_hbm,
    own_out,
    right_out,
    side_out,
    lower_ca_out,
    lower_b_out,
    corner_out,
    keep_out,
    give_out,
    region,
    grads,
    win,
    left_hi,
    left_lo,
    right_hi,
    right_lo,
    cols_f32,
    rows_f32,
    dwin,
    dpup,
    amps,
    pupil,
    mat_hi,
    mat_lo,
    mat_t_hi,
    mat_t_lo,
    in_sems,
    slot_sems,
    out_sems,
):
    side = pupil.shape[-1]
    short = side // RADIX
    tile_rows, tile_cols = tile_hbm.shape[1:]
    slots = amps_hbm.shape[0]
    lanes = 128
    wide = side + lanes
    half = side // 2
    top, bottom = pl.ds(0, tile_rows), pl.ds(tile_rows, side)

    def copy_in(src, row_range, start, sem):
        dst = region.at[:, row_range, pl.ds(start, src.shape[-1])]
        return pltpu.make_async_copy(src, dst, in_sems.at[sem])

    loads = [
        copy_in(tile_hbm, top, 0, 0),
        copy_in(right_a_hbm, top, tile_cols, 1),
        copy_in(right_b_hbm, top, tile_cols + half, 2),
        copy_in(lower_a_hbm, bottom, 0, 3),
        copy_in(lower_b_hbm, bottom, half, 4),
        copy_in(lower_c_hbm, bottom, side, 5),
        copy_in(corner_a_hbm, bottom, tile_cols, 6),
    ]
    for load in loads:
        load.start()
    from_side = copy_in(corner_side_hbm, bottom, tile_cols + half, 7)
    from_below_a = copy_in(corner_up_a_hbm, bottom, tile_cols + half, 7)
    from_below_b = copy_in(corner_up_b_hbm, bottom, tile_cols + half + half // 2, 7)
    odd = meta[slots, 0]
    pl.when(odd == 1)(from_side.start)

    @pl.when(odd != 1)
    def _():
        from_below_a.start()
        from_below_b.start()

    loads.append(from_side)
    late = (
        (mat_hi_hbm, mat_hi),
        (mat_lo_hbm, mat_lo),
        (mat_t_hi_hbm, mat_t_hi),
        (mat_t_lo_hbm, mat_t_lo),
    )
    late_loads = [
        pltpu.make_async_copy(src, dst, in_sems.at[8 + n]) for n, (src, dst) in enumerate(late)
    ]
    for load in late_loads:
        load.start()
    count = meta[0, 2]
    for slot in range(1, slots):
        count = count + meta[slot, 2]

    def slot_loads(slot):
        return (
            pltpu.make_async_copy(pupil_hbm.at[slot], pupil.at[slot], slot_sems.at[0, slot]),
            pltpu.make_async_copy(amps_hbm.at[slot], amps.at[slot], slot_sems.at[1, slot]),
        )

    @pl.loop(0, count)
    def _(slot):
        for load in slot_loads(slot):
            load.start()

    cut = corner_out.shape[-1]
    lower_c_out = lower_ca_out.at[:, :, pl.ds(0, tile_cols - side)]
    lower_a_out = lower_ca_out.at[:, :, pl.ds(tile_cols - side, half)]
    outs = (
        (corner_out, bottom, tile_cols),
        (lower_c_out, bottom, side),
        (lower_a_out, bottom, 0),
        (lower_b_out, bottom, half),
        (side_out, pl.ds(0, tile_rows + side), tile_cols + cut),
        (right_out, top, tile_cols),
        (own_out, top, 0),
    )
    stores = [
        pltpu.make_async_copy(
            grads.at[:, rows, pl.ds(start, dst.shape[-1])], dst, out_sems.at[n]
        )
        for n, (dst, rows, start) in enumerate(outs)
    ]
    dpup_stores = [
        [
            pltpu.make_async_copy(dpup.at[plane], keep_out, out_sems.at[7]),
            pltpu.make_async_copy(dpup.at[1 - plane], give_out, out_sems.at[8]),
        ]
        for plane in range(2)
    ]

    def store_dpup():
        for plane, copies in enumerate(dpup_stores):
            for copy in copies:
                pl.when(odd == plane)(copy.start)

    lower_stores = stores[:4]
    upper_stores = stores[4:]

    zero_rows = 16

    @pl.loop(0, grads.shape[1] // zero_rows)
    def _(step):
        rows = pl.ds(pl.multiple_of(step * zero_rows, zero_rows), zero_rows)
        grads[:, rows, :] = jnp.zeros((2, zero_rows, grads.shape[2]), jnp.float32)

    @pl.loop(0, side // zero_rows)
    def _(step):
        rows = pl.ds(pl.multiple_of(step * zero_rows, zero_rows), zero_rows)
        dpup[:, rows, :] = jnp.zeros((2, zero_rows, side), jnp.float32)

    def one_slot(slot):
        row = meta[slot, 0]
        col = meta[slot, 1]
        col_base = pl.multiple_of((col // lanes) * lanes, lanes)
        col_shift = col - col_base
        row_base = pl.multiple_of((row // 8) * 8, 8)
        row_shift = row - row_base

        def cut(step):
            base = pl.multiple_of(step * 32, 32)
            rows = pl.ds(pl.multiple_of(row_base + base, 8), 32)
            for plane in range(2):
                block = region[plane, rows, pl.ds(col_base, wide)]
                win[plane, pl.ds(base, 32), :] = wrap_lanes(block, col_shift)

        above = (tile_rows - row_base) // 32

        @pl.when(slot == 0)
        def _():
            for load in loads[:3]:
                load.wait()

        pl.loop(0, above)(cut)

        @pl.when(slot == 0)
        def _():
            for load in loads[3:]:
                load.wait()

        pl.loop(above, side // 32)(cut)

        first_keep = lax.broadcasted_iota(jnp.int32, (8, side), 0) >= row_shift
        last_rows = pl.ds(pl.multiple_of(row_base + side, 8), 8)
        for plane in range(2):
            block = region[plane, last_rows, pl.ds(col_base, wide)]
            block = wrap_lanes(block, col_shift)
            win[plane, :8, :] = jnp.where(first_keep, win[plane, :8, :], block)

        pupil_load, amps_load = slot_loads(slot)
        pupil_load.wait()

        @pl.when(slot == 0)
        def _():
            for load in late_loads:
                load.wait()

        for start in (0, half):
            for base in range(0, short, 16):
                for col0 in range(start, start + half, short):
                    cols = pl.ds(col0, short)
                    values = []
                    for q in range(RADIX):
                        rows = pl.ds(base + q * short, 16)
                        wr, wi = win[0, rows, cols], win[1, rows, cols]
                        pr, pi = pupil[slot, 0, rows, cols], pupil[slot, 1, rows, cols]
                        values.append((wr * pr - wi * pi, wr * pi + wi * pr))
                    for p, (re, im) in enumerate(butterfly(values, 1)):
                        for offset, value in ((0, re), (short, im)):
                            hi, lo = split(value)
                            rows = pl.ds(base + offset, 16)
                            left_hi[p, rows, cols] = hi
                            left_lo[p, rows, cols] = lo
            cols = pl.ds(start, half)
            for p in range(RADIX):
                rows_f32[p, :, cols] = left_dot(
                    mat_hi[p], mat_lo[p], left_hi[p, :, cols], left_lo[p, :, cols]
                )

        for p in range(RADIX):
            for base in range(0, short, 16):
                values = []
                for q in range(RADIX):
                    cols = pl.ds(q * short, short)
                    values.append(
                        (
                            rows_f32[p, pl.ds(base, 16), cols],
                            rows_f32[p, pl.ds(base + short, 16), cols],
                        )
                    )
                for t, (re, im) in enumerate(butterfly(values, 1)):
                    for offset, value in ((0, re), (short, im)):
                        hi, lo = split(value)
                        rows = pl.ds(base + p * short, 16)
                        right_hi[t, rows, pl.ds(offset, short)] = hi
                        right_lo[t, rows, pl.ds(offset, short)] = lo

        amps_load.wait()

        for t in range(RADIX):
            for start in (0, half):
                rows = pl.ds(start, half)
                field = right_dot(
                    right_hi[t, rows, :], right_lo[t, rows, :], mat_t_hi[t], mat_t_lo[t]
                )
                fre, fim = field[:, :short], field[:, short:]
                measured = amps[slot, rows, pl.ds(t * short, short)]
                factor = 1.0 - measured * lax.rsqrt(fre * fre + fim * fim + 1.0)
                residual = jnp.concatenate([factor * fre, factor * fim], axis=1)
                hi, lo = split(residual)
                cols_f32[t, rows, :] = right_dot(hi, lo, mat_hi[t], mat_lo[t])

        for p in range(RADIX):
            for base in range(0, short, 16):
                rows = pl.ds(base + p * short, 16)
                values = [
                    (cols_f32[t, rows, pl.ds(0, short)], cols_f32[t, rows, pl.ds(short, short)])
                    for t in range(RADIX)
                ]
                for q, (re, im) in enumerate(butterfly(values, -1)):
                    cols = pl.ds(q * short, short)
                    for offset, value in ((0, re), (short, im)):
                        hi, lo = split(value)
                        left_hi[p, pl.ds(base + offset, 16), cols] = hi
                        left_lo[p, pl.ds(base + offset, 16), cols] = lo

        for start in (0, half):
            cols = pl.ds(start, half)
            for p in range(RADIX):
                rows_f32[p, :, cols] = left_dot(
                    mat_t_hi[p], mat_t_lo[p], left_hi[p, :, cols], left_lo[p, :, cols]
                )
            for base in range(0, short, 8):
                for col0 in range(start, start + half, short):
                    cols = pl.ds(col0, short)
                    values = [
                        (
                            rows_f32[p, pl.ds(base, 8), cols],
                            rows_f32[p, pl.ds(base + short, 8), cols],
                        )
                        for p in range(RADIX)
                    ]
                    for q, (re, im) in enumerate(butterfly(values, -1)):
                        rows = pl.ds(base + q * short, 8)
                        pr, pi = pupil[slot, 0, rows, cols], pupil[slot, 1, rows, cols]
                        dwin[0, rows, cols] = pr * re + pi * im
                        dwin[1, rows, cols] = pr * im - pi * re
                        wr, wi = win[0, rows, cols], win[1, rows, cols]
                        win[0, rows, cols] = wr * re + wi * im
                        win[1, rows, cols] = wr * im - wi * re

        @pl.loop(0, side // 32, unroll=2)
        def _(step):
            base = pl.multiple_of(step * 32, 32)
            after = pl.multiple_of((base + 32) % side, 8)
            for plane in range(2):
                tiles = [win[plane, pl.ds(base + 8 * i, 8), :] for i in range(4)]
                tiles.append(win[plane, pl.ds(after, 8), :])
                for i, tile in enumerate(shift_back(tiles, row_shift, col_shift)):
                    dpup[plane, pl.ds(base + 8 * i, 8), :] += tile

        last = slot == count - 1
        pl.when(last)(store_dpup)

        zero = jnp.zeros((8, side), jnp.float32)
        for plane in range(2):
            block = dwin[plane, :8, :]
            dwin[plane, :8, :] = jnp.where(first_keep, block, zero)
            dwin[plane, pl.ds(side, 8), :] = jnp.where(first_keep, zero, block)

        def place(step):
            base = pl.multiple_of(step * 40, 8)
            rows = pl.ds(pl.multiple_of(row_base + base, 8), 40)
            for plane in range(2):
                block = unwrap_lanes(dwin[plane, pl.ds(base, 40), :], col_shift)
                target = (plane, rows, pl.ds(col_base, wide))
                grads[target] = grads[target] + block

        steps = (side + 8) // 40
        above = (tile_rows - row_base) // 40
        pl.loop(above, steps)(place)

        @pl.when(last)
        def _():
            for store in lower_stores:
                store.start()

        pl.loop(0, above)(place)

    pl.loop(0, count)(one_slot)

    @pl.when(count == 0)
    def _():
        store_dpup()
        for store in lower_stores:
            store.start()
        for load in loads + late_loads:
            load.wait()

    for store in upper_stores:
        store.start()
    for store in dpup_stores[0] + stores:
        store.wait()


def back_cut(side):
    return 3 * side // 4


def slots_call(meta, tile, parts, amps, pupils):
    side = pupils.shape[-1]
    short = side // RADIX
    slots = amps.shape[0]
    tile_rows, tile_cols = tile.shape[1:]
    high, low = dft_blocks(side)
    tables = [jnp.asarray(x) for x in (high, low, high.transpose(0, 2, 1), low.transpose(0, 2, 1))]
    anywhere = pl.BlockSpec(memory_space=pl.ANY)
    f32, bf16 = jnp.float32, jnp.bfloat16
    region = (2, tile_rows + side, tile_cols + side)
    cut = back_cut(side)
    plane = jax.ShapeDtypeStruct((side, side), f32)
    shapes = (
        (tile_rows, cut),
        (tile_rows + side, side - cut),
        (side, tile_cols - side // 2),
        (side, side // 2),
        (side, cut),
    )
    outs = (tile, *(jax.ShapeDtypeStruct((2, *shape), f32) for shape in shapes), plane, plane)
    table = pltpu.VMEM(high.shape, bf16)
    return pl.pallas_call(
        slots_kernel,
        out_shape=[jax.ShapeDtypeStruct(x.shape, f32) for x in outs],
        in_specs=[pl.BlockSpec(memory_space=pltpu.SMEM)] + [anywhere] * (len(parts) + 7),
        out_specs=[anywhere] * len(outs),
        scratch_shapes=[
            pltpu.VMEM(region, f32),
            pltpu.VMEM(region, f32),
            pltpu.VMEM((2, side, side), f32),
            pltpu.VMEM((RADIX, 2 * short, side), bf16),
            pltpu.VMEM((RADIX, 2 * short, side), bf16),
            pltpu.VMEM((RADIX, side, 2 * short), bf16),
            pltpu.VMEM((RADIX, side, 2 * short), bf16),
            pltpu.VMEM((RADIX, side, 2 * short), f32),
            pltpu.VMEM((RADIX, 2 * short, side), f32),
            pltpu.VMEM((2, side + 8, side), f32),
            pltpu.VMEM((2, side, side), f32),
            pltpu.VMEM(amps.shape, f32),
            pltpu.VMEM(pupils.shape, f32),
            table,
            table,
            table,
            table,
            pltpu.SemaphoreType.DMA((12,)),
            pltpu.SemaphoreType.DMA((2, slots)),
            pltpu.SemaphoreType.DMA((9,)),
        ],
        compiler_params=pltpu.CompilerParams(vmem_limit_bytes=56 * 1024 * 1024),
        cost_estimate=pl.CostEstimate(
            flops=slots * 48 * 2 * 4 * short * short * side,
            bytes_accessed=40 * 1024 * 1024,
            transcendentals=slots * side * side,
        ),
        name="slots",
    )(meta, tile, *parts, amps, pupils, *tables)


def exact_parts(value):
    hi, rest = split(value)
    rest = value - hi.astype(jnp.float32)
    return (hi, *split(rest))


def prepare_kernel(meta, amps, pupil, perm_rows, perm_cols, amps_out, pupil_out):
    value = sum(dot(part, perm_cols[...]) for part in exact_parts(amps[0]))
    amps_out[0] = sum(dot(perm_rows[...], part) for part in exact_parts(value))

    slot = pl.program_id(0)
    row_shift = meta[slot, 0] % 8
    col_shift = meta[slot, 1] % 128
    side = pupil.shape[-1]

    @pl.loop(0, side // 32, unroll=2)
    def _(step):
        base = pl.multiple_of(step * 32, 32)
        before = pl.multiple_of((base + side - 8) % side, 8)
        for plane in range(2):
            tiles = [pupil[plane, pl.ds(before, 8), :]]
            tiles += [pupil[plane, pl.ds(base + 8 * i, 8), :] for i in range(4)]
            for i, tile in enumerate(shift_on(tiles, row_shift, col_shift)):
                pupil_out[0, plane, pl.ds(base + 8 * i, 8), :] = tile


def prepare(meta, amps, pupil):
    slots, side, _ = amps.shape
    index = np.arange(side)
    perm = np.zeros((side, side), ml_dtypes.bfloat16)
    perm[index, (index % RADIX) * (side // RADIX) + index // RADIX] = 1
    block = pl.BlockSpec((1, side, side), lambda s: (s, 0, 0))
    table = pl.BlockSpec((side, side), lambda s: (0, 0))
    return pl.pallas_call(
        prepare_kernel,
        grid=(slots,),
        out_shape=[
            jax.ShapeDtypeStruct(amps.shape, amps.dtype),
            jax.ShapeDtypeStruct((slots, 2, side, side), pupil.dtype),
        ],
        in_specs=[
            pl.BlockSpec(memory_space=pltpu.SMEM),
            block,
            pl.BlockSpec((2, side, side), lambda s: (0, 0, 0)),
            table,
            table,
        ],
        out_specs=[block, pl.BlockSpec((1, 2, side, side), lambda s: (s, 0, 0, 0))],
        compiler_params=pltpu.CompilerParams(vmem_limit_bytes=32 * 1024 * 1024),
        cost_estimate=pl.CostEstimate(
            flops=slots * 12 * side**3, bytes_accessed=24 * slots * side**2, transcendentals=0
        ),
        name="prepare",
    )(meta, amps, pupil, jnp.asarray(perm.T), jnp.asarray(perm))


def along(axis_pairs, members):
    n_ty, n_tx = members
    pairs = []
    for i in range(n_ty):
        for j in range(n_tx):
            target = axis_pairs(i, j)
            if target is not None and 0 <= target[0] < n_ty and 0 <= target[1] < n_tx:
                pairs.append((i * n_tx + j, target[0] * n_tx + target[1]))
    return pairs


def send(array, rule):
    sizes = (lax.axis_size("ty"), lax.axis_size("tx"))
    return lax.ppermute(array, ("ty", "tx"), along(rule, sizes))


def double(value, bit):
    mine = lax.axis_index("ty") // bit % 2
    other = lax.ppermute(value, "ty", [(i, i ^ bit) for i in range(lax.axis_size("ty"))])
    first = jnp.where(mine == 0, value, other)
    second = jnp.where(mine == 0, other, value)
    return jnp.concatenate([first, second], axis=0)


def stepped(value, axis, inner, step):
    size = lax.axis_size(axis)
    return lax.ppermute(value, axis, [(i, (i + step * inner) % size) for i in range(size)])


def scatter(value, axis, inner):
    members, own = lax.axis_size(axis) // inner, lax.axis_index(axis) // inner
    rows = value.shape[0] // members
    total = lax.dynamic_slice_in_dim(value, own * rows, rows, 0)
    for step in range(1, members):
        piece = lax.dynamic_slice_in_dim(value, (own + step) % members * rows, rows, 0)
        total = total + stepped(piece, axis, inner, step)
    return total


def gather(value, axis, inner):
    members, own = lax.axis_size(axis) // inner, lax.axis_index(axis) // inner
    rows = value.shape[0]
    parts = [value] + [stepped(value, axis, inner, step) for step in range(1, members)]
    out = jnp.zeros((members * rows,) + value.shape[1:], value.dtype)
    for step, part in enumerate(parts):
        out = lax.dynamic_update_slice_in_dim(out, part, (own - step) % members * rows, 0)
    return out


def sum_all(value, axis):
    parts = [value] + [stepped(value, axis, 1, step) for step in range(1, lax.axis_size(axis))]
    while len(parts) > 1:
        middle = len(parts) // 2
        parts = [a + b for a, b in zip(parts[:middle], parts[middle:])]
    return parts[0]


def after(value, *arrivals):
    return lax.optimization_barrier((value, *arrivals))[0]


def body(spectrum, pupil, amplitudes, offsets, live):
    side = pupil.shape[-1]
    half = side // 2
    tile_rows, tile_cols = spectrum.shape[1:]
    n_ty, n_tx = lax.axis_size("ty"), lax.axis_size("tx")
    own_ty, own_tx = lax.axis_index("ty"), lax.axis_index("tx")
    rows_local = offsets[:, 0] - own_ty * tile_rows
    cols_local = offsets[:, 1] - own_tx * tile_cols
    meta = jnp.stack([rows_local, cols_local, live], axis=1)
    meta = jnp.concatenate([meta, jnp.full((1, 3), own_ty % 2, jnp.int32)], axis=0)

    def left(i, j):
        return (i, j - 1)

    def up(i, j):
        return (i - 1, j)

    def up_odd(i, j):
        return (i - 1, j) if i % 2 else None

    lower_b = send(spectrum[:, :side, half:side], up)
    right_a = send(spectrum[:, :, :half], left)
    right_b = send(spectrum[:, :, half:side], left)
    lower_a = send(spectrum[:, :side, :half], up)
    lower_c = send(spectrum[:, :side, side:], up)
    amps, pupils = prepare(meta, amplitudes, pupil)
    lower_b, amps = lax.optimization_barrier((lower_b, amps))
    corner_side = send(lower_b, lambda i, j: (i, j - 1) if i % 2 else None)
    corner_a = send(right_a[:, :side], up)
    corner_up_a = send(right_b[:, :side, : half // 2], up_odd)
    corner_up_b = send(right_b[:, :side, half // 2 :], up_odd)

    parts = (
        right_a,
        right_b,
        lower_a,
        lower_b,
        lower_c,
        corner_a,
        corner_up_a,
        corner_up_b,
        corner_side,
    )
    own_g, right_g, side_g, lower_ca_g, lower_b_g, corner_g, keep, give = slots_call(
        meta, spectrum, parts, amps, pupils
    )

    def down(i, j):
        return (i + 1, j)

    def right(i, j):
        return (i, j + 1)

    cut = back_cut(side)
    split_at = tile_cols - side
    part = keep + lax.ppermute(give, "ty", [(i, i ^ 1) for i in range(n_ty)])
    corner = send(corner_g, down)
    beside = send(side_g, right)
    part = scatter(part, "ty", 2)
    part, lower_ca_g, corner, beside = lax.optimization_barrier((part, lower_ca_g, corner, beside))
    lower_ca = send(lower_ca_g, down)
    part = sum_all(part, "tx") * (1.0 / math.sqrt(n_ty * n_tx))
    spec_grad = own_g.at[:, :, cut:side].add(beside[:, :tile_rows])
    part, spec_grad = lax.optimization_barrier((part, spec_grad))
    right_back = send(after(right_g + corner, part), right)
    part = gather(after(part, lower_ca), "ty", 2)
    spec_grad = spec_grad.at[:, :, side:].add(lower_ca[:, :, :split_at])
    spec_grad = spec_grad.at[:, :, :half].add(lower_ca[:, :, split_at:])
    part, spec_grad = lax.optimization_barrier((part, spec_grad))
    lower_b_g = lower_b_g.at[:, :, cut - half :].add(beside[:, tile_rows:])
    lower_b = send(after(lower_b_g, part), down)
    pupil_grad = double(part, 1)
    spec_grad, pupil_grad = lax.optimization_barrier((spec_grad, pupil_grad))
    spec_grad = spec_grad.at[:, :, :cut].add(right_back)
    spec_grad = spec_grad.at[:, :, half:side].add(lower_b)
    return spec_grad, pupil_grad.reshape(pupil.shape)


def solution(mesh):
    return jax.shard_map(
        body,
        mesh=mesh,
        in_specs=(
            P(None, "ty", "tx"),
            P(),
            P(("ty", "tx"), None, None),
            P(("ty", "tx"), None),
            P(("ty", "tx")),
        ),
        out_specs=(P(None, "ty", "tx"), P()),
        check_vma=False,
    )
```
